512 devices in a mesh: space: 128 (over y, z, core), chan: 4 (over x).
Axes of the slice: x: 4, y: 8, z: 8, core: 2. Of those that a mesh axis runs over, the one named last changes fastest.
Arguments:
- features: bfloat16 [128, 256, 512], P('chan', 'space'), may hold values from -6 to 6
- mask_packed: int32 [256, 16], P('space'), may hold values from -2147483648 to 2147483646
- neighbours: int32 [256, 26], P('space'), may hold values from 0 to 10, as said below
- send_list: int32 [128, 8, 1], P('space'), may hold values from 0 to 2, as said below
- weights: bfloat16 [27, 128, 128], P(None, 'chan'), may hold values from -0.109375 to 0.109375
- cotangent: bfloat16 [128, 256, 512], P('chan', 'space'), may hold values from -6 to 6
Outputs:
- activated: bfloat16 [128, 256, 512], P('chan', 'space')
- grad_features: bfloat16 [128, 256, 512], P('chan', 'space')
- grad_weights: float32 [27, 128, 128], P(None, 'chan')
The draws below stay inside these ranges and needn't reach their ends.
Inputs may be any that keep to these rules, and one draw needn't show every extreme that they name: `neighbours`: entry j of a brick's row names the neighbour at the j-th of the 26 offsets as a row of its partition's table: 0 to 1 the partition's own bricks, 2 + k + s the s-th brick received from the adjacent tile in the k-th planar move, used only where the offset's planar part is that move and the tile exists, 10 none. Every slot that is named is filled in send_list. send_list[q, k, s] is the local index of the s-th brick that partition q sends to the partition whose tile lies at q's tile moved by minus the k-th planar move, or 2 where that slot is empty; a slot is filled exactly when some brick of that partition names it.
All inputs are finite; a program needn't handle non-finite values.
Results may differ from the reference program's by a relative error of at most 0.005.
Values may be sent and summed in bfloat16 or wider, within the bound.
No kernel may reach another device: no remote copies, remote signals or barrier semaphores. Data moves between devices by JAX's collectives and lax.ppermute only.
A program may use at most 128 MiB of HBM per device.

```python
import math
import jax
import jax.numpy as jnp
from jax import lax

C = 128
BRICK = 8
BRICK_DEV = 2
SLOTS = 1
VOX = 512
BRICKS = 256
N_SPACE = 128


tile_moves = [(move_a, move_b) for move_a in (-1, 0, 1) for move_b in (-1, 0, 1) if (move_a, move_b) != (0, 0)]


cube_offsets = [(along_x, along_y, along_z) for along_x in (-1, 0, 1) for along_y in (-1, 0, 1) for along_z in (-1, 0, 1) if (along_x, along_y, along_z) != (0, 0, 0)]


def move_of(along_x, along_y):
    if (along_x, along_y) == (0, 0):
        return -1
    return tile_moves.index((along_x, along_y))


def geometry(key):
    key_kind, key_local, key_slot, key_pick = jax.random.split(key, 4)
    grid_shape = (N_SPACE, BRICK_DEV, 26)
    category = jax.random.randint(key_kind, grid_shape, 0, 20)
    local_pick = jax.random.randint(key_local, grid_shape, 0, BRICK_DEV)
    slot_pick = jax.random.randint(key_slot, grid_shape, 0, SLOTS)
    offset_x = jnp.array([entry[0] for entry in cube_offsets], dtype=jnp.int32)
    offset_y = jnp.array([entry[1] for entry in cube_offsets], dtype=jnp.int32)
    offset_move = jnp.array([move_of(entry[0], entry[1]) for entry in cube_offsets], dtype=jnp.int32)
    owners = jnp.arange(N_SPACE, dtype=jnp.int32)[:, None, None]
    tile_rows = N_SPACE // 4
    target_x = owners // 4 + offset_x[None, None, :]
    target_y = owners % 4 + offset_y[None, None, :]
    inside = (target_x >= 0) & (target_x < tile_rows) & (target_y >= 0) & (target_y < 4) & (offset_move[None, None, :] >= 0)
    remote_flag = (category >= 13) & inside
    slot_code = offset_move[None, None, :] * SLOTS + slot_pick
    empty_row = BRICK_DEV + 8 * SLOTS
    local_flag = (category >= 7) & ((category < 13) | (offset_move[None, None, :] < 0))
    neighbour_rows = jnp.where(remote_flag, BRICK_DEV + slot_code, jnp.where(local_flag, local_pick, empty_row))
    matches = (slot_code.reshape(N_SPACE, -1)[:, :, None] == jnp.arange(8 * SLOTS, dtype=jnp.int32)[None, None, :]) & remote_flag.reshape(N_SPACE, -1)[:, :, None]
    filled = jnp.any(matches, axis=1).reshape(N_SPACE, 8, SLOTS)
    move_x = jnp.array([entry[0] for entry in tile_moves], dtype=jnp.int32)
    move_y = jnp.array([entry[1] for entry in tile_moves], dtype=jnp.int32)
    senders = jnp.arange(N_SPACE, dtype=jnp.int32)[:, None]
    receiver_x = senders // 4 - move_x[None, :]
    receiver_y = senders % 4 - move_y[None, :]
    receiver_ok = (receiver_x >= 0) & (receiver_x < tile_rows) & (receiver_y >= 0) & (receiver_y < 4)
    receiver = jnp.clip(receiver_x * 4 + receiver_y, 0, N_SPACE - 1)
    sender_filled = filled[receiver, jnp.arange(8, dtype=jnp.int32)[None, :], :] & receiver_ok[:, :, None]
    chosen = jax.random.randint(key_pick, (N_SPACE, 8, SLOTS), 0, BRICK_DEV)
    send_rows = jnp.where(sender_filled, chosen, BRICK_DEV)
    return (neighbour_rows.reshape(N_SPACE * BRICK_DEV, 26).astype(jnp.int32), send_rows.astype(jnp.int32))


def draw_neighbours(key, part):
    neighbour_rows, send_rows = geometry(key)
    return neighbour_rows


def draw_send_list(key, part):
    neighbour_rows, send_rows = geometry(key)
    return send_rows


def set_ends(values, key, least, largest):
    place = [jax.random.randint(jax.random.fold_in(key, axis), (), 0, length) for axis, length in enumerate(values.shape)]
    longest = values.shape.index(max(values.shape))
    neighbour = place[:longest] + [(place[longest] + 1) % values.shape[longest]] + place[longest + 1:]
    return values.at[tuple(place)].set(least).at[tuple(neighbour)].set(largest)


def shard_levels(own_key, shape, shards, smallest, largest):
    loudness, own = 1.0, jax.random.fold_in(own_key, 6)
    for dim, shards_of in shards:
        draws = jnp.exp(jax.random.uniform(jax.random.fold_in(own, dim), (shards_of,), jnp.float32, smallest / len(shards), largest / len(shards)))
        loudness = loudness * jnp.repeat(draws, shape[dim] // shards_of).reshape([-1 if axis == dim else 1 for axis in range(len(shape))])
    return loudness


def centred(stream_key, dims, width, reach, cuts=(), held_as=jnp.bfloat16):
    gain = shard_levels(stream_key, dims, cuts, -0.22, 0.18) if cuts else 1.0
    values = jax.random.normal(stream_key, dims, jnp.float32) * width * gain
    return jnp.minimum(jnp.maximum(values, -reach), reach).astype(held_as)


def setup_inputs(seed: int = 0) -> dict:
    keys = jax.random.split(jax.random.key(seed), 7)
    return {
        "features": centred(keys[0], (C, BRICKS, VOX), 1.0, 6.0, ((0, 4), (1, 128))),
        "mask_packed": set_ends(jax.random.randint(keys[1], (BRICKS, VOX // 32), -2147483648, 2147483647), jax.random.fold_in(keys[1], 1), -2147483648, 2147483646).astype(jnp.int32),
        "neighbours": draw_neighbours(jax.random.fold_in(keys[6], 71), 0),
        "send_list": draw_send_list(jax.random.fold_in(keys[6], 71), 0),
        "weights": centred(keys[4], (27, C, C), (27 * C) ** -0.5, 0.109375, ((1, 4),)),
        "cotangent": centred(keys[5], (C, BRICKS, VOX), 1.0, 6.0, ((0, 4), (1, 128))),
    }


all_offsets = [(along_x, along_y, along_z) for along_x in (-1, 0, 1) for along_y in (-1, 0, 1) for along_z in (-1, 0, 1)]
tile_moves = [(move_a, move_b) for move_a in (-1, 0, 1) for move_b in (-1, 0, 1) if (move_a, move_b) != (0, 0)]
tile_steps = [move_a * 4 + move_b for move_a, move_b in tile_moves]

def unpack_mask(packed):
    shifts = jnp.arange(32, dtype=jnp.int32)
    bitflags = lax.shift_right_logical(packed[:, :, None], shifts[None, None, :]) & 1
    return bitflags.reshape(packed.shape[0], packed.shape[1] * 32).astype(jnp.float32)

def side_slice(direction, extent):
    if direction == -1:
        return slice(extent - 1, extent)
    if direction == 0:
        return slice(0, extent)
    return slice(0, 1)

def cycle_slice(direction, extent):
    if direction == -1:
        return slice(0, 1)
    if direction == 0:
        return slice(1, extent + 1)
    return slice(extent + 1, extent + 2)

def neighbour_slot(along_x, along_y, along_z):
    linear = (along_x + 1) * 9 + (along_y + 1) * 3 + (along_z + 1)
    return linear if linear < 13 else linear - 1

def window_start(extent):
    padded = extent + 2
    return padded * padded + padded + 1

def flat_length(extent):
    padded = extent + 2
    needed = 2 * (padded * padded + padded + 1) + extent * padded * padded
    return (needed + 127) // 128 * 128

def assemble(source_table, center, indices, extent):
    channels, brick_count = (center.shape[0], center.shape[1])
    planes = []
    for along_x in (-1, 0, 1):
        columns = []
        for along_y in (-1, 0, 1):
            pieces = []
            for along_z in (-1, 0, 1):
                if (along_x, along_y, along_z) == (0, 0, 0):
                    source = center
                else:
                    source = jnp.take(source_table, indices[:, neighbour_slot(along_x, along_y, along_z)], axis=1)
                source = source.reshape(channels, brick_count, extent, extent, extent)
                pieces.append(source[:, :, side_slice(along_x, extent), side_slice(along_y, extent), side_slice(along_z, extent)])
            columns.append(jnp.concatenate(pieces, axis=4))
        planes.append(jnp.concatenate(columns, axis=3))
    padded_cube = jnp.concatenate(planes, axis=2)
    padded_edge = extent + 2
    flattened = padded_cube.reshape(channels, brick_count, padded_edge ** 3)
    return jnp.pad(flattened, ((0, 0), (0, 0), (0, flat_length(extent) - padded_edge ** 3)))

def columns_of(padded_block, extent):
    padded = extent + 2
    anchor = window_start(extent)
    length = extent * padded * padded
    windows = []
    for along_x, along_y, along_z in all_offsets:
        offset_flat = along_x * padded * padded + along_y * padded + along_z
        windows.append(padded_block[:, :, anchor + offset_flat:anchor + offset_flat + length])
    return jnp.stack(windows, axis=0)

def interior(window, extent):
    padded = extent + 2
    leading = window.shape[:-1]
    shaped = window.reshape(leading + (extent, padded, padded))[..., :extent, :extent]
    return shaped.reshape(leading + (extent ** 3,))

def embed_window(values, extent):
    padded = extent + 2
    leading = values.shape[:-1]
    shaped = values.reshape(leading + (extent, extent, extent))
    widths = [(0, 0)] * len(leading) + [(0, 0), (0, padded - extent), (0, padded - extent)]
    return jnp.pad(shaped, widths).reshape(leading + (extent * padded * padded,))

def spread(products, extent, full_length, first_offset):
    padded = extent + 2
    anchor = window_start(extent)
    length = products.shape[-1]
    result = jnp.zeros(products.shape[1:-1] + (full_length,), jnp.float32)
    for position in range(products.shape[0]):
        along_x, along_y, along_z = all_offsets[first_offset + position]
        placed_at = anchor + along_x * padded * padded + along_y * padded + along_z
        result = result + jnp.pad(products[position], ((0, 0), (0, 0), (placed_at, full_length - placed_at - length)))
    return result

def scatter_block(grad_block, indices, table_rows, extent):
    channels, brick_count = (grad_block.shape[0], grad_block.shape[1])
    padded = extent + 2
    padded_cube = grad_block[:, :, :padded ** 3].reshape(channels, brick_count, padded, padded, padded)
    interior_span = slice(1, extent + 1)
    center = padded_cube[:, :, interior_span, interior_span, interior_span].reshape(channels, brick_count, extent ** 3)
    accumulated = jnp.zeros((channels, table_rows, extent, extent, extent), jnp.float32)
    for along_x, along_y, along_z in all_offsets:
        if (along_x, along_y, along_z) == (0, 0, 0):
            continue
        column = neighbour_slot(along_x, along_y, along_z)
        rim_piece = padded_cube[:, :, cycle_slice(along_x, extent), cycle_slice(along_y, extent), cycle_slice(along_z, extent)]
        accumulated = accumulated.at[:, indices[:, column], side_slice(along_x, extent), side_slice(along_y, extent), side_slice(along_z, extent)].add(rim_piece)
    return (center, accumulated.reshape(channels, table_rows, extent ** 3))

def reference(features, mask_packed, neighbours, send_list, weights, cotangent):
    mask_full = unpack_mask(mask_packed)
    masked = features * mask_full[None].astype(jnp.bfloat16)
    source_table = jnp.concatenate([masked, jnp.zeros((C, 1, VOX), jnp.bfloat16)], axis=1)
    empty_row = BRICK_DEV + 8 * SLOTS
    weight_rows = weights.reshape(27 * C, C).astype(jnp.float32)
    grad_scale = 1.0 / math.sqrt(BRICKS * VOX)
    step_values = jnp.array(tile_steps, dtype=jnp.int32)
    move_ids = jnp.arange(8, dtype=jnp.int32)

    def partition(running, part_index):
        grad_weight, grad_total = running
        first_brick = part_index * BRICK_DEV
        local_ids = lax.dynamic_slice_in_dim(neighbours, first_brick, BRICK_DEV, 0)
        slot_index = jnp.maximum(local_ids - BRICK_DEV, 0)
        move_index = jnp.minimum(slot_index // SLOTS, 7)
        slot_number = slot_index % SLOTS
        sender = part_index + step_values[move_index]
        sender_inside = (sender >= 0) & (sender < N_SPACE)
        sender_kept = jnp.clip(sender, 0, N_SPACE - 1).astype(jnp.int32)
        sent_local = send_list[sender_kept, move_index, slot_number]
        remote_ids = jnp.where((sent_local >= BRICK_DEV) | ~sender_inside, BRICKS, sender_kept * BRICK_DEV + sent_local)
        global_ids = jnp.where(local_ids < BRICK_DEV, first_brick + local_ids, jnp.where(local_ids < empty_row, remote_ids, BRICKS)).astype(jnp.int32)
        own_bricks = lax.dynamic_slice_in_dim(masked, first_brick, BRICK_DEV, 1)
        own_mask = lax.dynamic_slice_in_dim(mask_full, first_brick, BRICK_DEV, 0)
        padded_block = assemble(source_table, own_bricks, global_ids, BRICK)
        stacked = columns_of(padded_block, BRICK).reshape(27 * C, BRICK_DEV, -1).astype(jnp.float32)
        conv_out = jnp.einsum('rc,rbt->cbt', weight_rows, stacked)
        pre_act = interior(conv_out, BRICK) * own_mask[None]
        gate_value = jax.nn.sigmoid(pre_act)
        activated = (pre_act * gate_value).astype(jnp.bfloat16)
        grad_out = lax.dynamic_slice_in_dim(cotangent, first_brick, BRICK_DEV, 1).astype(jnp.float32)
        grad_conv = (grad_out * own_mask[None] * gate_value * (1.0 + pre_act * (1.0 - gate_value))).astype(jnp.bfloat16)
        grad_window = embed_window(grad_conv, BRICK).astype(jnp.float32)
        grad_weight = grad_weight + jnp.einsum('rbt,cbt->rc', stacked, grad_window)
        products = jnp.einsum('rc,cbt->rbt', weight_rows, grad_window).reshape(27, C, BRICK_DEV, -1)
        grad_block = spread(products, BRICK, padded_block.shape[2], 0)
        center, accumulated = scatter_block(grad_block, local_ids, empty_row + 1, BRICK)
        local_total = center + accumulated[:, :BRICK_DEV]
        current = lax.dynamic_slice_in_dim(grad_total, first_brick, BRICK_DEV, 1)
        grad_total = lax.dynamic_update_slice_in_dim(grad_total, current + local_total, first_brick, 1)
        slot_values = lax.optimization_barrier(accumulated[:, BRICK_DEV:empty_row].astype(jnp.bfloat16)).astype(jnp.float32)
        owners = part_index + step_values
        owners_inside = (owners >= 0) & (owners < N_SPACE)
        owners_kept = jnp.clip(owners, 0, N_SPACE - 1).astype(jnp.int32)
        sent_lists = send_list[owners_kept, move_ids, :]
        targets = jnp.where((sent_lists >= BRICK_DEV) | ~owners_inside[:, None], BRICKS, owners_kept[:, None] * BRICK_DEV + sent_lists).reshape(-1).astype(jnp.int32)
        grad_total = grad_total.at[:, targets].add(slot_values)
        return ((grad_weight, grad_total), activated)
    starting = (jnp.zeros((27 * C, C), jnp.float32), jnp.zeros((C, BRICKS + 1, VOX), jnp.float32))
    (grad_weight, grad_total), outputs = lax.scan(partition, starting, jnp.arange(N_SPACE, dtype=jnp.int32))
    activated = jnp.transpose(outputs, (1, 0, 2, 3)).reshape(C, BRICKS, VOX)
    grad_features = (grad_total[:, :BRICKS] * mask_full[None]).astype(jnp.bfloat16)
    grad_weights = (grad_weight * grad_scale).reshape(27, C, C)
    return (activated, grad_features, grad_weights)
```

```python
import math

import jax
import jax.numpy as jnp
from jax import lax
from jax.experimental import pallas as pl
from jax.experimental.pallas import tpu as pltpu
from jax.sharding import PartitionSpec as P

BF = jnp.bfloat16
F32 = jnp.float32
SIDE = {-1: slice(7, 8), 0: slice(0, 8), 1: slice(0, 1)}
RIM = {-1: slice(0, 1), 0: slice(1, 9), 1: slice(9, 10)}
PLANAR = [(a, b) for a in (-1, 0, 1) for b in (-1, 0, 1)]
MOVES = [m for m in PLANAR if m != (0, 0)]
DW_ROWS = 28 * 32


def slot_of(dx, dy, dz):
    linear = (dx + 1) * 9 + (dy + 1) * 3 + dz + 1
    return linear if linear < 13 else linear - 1


def planar_slots(dx, dy):
    return [None if (dx, dy, dz) == (0, 0, 0) else slot_of(dx, dy, dz) for dz in (-1, 0, 1)]


def tiles(ref_or_value, dx, dy):
    part = ref_or_value[SIDE[dx], SIDE[dy]]
    return part.reshape(-1, 8, 128)


def rims_kernel(send, mask, gathered, local, to_b, face_a):
    for brick in range(2):
        rows = gathered[:, 0, brick].reshape(128, 512).astype(F32) * mask[brick : brick + 1, :]
        local[brick] = rows.T.reshape(8, 8, 8, 128)

    def chosen(move):
        s = send[MOVES.index(move)]
        first, second = (tiles(local[brick], *move) for brick in range(2))
        return jnp.where(s == 0, first, jnp.where(s == 1, second, 0.0))

    for i, b in enumerate((-1, 1)):
        parts = [chosen((0, b)), chosen((-1, b)), chosen((1, b))]
        to_b[i] = jnp.concatenate(parts, axis=0).reshape(80, 128).astype(BF)
    for i, a in enumerate((-1, 1)):
        face_a[i] = chosen((a, 0)).reshape(64, 128).astype(BF)


def main_kernel(
    near, chan, mask, local, from_bm, from_bp, from_am, from_ap, gathered, weights, own_weights,
    act_out, dw_out, own_out, ret_a, ret_b,
    blocks, grads, own_block, act_all, terms,
):
    z = lax.broadcasted_iota(jnp.int32, (1, 8, 128), 1)
    from_b = {-1: from_bm, 1: from_bp}
    from_a = {-1: from_am, 1: from_ap}

    def arrived(dx, dy):
        if dx == 0:
            return from_b[dy][0:64].astype(F32).reshape(8, 8, 128)
        if dy == 0:
            return from_a[dx][0:64].astype(F32).reshape(8, 8, 128)
        edges = from_a[dx][64:80].astype(F32).reshape(2, 8, 128)
        return edges[0:1] if dy == -1 else edges[1:2]

    for dx, dy in PLANAR:
        options = [tiles(local[0], dx, dy), tiles(local[1], dx, dy)]
        rows = [0, 1]
        if (dx, dy) != (0, 0):
            options.append(arrived(dx, dy))
            rows.append(2 + MOVES.index((dx, dy)))

        def pick(r):
            value = 0.0
            for row, option in zip(rows, options):
                value = jnp.where(r == row, option, value)
            return value

        shifted = [[], [], []]
        for brick in range(2):
            below, level, above = planar_slots(dx, dy)
            center = options[brick] if level is None else pick(near[brick, level])
            under, over = pick(near[brick, below]), pick(near[brick, above])
            shifted[0].append(pltpu.roll(jnp.where(z == 7, under, center), 1, 1))
            shifted[1].append(center)
            shifted[2].append(pltpu.roll(jnp.where(z == 0, over, center), 7, 1))
        for i in range(3):
            both = jnp.stack(shifted[i], axis=1)
            count = both.shape[0]
            nx = 8 if dx == 0 else 1
            blocks[i, RIM[dx], RIM[dy]] = both.reshape(nx, count // nx, 16, 128).astype(BF)

    pre = jnp.zeros((1024, 128), F32)
    for dx in range(3):
        left = jnp.concatenate(
            [
                blocks[dz, dx : dx + 8, dy : dy + 8].reshape(1024, 128)
                for dy in range(3)
                for dz in range(3)
            ],
            axis=1,
        )
        right = jnp.concatenate([weights[:, 9 * dx + o].reshape(128, 128) for o in range(9)], axis=0)
        pre = pre + jnp.dot(left, right, preferred_element_type=F32)
    pre = pre.reshape(64, 2, 8, 128)

    back = []
    for brick in range(2):
        on = mask[brick : brick + 1, :]
        pre_act = pre[:, brick].reshape(512, 128).T * on
        gate = jax.nn.sigmoid(pre_act)
        act_all[brick] = (pre_act * gate).astype(BF)
        cotangent = gathered[:, 1, brick].reshape(128, 512).astype(F32)
        grad = cotangent * on * gate * (1.0 + pre_act * (1.0 - gate))
        back.append(grad.T.reshape(64, 8, 128))
    start = pl.multiple_of(chan[0] * 32, 32)
    for brick in range(2):
        act_out[brick] = act_all[brick, pl.ds(start, 32), :]
    back = jnp.stack(back, axis=1).reshape(1024, 128)
    grads[...] = jnp.zeros(grads.shape, BF)
    grads[2:10, 2:10] = back.astype(BF).reshape(8, 8, 16, 128)
    back_t = back.T.astype(BF)

    row = lax.broadcasted_iota(jnp.int32, (384, 128), 0)
    column = lax.broadcasted_iota(jnp.int32, (384, 128), 1)
    wanted = (row >> 7 == column >> 5) & ((row & 127) == chan[0] * 32 + (column & 31))
    select = jnp.where(wanted, 1.0, 0.0).astype(BF)
    stacked = jnp.concatenate([blocks[dz].reshape(1600, 128) for dz in range(3)], axis=1)
    own_block[...] = (
        jnp.dot(stacked, select, preferred_element_type=F32).astype(BF).reshape(10, 10, 16, 128)
    )
    for i, (dx, dy) in enumerate(PLANAR):
        window = own_block[dx + 1 : dx + 9, dy + 1 : dy + 9].reshape(1024, 128)
        product = jnp.dot(back_t, window, preferred_element_type=F32)
        dw_out[96 * i : 96 * i + 96] = product.T[0:96].astype(BF)
    dw_out[864:896] = jnp.zeros((32, 128), BF)

    spread = jnp.zeros((1600, 128), F32)
    for dx in (-1, 0, 1):
        left = jnp.concatenate(
            [
                grads[1 - dx : 11 - dx, 1 - dy : 11 - dy].reshape(1600, 128)
                for dy in (-1, 0, 1)
            ],
            axis=1,
        )
        rights = []
        for dy in (-1, 0, 1):
            first = (dx + 1) * 9 + (dy + 1) * 3
            piece = own_weights[first : first + 3].reshape(96, 128).astype(F32)
            piece = jnp.concatenate([piece, jnp.zeros((32, 128), F32)], axis=0)
            rights.append(piece.T.astype(BF))
        spread = spread + jnp.dot(left, jnp.concatenate(rights, axis=0), preferred_element_type=F32)
    spread = spread.reshape(100, 2, 8, 128)
    for brick in range(2):
        part = spread[:, brick]
        up = pltpu.roll(part, 7, 1)
        down = pltpu.roll(pltpu.roll(part, 64, 2), 1, 1)
        center = (
            pltpu.roll(part, 96, 2) + jnp.where(z < 7, up, 0.0) + jnp.where(z > 0, down, 0.0)
        )
        terms[0, brick] = jnp.where(z == 7, up, 0.0).reshape(10, 10, 8, 128)
        terms[1, brick] = center.reshape(10, 10, 8, 128)
        terms[2, brick] = jnp.where(z == 0, down, 0.0).reshape(10, 10, 8, 128)
    for brick in range(2):
        own_out[brick] = terms[1, brick, 1:9, 1:9]
    edges = {}
    for dx, dy in PLANAR:
        pieces = [
            (near[brick, slot], terms[i, brick, RIM[dx], RIM[dy]])
            for brick in range(2)
            for i, slot in enumerate(planar_slots(dx, dy))
            if slot is not None
        ]

        def collected(target):
            total = 0.0
            for r, piece in pieces:
                total = total + jnp.where(r == target, piece, 0.0)
            return total

        for brick in range(2):
            own_out[brick, SIDE[dx], SIDE[dy]] += collected(brick)
        if (dx, dy) != (0, 0):
            edges[dx, dy] = collected(2 + MOVES.index((dx, dy))).reshape(-1, 8, 128)
    for i, a in enumerate((-1, 1)):
        parts = [edges[a, 0], edges[a, -1], edges[a, 1]]
        ret_a[i] = jnp.concatenate(parts, axis=0).reshape(80, 128).astype(BF)
    for i, b in enumerate((-1, 1)):
        ret_b[i] = edges[0, b].reshape(64, 128).astype(BF)


def final_kernel(send, mask, own, from_am, from_ap, from_bm, from_bp, out, total):
    total[...] = own[...]
    from_a = {-1: from_am, 1: from_ap}
    from_b = {-1: from_bm, 1: from_bp}
    for dx, dy in MOVES:
        s = send[MOVES.index((dx, dy))]
        if dy == 0:
            piece = from_a[dx][0:64].astype(F32).reshape(1, 8, 8, 128)
        elif dx == 0:
            piece = from_b[dy][0:64].astype(F32).reshape(8, 1, 8, 128)
        else:
            both = from_b[dy][64:80].astype(F32).reshape(2, 1, 1, 8, 128)
            piece = both[0] if dx == -1 else both[1]
        for brick in range(2):
            total[brick, SIDE[dx], SIDE[dy]] += jnp.where(s == brick, piece, 0.0)
    for brick in range(2):
        rows = total[brick].reshape(512, 128).T[0:32] * mask[brick : brick + 1, :]
        out[brick] = rows.astype(BF)


SMEM = pl.BlockSpec(memory_space=pltpu.SMEM)
VMEM = pl.BlockSpec(memory_space=pltpu.VMEM)


def call(kernel, name, smem, vmem, outs, scratch, limit):
    shapes = [jax.ShapeDtypeStruct(s, d) for s, d in outs]
    return pl.pallas_call(
        kernel,
        out_shape=shapes,
        in_specs=[SMEM] * len(smem) + [VMEM] * len(vmem),
        out_specs=[VMEM] * len(outs),
        scratch_shapes=[pltpu.VMEM(s, d) for s, d in scratch],
        compiler_params=pltpu.CompilerParams(vmem_limit_bytes=limit << 20),
        name=name,
    )(*smem, *vmem)


def passed_along(shard, by):
    count = lax.axis_size("space")
    pairs = [(i, i + by) for i in range(count) if 0 <= i + by < count]
    return lax.ppermute(shard, "space", pairs)


def unpack_mask(packed):
    shifts = jnp.arange(32, dtype=jnp.int32)
    bits = lax.shift_right_logical(packed[:, :, None], shifts[None, None, :]) & 1
    return bits.reshape(packed.shape[0], packed.shape[1] * 32).astype(F32)


def summed_over_space(part, scale):
    count = lax.axis_size("space")
    inner = 16 if count == 128 else count // 2
    outer = count // inner
    near = [[j * inner + i for i in range(inner)] for j in range(outer)]
    far = [[j * inner + i for j in range(outer)] for i in range(inner)]
    rows = DW_ROWS // inner

    def exchange(values, groups):
        return lax.all_to_all(values, "space", 0, 0, tiled=True, axis_index_groups=groups)

    mine = exchange(part, near).astype(F32).reshape(inner, rows, 128).sum(0)
    mine = exchange(jnp.tile(mine, (outer, 1)), far).reshape(outer, rows, 128).sum(0)
    mine = (mine * scale).astype(BF)
    return exchange(jnp.tile(mine, (inner, 1)), near)


def on_device(features, mask_packed, neighbours, send_list, weights, cotangent):
    chan = lax.axis_index("chan").astype(jnp.int32).reshape(1)
    send = send_list.reshape(8)
    mask = unpack_mask(mask_packed)
    values = jnp.stack([features.transpose(1, 0, 2), cotangent.transpose(1, 0, 2)])
    gathered = lax.all_gather(values, "chan", axis=0)
    all_weights = lax.all_gather(weights, "chan", axis=0)
    local, to_b, face_a = call(
        rims_kernel, "rims", [send], [mask, gathered],
        [((2, 8, 8, 8, 128), F32), ((2, 80, 128), BF), ((2, 64, 128), BF)], [], 16,
    )
    from_bm, from_bp = passed_along(to_b[0], 1), passed_along(to_b[1], -1)
    to_am = jnp.concatenate([face_a[0], from_bm[64:72], from_bp[64:72]], axis=0)
    to_ap = jnp.concatenate([face_a[1], from_bm[72:80], from_bp[72:80]], axis=0)
    from_am, from_ap = passed_along(to_am, 4), passed_along(to_ap, -4)
    act, dw, own, ret_a, ret_b = call(
        main_kernel, "conv", [neighbours, chan],
        [mask, local, from_bm, from_bp, from_am, from_ap, gathered, all_weights, weights],
        [
            ((2, 32, 512), BF), ((DW_ROWS, 128), BF), ((2, 8, 8, 8, 128), F32),
            ((2, 80, 128), BF), ((2, 64, 128), BF),
        ],
        [
            ((3, 10, 10, 16, 128), BF), ((12, 12, 16, 128), BF), ((10, 10, 16, 128), BF),
            ((2, 128, 512), BF), ((3, 2, 10, 10, 8, 128), F32),
        ],
        40,
    )
    back_am, back_ap = passed_along(ret_a[0], -4), passed_along(ret_a[1], 4)
    to_bm = jnp.concatenate([ret_b[0], back_am[64:72], back_ap[64:72]], axis=0)
    to_bp = jnp.concatenate([ret_b[1], back_am[72:80], back_ap[72:80]], axis=0)
    back_bm, back_bp = passed_along(to_bm, -1), passed_along(to_bp, 1)
    scale = 1.0 / math.sqrt(2 * lax.axis_size("space") * 512)
    grad_weights = summed_over_space(dw, scale)[:864].astype(F32).reshape(27, 32, 128)
    (grad,) = call(
        final_kernel, "grad", [send], [mask, own, back_am, back_ap, back_bm, back_bp],
        [((2, 32, 512), BF)], [((2, 8, 8, 8, 128), F32)], 16,
    )
    return act.transpose(1, 0, 2), grad.transpose(1, 0, 2), grad_weights


def solution(mesh):
    return jax.shard_map(
        on_device,
        mesh=mesh,
        in_specs=(
            P("chan", "space", None),
            P("space", None),
            P("space", None),
            P("space", None, None),
            P(None, "chan", None),
            P("chan", "space", None),
        ),
        out_specs=(P("chan", "space", None), P("chan", "space", None), P(None, "chan", None)),
        check_vma=False,
    )
```

```python
import math

import jax
import jax.numpy as jnp
from jax import lax
from jax.experimental import pallas as pl
from jax.experimental.pallas import tpu as pltpu
from jax.sharding import PartitionSpec as P

BF = jnp.bfloat16
F32 = jnp.float32
SIDE = {-1: slice(7, 8), 0: slice(0, 8), 1: slice(0, 1)}
RIM = {-1: slice(0, 1), 0: slice(1, 9), 1: slice(9, 10)}
PLANAR = [(a, b) for a in (-1, 0, 1) for b in (-1, 0, 1)]
MOVES = [m for m in PLANAR if m != (0, 0)]
DW_ROWS = 28 * 32


def slot_of(dx, dy, dz):
    linear = (dx + 1) * 9 + (dy + 1) * 3 + dz + 1
    return linear if linear < 13 else linear - 1


def planar_slots(dx, dy):
    return [None if (dx, dy, dz) == (0, 0, 0) else slot_of(dx, dy, dz) for dz in (-1, 0, 1)]


def tiles(ref_or_value, dx, dy):
    part = ref_or_value[SIDE[dx], SIDE[dy]]
    return part.reshape(-1, 8, 128)


def rims_kernel(send, mask, gathered, local, to_b, face_a):
    for brick in range(2):
        rows = gathered[:, 0, brick].reshape(128, 512).astype(F32) * mask[brick : brick + 1, :]
        local[brick] = rows.T.reshape(8, 8, 8, 128)

    def chosen(move):
        s = send[MOVES.index(move)]
        first, second = (tiles(local[brick], *move) for brick in range(2))
        return jnp.where(s == 0, first, jnp.where(s == 1, second, 0.0))

    for i, b in enumerate((-1, 1)):
        parts = [chosen((0, b)), chosen((-1, b)), chosen((1, b))]
        to_b[i] = jnp.concatenate(parts, axis=0).reshape(80, 128).astype(BF)
    for i, a in enumerate((-1, 1)):
        face_a[i] = chosen((a, 0)).reshape(64, 128).astype(BF)


def main_kernel(
    near, chan, mask, local, from_bm, from_bp, from_am, from_ap, gathered, weights, own_weights,
    act_out, dw_out, own_out, ret_a, ret_b,
    blocks, grads, own_block, act_all, terms,
):
    z = lax.broadcasted_iota(jnp.int32, (1, 8, 128), 1)
    from_b = {-1: from_bm, 1: from_bp}
    from_a = {-1: from_am, 1: from_ap}

    def arrived(dx, dy):
        if dx == 0:
            return from_b[dy][0:64].astype(F32).reshape(8, 8, 128)
        if dy == 0:
            return from_a[dx][0:64].astype(F32).reshape(8, 8, 128)
        edges = from_a[dx][64:80].astype(F32).reshape(2, 8, 128)
        return edges[0:1] if dy == -1 else edges[1:2]

    for dx, dy in PLANAR:
        options = [tiles(local[0], dx, dy), tiles(local[1], dx, dy)]
        rows = [0, 1]
        if (dx, dy) != (0, 0):
            options.append(arrived(dx, dy))
            rows.append(2 + MOVES.index((dx, dy)))

        def pick(r):
            value = 0.0
            for row, option in zip(rows, options):
                value = jnp.where(r == row, option, value)
            return value

        shifted = [[], [], []]
        for brick in range(2):
            below, level, above = planar_slots(dx, dy)
            center = options[brick] if level is None else pick(near[brick, level])
            under, over = pick(near[brick, below]), pick(near[brick, above])
            shifted[0].append(pltpu.roll(jnp.where(z == 7, under, center), 1, 1))
            shifted[1].append(center)
            shifted[2].append(pltpu.roll(jnp.where(z == 0, over, center), 7, 1))
        for i in range(3):
            both = jnp.stack(shifted[i], axis=1)
            count = both.shape[0]
            nx = 8 if dx == 0 else 1
            blocks[i, RIM[dx], RIM[dy]] = both.reshape(nx, count // nx, 16, 128).astype(BF)

    pre = jnp.zeros((1024, 128), F32)
    for dx in range(3):
        left = jnp.concatenate(
            [
                blocks[dz, dx : dx + 8, dy : dy + 8].reshape(1024, 128)
                for dy in range(3)
                for dz in range(3)
            ],
            axis=1,
        )
        right = jnp.concatenate([weights[:, 9 * dx + o].reshape(128, 128) for o in range(9)], axis=0)
        pre = pre + jnp.dot(left, right, preferred_element_type=F32)
    pre = pre.reshape(64, 2, 8, 128)

    back = []
    for brick in range(2):
        on = mask[brick : brick + 1, :]
        pre_act = pre[:, brick].reshape(512, 128).T * on
        gate = jax.nn.sigmoid(pre_act)
        act_all[brick] = (pre_act * gate).astype(BF)
        cotangent = gathered[:, 1, brick].reshape(128, 512).astype(F32)
        grad = cotangent * on * gate * (1.0 + pre_act * (1.0 - gate))
        back.append(grad.T.reshape(64, 8, 128))
    start = pl.multiple_of(chan[0] * 32, 32)
    for brick in range(2):
        act_out[brick] = act_all[brick, pl.ds(start, 32), :]
    back = jnp.stack(back, axis=1).reshape(1024, 128)
    grads[...] = jnp.zeros(grads.shape, BF)
    grads[2:10, 2:10] = back.astype(BF).reshape(8, 8, 16, 128)
    back_t = back.T.astype(BF)

    row = lax.broadcasted_iota(jnp.int32, (384, 128), 0)
    column = lax.broadcasted_iota(jnp.int32, (384, 128), 1)
    wanted = (row >> 7 == column >> 5) & ((row & 127) == chan[0] * 32 + (column & 31))
    select = jnp.where(wanted, 1.0, 0.0).astype(BF)
    stacked = jnp.concatenate([blocks[dz].reshape(1600, 128) for dz in range(3)], axis=1)
    own_block[...] = (
        jnp.dot(stacked, select, preferred_element_type=F32).astype(BF).reshape(10, 10, 16, 128)
    )
    for i, (dx, dy) in enumerate(PLANAR):
        window = own_block[dx + 1 : dx + 9, dy + 1 : dy + 9].reshape(1024, 128)
        product = jnp.dot(back_t, window, preferred_element_type=F32)
        dw_out[96 * i : 96 * i + 96] = product.T[0:96].astype(BF)
    dw_out[864:896] = jnp.zeros((32, 128), BF)

    spread = jnp.zeros((1600, 128), F32)
    for dx in (-1, 0, 1):
        left = jnp.concatenate(
            [
                grads[1 - dx : 11 - dx, 1 - dy : 11 - dy].reshape(1600, 128)
                for dy in (-1, 0, 1)
            ],
            axis=1,
        )
        rights = []
        for dy in (-1, 0, 1):
            first = (dx + 1) * 9 + (dy + 1) * 3
            piece = own_weights[first : first + 3].reshape(96, 128).astype(F32)
            piece = jnp.concatenate([piece, jnp.zeros((32, 128), F32)], axis=0)
            rights.append(piece.T.astype(BF))
        spread = spread + jnp.dot(left, jnp.concatenate(rights, axis=0), preferred_element_type=F32)
    spread = spread.reshape(100, 2, 8, 128)
    for brick in range(2):
        part = spread[:, brick]
        up = pltpu.roll(part, 7, 1)
        down = pltpu.roll(pltpu.roll(part, 64, 2), 1, 1)
        center = (
            pltpu.roll(part, 96, 2) + jnp.where(z < 7, up, 0.0) + jnp.where(z > 0, down, 0.0)
        )
        terms[0, brick] = jnp.where(z == 7, up, 0.0).reshape(10, 10, 8, 128)
        terms[1, brick] = center.reshape(10, 10, 8, 128)
        terms[2, brick] = jnp.where(z == 0, down, 0.0).reshape(10, 10, 8, 128)
    for brick in range(2):
        own_out[brick] = terms[1, brick, 1:9, 1:9]
    edges = {}
    for dx, dy in PLANAR:
        pieces = [
            (near[brick, slot], terms[i, brick, RIM[dx], RIM[dy]])
            for brick in range(2)
            for i, slot in enumerate(planar_slots(dx, dy))
            if slot is not None
        ]

        def collected(target):
            total = 0.0
            for r, piece in pieces:
                total = total + jnp.where(r == target, piece, 0.0)
            return total

        for brick in range(2):
            own_out[brick, SIDE[dx], SIDE[dy]] += collected(brick)
        if (dx, dy) != (0, 0):
            edges[dx, dy] = collected(2 + MOVES.index((dx, dy))).reshape(-1, 8, 128)
    for i, a in enumerate((-1, 1)):
        parts = [edges[a, 0], edges[a, -1], edges[a, 1]]
        ret_a[i] = jnp.concatenate(parts, axis=0).reshape(80, 128).astype(BF)
    for i, b in enumerate((-1, 1)):
        ret_b[i] = edges[0, b].reshape(64, 128).astype(BF)


def final_kernel(send, mask, own, from_am, from_ap, from_bm, from_bp, out, total):
    total[...] = own[...]
    from_a = {-1: from_am, 1: from_ap}
    from_b = {-1: from_bm, 1: from_bp}
    for dx, dy in MOVES:
        s = send[MOVES.index((dx, dy))]
        if dy == 0:
            piece = from_a[dx][0:64].astype(F32).reshape(1, 8, 8, 128)
        elif dx == 0:
            piece = from_b[dy][0:64].astype(F32).reshape(8, 1, 8, 128)
        else:
            both = from_b[dy][64:80].astype(F32).reshape(2, 1, 1, 8, 128)
            piece = both[0] if dx == -1 else both[1]
        for brick in range(2):
            total[brick, SIDE[dx], SIDE[dy]] += jnp.where(s == brick, piece, 0.0)
    for brick in range(2):
        rows = total[brick].reshape(512, 128).T[0:32] * mask[brick : brick + 1, :]
        out[brick] = rows.astype(BF)


SMEM = pl.BlockSpec(memory_space=pltpu.SMEM)
VMEM = pl.BlockSpec(memory_space=pltpu.VMEM)


def call(kernel, name, smem, vmem, outs, scratch, limit):
    shapes = [jax.ShapeDtypeStruct(s, d) for s, d in outs]
    return pl.pallas_call(
        kernel,
        out_shape=shapes,
        in_specs=[SMEM] * len(smem) + [VMEM] * len(vmem),
        out_specs=[VMEM] * len(outs),
        scratch_shapes=[pltpu.VMEM(s, d) for s, d in scratch],
        compiler_params=pltpu.CompilerParams(vmem_limit_bytes=limit << 20),
        name=name,
    )(*smem, *vmem)


def passed_along(shard, by):
    count = lax.axis_size("space")
    pairs = [(i, i + by) for i in range(count) if 0 <= i + by < count]
    return lax.ppermute(shard, "space", pairs)


def unpack_mask(packed):
    shifts = jnp.arange(32, dtype=jnp.int32)
    bits = lax.shift_right_logical(packed[:, :, None], shifts[None, None, :]) & 1
    return bits.reshape(packed.shape[0], packed.shape[1] * 32).astype(F32)


def summed_over_space(part, scale):
    count = lax.axis_size("space")
    inner = 16 if count == 128 else count // 2
    outer = count // inner
    near = [[j * inner + i for i in range(inner)] for j in range(outer)]
    far = [[j * inner + i for j in range(outer)] for i in range(inner)]
    rows = DW_ROWS // inner

    def exchange(values, groups):
        return lax.all_to_all(values, "space", 0, 0, tiled=True, axis_index_groups=groups)

    mine = exchange(part, near).astype(F32).reshape(inner, rows, 128).sum(0)
    mine = exchange(jnp.tile(mine, (outer, 1)), far).reshape(outer, rows, 128).sum(0)
    mine = (mine * scale).astype(BF)
    return exchange(jnp.tile(mine, (inner, 1)), near)


def from_all_chan(part):
    count = lax.axis_size("chan")
    copies = jnp.broadcast_to(part[None], (count,) + part.shape)
    return lax.all_to_all(copies, "chan", 0, 0, tiled=True)


def on_device(features, mask_packed, neighbours, send_list, weights, cotangent):
    chan = lax.axis_index("chan").astype(jnp.int32).reshape(1)
    send = send_list.reshape(8)
    mask = unpack_mask(mask_packed)
    values = jnp.stack([features.transpose(1, 0, 2), cotangent.transpose(1, 0, 2)])
    all_weights = from_all_chan(weights)
    gathered = from_all_chan(values)
    local, to_b, face_a = call(
        rims_kernel, "rims", [send], [mask, gathered],
        [((2, 8, 8, 8, 128), F32), ((2, 80, 128), BF), ((2, 64, 128), BF)], [], 16,
    )
    from_bm, from_bp = passed_along(to_b[0], 1), passed_along(to_b[1], -1)
    to_am = jnp.concatenate([face_a[0], from_bm[64:72], from_bp[64:72]], axis=0)
    to_ap = jnp.concatenate([face_a[1], from_bm[72:80], from_bp[72:80]], axis=0)
    from_am, from_ap = passed_along(to_am, 4), passed_along(to_ap, -4)
    act, dw, own, ret_a, ret_b = call(
        main_kernel, "conv", [neighbours, chan],
        [mask, local, from_bm, from_bp, from_am, from_ap, gathered, all_weights, weights],
        [
            ((2, 32, 512), BF), ((DW_ROWS, 128), BF), ((2, 8, 8, 8, 128), F32),
            ((2, 80, 128), BF), ((2, 64, 128), BF),
        ],
        [
            ((3, 10, 10, 16, 128), BF), ((12, 12, 16, 128), BF), ((10, 10, 16, 128), BF),
            ((2, 128, 512), BF), ((3, 2, 10, 10, 8, 128), F32),
        ],
        40,
    )
    back_am, back_ap = passed_along(ret_a[0], -4), passed_along(ret_a[1], 4)
    to_bm = jnp.concatenate([ret_b[0], back_am[64:72], back_ap[64:72]], axis=0)
    to_bp = jnp.concatenate([ret_b[1], back_am[72:80], back_ap[72:80]], axis=0)
    back_bm, back_bp = passed_along(to_bm, -1), passed_along(to_bp, 1)
    scale = 1.0 / math.sqrt(2 * lax.axis_size("space") * 512)
    grad_weights = summed_over_space(dw, scale)[:864].astype(F32).reshape(27, 32, 128)
    (grad,) = call(
        final_kernel, "grad", [send], [mask, own, back_am, back_ap, back_bm, back_bp],
        [((2, 32, 512), BF)], [((2, 8, 8, 8, 128), F32)], 16,
    )
    return act.transpose(1, 0, 2), grad.transpose(1, 0, 2), grad_weights


def solution(mesh):
    return jax.shard_map(
        on_device,
        mesh=mesh,
        in_specs=(
            P("chan", "space", None),
            P("space", None),
            P("space", None),
            P("space", None, None),
            P(None, "chan", None),
            P("chan", "space", None),
        ),
        out_specs=(P("chan", "space", None), P("chan", "space", None), P(None, "chan", None)),
        check_vma=False,
    )
```

```python
import functools
import math

import jax
import jax.numpy as jnp
from jax import lax
from jax.experimental import pallas as pl
from jax.experimental.pallas import tpu as pltpu
from jax.sharding import PartitionSpec as P

BF = jnp.bfloat16
F32 = jnp.float32
SIDE = {-1: slice(7, 8), 0: slice(0, 8), 1: slice(0, 1)}
RIM = {-1: slice(0, 1), 0: slice(1, 9), 1: slice(9, 10)}
PLANAR = [(a, b) for a in (-1, 0, 1) for b in (-1, 0, 1)]
MOVES = [m for m in PLANAR if m != (0, 0)]
STEPS = {(a, b): 4 * a + b for a, b in MOVES}
GROUP = 16
PART = 64
SENT = PART + 16


def slot_of(dx, dy, dz):
    linear = (dx + 1) * 9 + (dy + 1) * 3 + dz + 1
    return linear if linear < 13 else linear - 1


def planar_slots(dx, dy):
    return [None if (dx, dy, dz) == (0, 0, 0) else slot_of(dx, dy, dz) for dz in (-1, 0, 1)]


def tiles(ref_or_value, dx, dy):
    part = ref_or_value[SIDE[dx], SIDE[dy]]
    return part.reshape(-1, 8, 128)


def packed(rim):
    if rim.shape[0] == 1:
        return jnp.concatenate([rim[0], jnp.zeros((8, 128), F32)], axis=0)
    lane = lax.broadcasted_iota(jnp.int32, (8, 128), 1)
    halves = []
    for first in (0, 4):
        value = rim[first]
        for j in (1, 2, 3):
            value = jnp.where(lane < 32 * j, value, pltpu.roll(rim[first + j], 32 * j, 1))
        halves.append(value)
    return jnp.concatenate(halves, axis=0)


def unpacked(rows, count):
    pieces = []
    for i in range(count):
        value = rows[8 * (i // 4) : 8 * (i // 4) + 8]
        pieces.append(pltpu.roll(value, 128 - 32 * (i % 4), 1) if i % 4 else value)
    return jnp.stack(pieces)


def rims_kernel(send, mask, gathered, local, to_b, face_a):
    for brick in range(2):
        rows = gathered[:, 0, brick].reshape(128, 512).astype(F32) * mask[brick : brick + 1, :]
        local[brick] = rows.T.reshape(8, 8, 8, 128)

    def chosen(move):
        s = send[MOVES.index(move)]
        first, second = (tiles(local[brick], *move) for brick in range(2))
        return jnp.where(s == 0, first, jnp.where(s == 1, second, 0.0))

    for i, b in enumerate((-1, 1)):
        parts = [chosen((0, b)), chosen((-1, b)), chosen((1, b))]
        to_b[i] = jnp.concatenate(parts, axis=0).reshape(80, 128).astype(BF)
    for i, a in enumerate((-1, 1)):
        face_a[i] = chosen((a, 0)).reshape(64, 128).astype(BF)


def main_kernel(
    near, chan, place, mask, local, from_bm, from_bp, from_am, from_ap, gathered, weights, own_weights,
    act_out, sent, own_out,
    blocks, grads, own_block, act_all, terms,
):
    z = lax.broadcasted_iota(jnp.int32, (1, 8, 128), 1)
    from_b = {-1: from_bm, 1: from_bp}
    from_a = {-1: from_am, 1: from_ap}

    def arrived(dx, dy):
        if dx == 0:
            return from_b[dy][0:64].astype(F32).reshape(8, 8, 128)
        if dy == 0:
            return from_a[dx][0:64].astype(F32).reshape(8, 8, 128)
        edges = from_a[dx][64:80].astype(F32).reshape(2, 8, 128)
        return edges[0:1] if dy == -1 else edges[1:2]

    for dx, dy in PLANAR:
        options = [tiles(local[0], dx, dy), tiles(local[1], dx, dy)]
        rows = [0, 1]
        if (dx, dy) != (0, 0):
            options.append(arrived(dx, dy))
            rows.append(2 + MOVES.index((dx, dy)))

        def pick(r):
            value = 0.0
            for row, option in zip(rows, options):
                value = jnp.where(r == row, option, value)
            return value

        shifted = [[], [], []]
        for brick in range(2):
            below, level, above = planar_slots(dx, dy)
            center = options[brick] if level is None else pick(near[brick, level])
            under, over = pick(near[brick, below]), pick(near[brick, above])
            shifted[0].append(pltpu.roll(jnp.where(z == 7, under, center), 1, 1))
            shifted[1].append(center)
            shifted[2].append(pltpu.roll(jnp.where(z == 0, over, center), 7, 1))
        for i in range(3):
            both = jnp.stack(shifted[i], axis=1)
            count = both.shape[0]
            nx = 8 if dx == 0 else 1
            blocks[i, RIM[dx], RIM[dy]] = both.reshape(nx, count // nx, 16, 128).astype(BF)

    pre = jnp.zeros((1024, 128), F32)
    for dx in range(3):
        left = jnp.concatenate(
            [
                blocks[dz, dx : dx + 8, dy : dy + 8].reshape(1024, 128)
                for dy in range(3)
                for dz in range(3)
            ],
            axis=1,
        )
        right = jnp.concatenate([weights[:, 9 * dx + o].reshape(128, 128) for o in range(9)], axis=0)
        pre = pre + jnp.dot(left, right, preferred_element_type=F32)
    pre = pre.reshape(64, 2, 8, 128)

    back = []
    for brick in range(2):
        on = mask[brick : brick + 1, :]
        pre_act = pre[:, brick].reshape(512, 128).T * on
        gate = jax.nn.sigmoid(pre_act)
        act_all[brick] = (pre_act * gate).astype(BF)
        cotangent = gathered[:, 1, brick].reshape(128, 512).astype(F32)
        grad = cotangent * on * gate * (1.0 + pre_act * (1.0 - gate))
        back.append(grad.T.reshape(64, 8, 128))
    start = pl.multiple_of(chan[0] * 32, 32)
    for brick in range(2):
        act_out[brick] = act_all[brick, pl.ds(start, 32), :]
    back = jnp.stack(back, axis=1).reshape(1024, 128)
    grads[...] = jnp.zeros(grads.shape, BF)
    grads[2:10, 2:10] = back.astype(BF).reshape(8, 8, 16, 128)
    back_t = back.T.astype(BF)

    row = lax.broadcasted_iota(jnp.int32, (384, 128), 0)
    column = lax.broadcasted_iota(jnp.int32, (384, 128), 1)
    wanted = (row >> 7 == column >> 5) & ((row & 127) == chan[0] * 32 + (column & 31))
    select = jnp.where(wanted, 1.0, 0.0).astype(BF)
    stacked = jnp.concatenate([blocks[dz].reshape(1600, 128) for dz in range(3)], axis=1)
    own_block[...] = (
        jnp.dot(stacked, select, preferred_element_type=F32).astype(BF).reshape(10, 10, 16, 128)
    )
    for i, (dx, dy) in enumerate(PLANAR):
        window = own_block[dx + 1 : dx + 9, dy + 1 : dy + 9].reshape(1024, 128)
        product = jnp.dot(back_t, window, preferred_element_type=F32)
        product = product.T[0:96].astype(BF)
        for dz in range(3):
            j, half = divmod(3 * i + dz, 2)
            sent[j, 32 * half : 32 * half + 32] = product[32 * dz : 32 * dz + 32]
    sent[13, 32:64] = jnp.zeros((32, 128), BF)
    for j in range(14, GROUP):
        sent[j, 0:PART] = jnp.zeros((PART, 128), BF)
    for j in range(GROUP):
        sent[j, PART:SENT] = jnp.zeros((16, 128), BF)

    spread = jnp.zeros((1600, 128), F32)
    for dx in (-1, 0, 1):
        left = jnp.concatenate(
            [
                grads[1 - dx : 11 - dx, 1 - dy : 11 - dy].reshape(1600, 128)
                for dy in (-1, 0, 1)
            ],
            axis=1,
        )
        rights = []
        for dy in (-1, 0, 1):
            first = (dx + 1) * 9 + (dy + 1) * 3
            piece = own_weights[first : first + 3].reshape(96, 128).astype(F32)
            piece = jnp.concatenate([piece, jnp.zeros((32, 128), F32)], axis=0)
            rights.append(piece.T.astype(BF))
        spread = spread + jnp.dot(left, jnp.concatenate(rights, axis=0), preferred_element_type=F32)
    spread = spread.reshape(100, 2, 8, 128)
    for brick in range(2):
        part = spread[:, brick]
        up = pltpu.roll(part, 7, 1)
        down = pltpu.roll(pltpu.roll(part, 64, 2), 1, 1)
        center = (
            pltpu.roll(part, 96, 2) + jnp.where(z < 7, up, 0.0) + jnp.where(z > 0, down, 0.0)
        )
        terms[0, brick] = jnp.where(z == 7, up, 0.0).reshape(10, 10, 8, 128)
        terms[1, brick] = center.reshape(10, 10, 8, 128)
        terms[2, brick] = jnp.where(z == 0, down, 0.0).reshape(10, 10, 8, 128)
    for brick in range(2):
        own_out[brick] = terms[1, brick, 1:9, 1:9]
    for dx, dy in PLANAR:
        pieces = [
            (near[brick, slot], terms[i, brick, RIM[dx], RIM[dy]])
            for brick in range(2)
            for i, slot in enumerate(planar_slots(dx, dy))
            if slot is not None
        ]

        def collected(target):
            total = 0.0
            for r, piece in pieces:
                total = total + jnp.where(r == target, piece, 0.0)
            return total

        for brick in range(2):
            own_out[brick, SIDE[dx], SIDE[dy]] += collected(brick)
        if (dx, dy) != (0, 0):
            rim = collected(2 + MOVES.index((dx, dy))).reshape(-1, 8, 128)
            target = lax.rem(place[0] + STEPS[dx, dy] + GROUP, GROUP)
            sent[target, PART:SENT] = packed(rim).astype(BF)


def middle_kernel(place, arrived, sent):
    total = arrived[0, 0:PART].astype(F32)
    for j in range(1, GROUP):
        total = total + arrived[j, 0:PART].astype(F32)
    zero = jnp.zeros((16, 128), F32)
    for j in range(sent.shape[0]):
        sent[j, 0:PART] = total
        sent[j, PART : PART + 16] = zero
        sent[j, PART + 16 : PART + 32] = zero
    for a in (-1, 1):
        rims = [
            arrived[lax.rem(place[0] - STEPS[a, b] + GROUP, GROUP), PART:SENT].astype(F32)
            for b in (-1, 0, 1)
        ]
        target = place[1] + a

        @pl.when((target >= 0) & (target < sent.shape[0]))
        def _():
            sent[target, PART : PART + 16] = rims[1]
            sent[target, PART + 16 : PART + 24] = rims[0][0:8]
            sent[target, PART + 24 : PART + 32] = rims[2][0:8]


def sum_kernel(scale, arrived, sent):
    total = arrived[0, 0:PART]
    for j in range(1, arrived.shape[0]):
        total = total + arrived[j, 0:PART]
    total = (total * scale).astype(BF)
    for j in range(GROUP):
        sent[j] = total


def final_kernel(send, place, mask, own, direct, onward, out, total):
    total[...] = own[...]
    inner, outer = place[0], place[1]
    for dx, dy in MOVES:
        s = send[MOVES.index((dx, dy))]
        origin = inner - STEPS[dx, dy]
        rows = direct[lax.rem(origin + GROUP, GROUP), PART:SENT].astype(F32)
        if dx:
            passer = jnp.clip(outer - dx, 0, onward.shape[0] - 1)
            first = PART if dy == 0 else PART + 16 if dy == -1 else PART + 24
            other = onward[passer, first : first + (16 if dy == 0 else 8)]
            inside = (origin >= 0) & (origin < GROUP)
            rows = jnp.where(inside, rows[0 : other.shape[0]], other)
        piece = unpacked(rows, 1 if dx and dy else 8)
        nx = 8 if dx == 0 else 1
        piece = piece.reshape(nx, piece.shape[0] // nx, 8, 128)
        for brick in range(2):
            total[brick, SIDE[dx], SIDE[dy]] += jnp.where(s == brick, piece, 0.0)
    for brick in range(2):
        rows = total[brick].reshape(512, 128).T[0:32] * mask[brick : brick + 1, :]
        out[brick] = rows.astype(BF)


SMEM = pl.BlockSpec(memory_space=pltpu.SMEM)
VMEM = pl.BlockSpec(memory_space=pltpu.VMEM)


def call(kernel, name, smem, vmem, outs, scratch, limit):
    shapes = [jax.ShapeDtypeStruct(s, d) for s, d in outs]
    return pl.pallas_call(
        kernel,
        out_shape=shapes,
        in_specs=[SMEM] * len(smem) + [VMEM] * len(vmem),
        out_specs=[VMEM] * len(outs),
        scratch_shapes=[pltpu.VMEM(s, d) for s, d in scratch],
        compiler_params=pltpu.CompilerParams(vmem_limit_bytes=limit << 20),
        name=name,
    )(*smem, *vmem)


def passed_along(shard, by):
    count = lax.axis_size("space")
    pairs = [(i, i + by) for i in range(count) if 0 <= i + by < count]
    if abs(by) == 1:
        pairs = [(i, j) for i, j in pairs if i // 4 == j // 4]
    return lax.ppermute(shard, "space", pairs)


def unpack_mask(packed):
    shifts = jnp.arange(32, dtype=jnp.int32)
    bits = lax.shift_right_logical(packed[:, :, None], shifts[None, None, :]) & 1
    return bits.reshape(packed.shape[0], packed.shape[1] * 32).astype(F32)


def exchanged(values, far):
    count = lax.axis_size("space")
    planes = count // GROUP
    groups = [[j * GROUP + i for i in range(GROUP)] for j in range(planes)]
    if far:
        groups = [list(members) for members in zip(*groups)]
    return lax.all_to_all(values, "space", 0, 0, tiled=True, axis_index_groups=groups)


def from_all_chan(part):
    count = lax.axis_size("chan")
    copies = jnp.broadcast_to(part[None], (count,) + part.shape)
    return lax.all_to_all(copies, "chan", 0, 0, tiled=True)


def on_device(features, mask_packed, neighbours, send_list, weights, cotangent):
    chan = lax.axis_index("chan").astype(jnp.int32).reshape(1)
    send = send_list.reshape(8)
    where = lax.axis_index("space").astype(jnp.int32)
    place = jnp.stack([where % GROUP, where // GROUP])
    planes = lax.axis_size("space") // GROUP
    mask = unpack_mask(mask_packed)
    values = jnp.stack([features.transpose(1, 0, 2), cotangent.transpose(1, 0, 2)])
    all_weights = from_all_chan(weights)
    gathered = from_all_chan(values)
    local, to_b, face_a = call(
        rims_kernel, "rims", [send], [mask, gathered],
        [((2, 8, 8, 8, 128), F32), ((2, 80, 128), BF), ((2, 64, 128), BF)], [], 16,
    )
    from_bm, from_bp = passed_along(to_b[0], 1), passed_along(to_b[1], -1)
    to_am = jnp.concatenate([face_a[0], from_bm[64:72], from_bp[64:72]], axis=0)
    to_ap = jnp.concatenate([face_a[1], from_bm[72:80], from_bp[72:80]], axis=0)
    from_am, from_ap = passed_along(to_am, 4), passed_along(to_ap, -4)
    act, sent, own = call(
        main_kernel, "conv", [neighbours, chan, place],
        [mask, local, from_bm, from_bp, from_am, from_ap, gathered, all_weights, weights],
        [
            ((2, 32, 512), BF), ((GROUP, SENT, 128), BF), ((2, 8, 8, 8, 128), F32),
        ],
        [
            ((3, 10, 10, 16, 128), BF), ((12, 12, 16, 128), BF), ((10, 10, 16, 128), BF),
            ((2, 128, 512), BF), ((3, 2, 10, 10, 8, 128), F32),
        ],
        40,
    )
    scale = 1.0 / math.sqrt(2 * lax.axis_size("space") * 512)
    direct = exchanged(sent, False)
    (sent,) = call(
        middle_kernel, "middle", [place], [direct], [((planes, PART + 32, 128), F32)], [], 16
    )
    onward = exchanged(sent, True)
    (sent,) = call(
        functools.partial(sum_kernel, scale), "sums", [], [onward], [((GROUP, PART, 128), BF)], [], 16
    )
    summed = exchanged(sent, False).reshape(GROUP * PART, 128)
    grad_weights = summed[:864].astype(F32).reshape(27, 32, 128)
    (grad,) = call(
        final_kernel, "grad", [send, place], [mask, own, direct, onward],
        [((2, 32, 512), BF)], [((2, 8, 8, 8, 128), F32)], 16,
    )
    return act.transpose(1, 0, 2), grad.transpose(1, 0, 2), grad_weights


def solution(mesh):
    return jax.shard_map(
        on_device,
        mesh=mesh,
        in_specs=(
            P("chan", "space", None),
            P("space", None),
            P("space", None),
            P("space", None, None),
            P(None, "chan", None),
            P("chan", "space", None),
        ),
        out_specs=(P("chan", "space", None), P("chan", "space", None), P(None, "chan", None)),
        check_vma=False,
    )
```

```python
import functools
import math

import jax
import jax.numpy as jnp
from jax import lax
from jax.experimental import pallas as pl
from jax.experimental.pallas import tpu as pltpu
from jax.sharding import PartitionSpec as P

BF = jnp.bfloat16
F32 = jnp.float32
SIDE = {-1: slice(7, 8), 0: slice(0, 8), 1: slice(0, 1)}
RIM = {-1: slice(0, 1), 0: slice(1, 9), 1: slice(9, 10)}
PLANAR = [(a, b) for a in (-1, 0, 1) for b in (-1, 0, 1)]
MOVES = [m for m in PLANAR if m != (0, 0)]
STEPS = {(a, b): 4 * a + b for a, b in MOVES}
GROUP = 16
PART = 56
SENT = PART + 16
ONWARD = PART + 24


def slot_of(dx, dy, dz):
    linear = (dx + 1) * 9 + (dy + 1) * 3 + dz + 1
    return linear if linear < 13 else linear - 1


def planar_slots(dx, dy):
    return [None if (dx, dy, dz) == (0, 0, 0) else slot_of(dx, dy, dz) for dz in (-1, 0, 1)]


def tiles(ref_or_value, dx, dy):
    part = ref_or_value[SIDE[dx], SIDE[dy]]
    return part.reshape(-1, 8, 128)


def packed(rim):
    if rim.shape[0] == 1:
        return jnp.concatenate([rim[0], jnp.zeros((8, 128), F32)], axis=0)
    lane = lax.broadcasted_iota(jnp.int32, (8, 128), 1)
    halves = []
    for first in (0, 4):
        value = rim[first]
        for j in (1, 2, 3):
            value = jnp.where(lane < 32 * j, value, pltpu.roll(rim[first + j], 32 * j, 1))
        halves.append(value)
    return jnp.concatenate(halves, axis=0)


def unpacked(rows, count):
    pieces = []
    for i in range(count):
        value = rows[8 * (i // 4) : 8 * (i // 4) + 8]
        pieces.append(pltpu.roll(value, 128 - 32 * (i % 4), 1) if i % 4 else value)
    return jnp.stack(pieces)


def rows_of(index, stride, first, count):
    return pl.ds(pl.multiple_of(index * stride + first, 8), count)


def rims_kernel(send, mask, gathered, local, to_b, face_a):
    for brick in range(2):
        rows = gathered[:, 0, brick].reshape(128, 512).astype(F32) * mask[brick : brick + 1, :]
        local[brick] = rows.T.reshape(8, 8, 8, 128)

    def chosen(move):
        s = send[MOVES.index(move)]
        first, second = (tiles(local[brick], *move) for brick in range(2))
        return jnp.where(s == 0, first, jnp.where(s == 1, second, 0.0))

    for i, b in enumerate((-1, 1)):
        parts = [chosen((0, b)), chosen((-1, b)), chosen((1, b))]
        to_b[i] = jnp.concatenate(parts, axis=0).reshape(80, 128).astype(BF)
    for i, a in enumerate((-1, 1)):
        face_a[i] = chosen((a, 0)).reshape(64, 128).astype(BF)


def main_kernel(
    near, chan, place, mask, local, from_bm, from_bp, from_am, from_ap, gathered, weights, own_weights,
    act_out, sent, own_out,
    blocks, grads, own_block, act_all, terms, stage,
):
    z = lax.broadcasted_iota(jnp.int32, (1, 8, 128), 1)
    from_b = {-1: from_bm, 1: from_bp}
    from_a = {-1: from_am, 1: from_ap}

    def arrived(dx, dy):
        if dx == 0:
            return from_b[dy][0:64].astype(F32).reshape(8, 8, 128)
        if dy == 0:
            return from_a[dx][0:64].astype(F32).reshape(8, 8, 128)
        edges = from_a[dx][64:80].astype(F32).reshape(2, 8, 128)
        return edges[0:1] if dy == -1 else edges[1:2]

    for dx, dy in PLANAR:
        options = [tiles(local[0], dx, dy), tiles(local[1], dx, dy)]
        rows = [0, 1]
        if (dx, dy) != (0, 0):
            options.append(arrived(dx, dy))
            rows.append(2 + MOVES.index((dx, dy)))

        def pick(r):
            value = 0.0
            for row, option in zip(rows, options):
                value = jnp.where(r == row, option, value)
            return value

        shifted = [[], [], []]
        for brick in range(2):
            below, level, above = planar_slots(dx, dy)
            center = options[brick] if level is None else pick(near[brick, level])
            under, over = pick(near[brick, below]), pick(near[brick, above])
            shifted[0].append(pltpu.roll(jnp.where(z == 7, under, center), 1, 1))
            shifted[1].append(center)
            shifted[2].append(pltpu.roll(jnp.where(z == 0, over, center), 7, 1))
        for i in range(3):
            both = jnp.stack(shifted[i], axis=1)
            count = both.shape[0]
            nx = 8 if dx == 0 else 1
            blocks[i, RIM[dx], RIM[dy]] = both.reshape(nx, count // nx, 16, 128).astype(BF)

    pre = jnp.zeros((1024, 128), F32)
    for dx in range(3):
        left = jnp.concatenate(
            [
                blocks[dz, dx : dx + 8, dy : dy + 8].reshape(1024, 128)
                for dy in range(3)
                for dz in range(3)
            ],
            axis=1,
        )
        right = jnp.concatenate([weights[:, 9 * dx + o].reshape(128, 128) for o in range(9)], axis=0)
        pre = pre + jnp.dot(left, right, preferred_element_type=F32)
    pre = pre.reshape(64, 2, 8, 128)

    back = []
    for brick in range(2):
        on = mask[brick : brick + 1, :]
        pre_act = pre[:, brick].reshape(512, 128).T * on
        gate = jax.nn.sigmoid(pre_act)
        act_all[brick] = (pre_act * gate).astype(BF)
        cotangent = gathered[:, 1, brick].reshape(128, 512).astype(F32)
        grad = cotangent * on * gate * (1.0 + pre_act * (1.0 - gate))
        back.append(grad.T.reshape(64, 8, 128))
    start = pl.multiple_of(chan[0] * 32, 32)
    for brick in range(2):
        act_out[brick] = act_all[brick, pl.ds(start, 32), :]
    back = jnp.stack(back, axis=1).reshape(1024, 128)
    grads[...] = jnp.zeros(grads.shape, BF)
    grads[2:10, 2:10] = back.astype(BF).reshape(8, 8, 16, 128)
    back_t = back.T.astype(BF)

    row = lax.broadcasted_iota(jnp.int32, (384, 128), 0)
    column = lax.broadcasted_iota(jnp.int32, (384, 128), 1)
    wanted = (row >> 7 == column >> 5) & ((row & 127) == chan[0] * 32 + (column & 31))
    select = jnp.where(wanted, 1.0, 0.0).astype(BF)
    stacked = jnp.concatenate([blocks[dz].reshape(1600, 128) for dz in range(3)], axis=1)
    own_block[...] = (
        jnp.dot(stacked, select, preferred_element_type=F32).astype(BF).reshape(10, 10, 16, 128)
    )

    def put_part(tile, value):
        first = tile // 7 * SENT + tile % 7 * 8
        stage[first : first + 8] = value

    for i, (dx, dy) in enumerate(PLANAR):
        window = own_block[dx + 1 : dx + 9, dy + 1 : dy + 9].reshape(1024, 128)
        product = jnp.dot(back_t, window, preferred_element_type=F32)
        product = product.T
        for tile in range(12):
            put_part(12 * i + tile, product[8 * tile : 8 * tile + 8])
    for tile in range(108, 112):
        put_part(tile, jnp.zeros((8, 128), F32))
    for j in range(GROUP):
        stage[j * SENT + PART : (j + 1) * SENT] = jnp.zeros((16, 128), F32)

    spread = jnp.zeros((1600, 128), F32)
    for dx in (-1, 0, 1):
        left = jnp.concatenate(
            [
                grads[1 - dx : 11 - dx, 1 - dy : 11 - dy].reshape(1600, 128)
                for dy in (-1, 0, 1)
            ],
            axis=1,
        )
        rights = []
        for dy in (-1, 0, 1):
            first = (dx + 1) * 9 + (dy + 1) * 3
            piece = own_weights[first : first + 3].reshape(96, 128).astype(F32)
            piece = jnp.concatenate([piece, jnp.zeros((32, 128), F32)], axis=0)
            rights.append(piece.T.astype(BF))
        spread = spread + jnp.dot(left, jnp.concatenate(rights, axis=0), preferred_element_type=F32)
    spread = spread.reshape(100, 2, 8, 128)
    for brick in range(2):
        part = spread[:, brick]
        up = pltpu.roll(part, 7, 1)
        down = pltpu.roll(pltpu.roll(part, 64, 2), 1, 1)
        center = (
            pltpu.roll(part, 96, 2) + jnp.where(z < 7, up, 0.0) + jnp.where(z > 0, down, 0.0)
        )
        terms[0, brick] = jnp.where(z == 7, up, 0.0).reshape(10, 10, 8, 128)
        terms[1, brick] = center.reshape(10, 10, 8, 128)
        terms[2, brick] = jnp.where(z == 0, down, 0.0).reshape(10, 10, 8, 128)
    for brick in range(2):
        own_out[brick] = terms[1, brick, 1:9, 1:9]
    for dx, dy in PLANAR:
        pieces = [
            (near[brick, slot], terms[i, brick, RIM[dx], RIM[dy]])
            for brick in range(2)
            for i, slot in enumerate(planar_slots(dx, dy))
            if slot is not None
        ]

        def collected(target):
            total = 0.0
            for r, piece in pieces:
                total = total + jnp.where(r == target, piece, 0.0)
            return total

        for brick in range(2):
            own_out[brick, SIDE[dx], SIDE[dy]] += collected(brick)
        if (dx, dy) != (0, 0):
            rim = collected(2 + MOVES.index((dx, dy))).reshape(-1, 8, 128)
            target = lax.rem(place[0] + STEPS[dx, dy] + GROUP, GROUP)
            stage[rows_of(target, SENT, PART, 16)] = packed(rim)
    sent[...] = stage[...].astype(BF)


def middle_kernel(place, arrived, sent, held, stage):
    held[...] = arrived[...].astype(F32)
    total = held[0:PART]
    for j in range(1, GROUP):
        total = total + held[j * SENT : j * SENT + PART]
    planes = stage.shape[0] // ONWARD
    for j in range(planes):
        stage[j * ONWARD : j * ONWARD + PART] = total
        stage[j * ONWARD + PART : (j + 1) * ONWARD] = jnp.zeros((24, 128), F32)
    lane = lax.broadcasted_iota(jnp.int32, (8, 128), 1)
    for a in (-1, 1):
        rims = {
            b: held[rows_of(lax.rem(place[0] - STEPS[a, b] + GROUP, GROUP), SENT, PART, 16 if b == 0 else 8)]
            for b in (-1, 0, 1)
        }
        edges = jnp.where(lane < 32, rims[-1], pltpu.roll(rims[1], 32, 1))
        target = place[1] + a

        @pl.when((target >= 0) & (target < planes))
        def _():
            stage[rows_of(target, ONWARD, PART, 24)] = jnp.concatenate([rims[0], edges], axis=0)

    sent[...] = stage[...].astype(BF)


def sum_kernel(scale, arrived, sent):
    values = arrived[...].astype(F32)
    total = values[0:PART]
    for j in range(1, values.shape[0] // ONWARD):
        total = total + values[j * ONWARD : j * ONWARD + PART]
    sent[...] = jnp.concatenate([total * scale] * GROUP, axis=0).astype(BF)


def final_kernel(send, place, mask, own, direct, onward, out, total, held, passed):
    total[...] = own[...]
    held[...] = direct[...].astype(F32)
    passed[...] = onward[...].astype(F32)
    inner, outer = place[0], place[1]
    for dx, dy in MOVES:
        s = send[MOVES.index((dx, dy))]
        origin = inner - STEPS[dx, dy]
        size = 8 if dx and dy else 16
        rows = held[rows_of(lax.rem(origin + GROUP, GROUP), SENT, PART, size)]
        if dx:
            passer = jnp.clip(outer - dx, 0, passed.shape[0] // ONWARD - 1)
            other = passed[rows_of(passer, ONWARD, PART + 16 if dy else PART, size)]
            if dy == 1:
                other = pltpu.roll(other, 96, 1)
            rows = jnp.where((origin >= 0) & (origin < GROUP), rows, other)
        piece = unpacked(rows, 1 if dx and dy else 8)
        nx = 8 if dx == 0 else 1
        piece = piece.reshape(nx, piece.shape[0] // nx, 8, 128)
        for brick in range(2):
            total[brick, SIDE[dx], SIDE[dy]] += jnp.where(s == brick, piece, 0.0)
    for brick in range(2):
        rows = total[brick].reshape(512, 128).T[0:32] * mask[brick : brick + 1, :]
        out[brick] = rows.astype(BF)


SMEM = pl.BlockSpec(memory_space=pltpu.SMEM)
VMEM = pl.BlockSpec(memory_space=pltpu.VMEM)


def call(kernel, name, smem, vmem, outs, scratch, limit):
    shapes = [jax.ShapeDtypeStruct(s, d) for s, d in outs]
    return pl.pallas_call(
        kernel,
        out_shape=shapes,
        in_specs=[SMEM] * len(smem) + [VMEM] * len(vmem),
        out_specs=[VMEM] * len(outs),
        scratch_shapes=[pltpu.VMEM(s, d) for s, d in scratch],
        compiler_params=pltpu.CompilerParams(vmem_limit_bytes=limit << 20),
        name=name,
    )(*smem, *vmem)


def passed_along(shard, by):
    count = lax.axis_size("space")
    pairs = [(i, i + by) for i in range(count) if 0 <= i + by < count]
    if abs(by) == 1:
        pairs = [(i, j) for i, j in pairs if i // 4 == j // 4]
    return lax.ppermute(shard, "space", pairs)


def unpack_mask(packed):
    shifts = jnp.arange(32, dtype=jnp.int32)
    bits = lax.shift_right_logical(packed[:, :, None], shifts[None, None, :]) & 1
    return bits.reshape(packed.shape[0], packed.shape[1] * 32).astype(F32)


def exchanged(values, far):
    count = lax.axis_size("space")
    planes = count // GROUP
    groups = [[j * GROUP + i for i in range(GROUP)] for j in range(planes)]
    if far:
        groups = [list(members) for members in zip(*groups)]
    return lax.all_to_all(values, "space", 0, 0, tiled=True, axis_index_groups=groups)


def from_all_chan(part):
    count = lax.axis_size("chan")
    copies = jnp.broadcast_to(part[None], (count,) + part.shape)
    return lax.all_to_all(copies, "chan", 0, 0, tiled=True)


def on_device(features, mask_packed, neighbours, send_list, weights, cotangent):
    chan = lax.axis_index("chan").astype(jnp.int32).reshape(1)
    send = send_list.reshape(8)
    where = lax.axis_index("space").astype(jnp.int32)
    place = jnp.stack([where % GROUP, where // GROUP])
    planes = lax.axis_size("space") // GROUP
    mask = unpack_mask(mask_packed)
    values = jnp.stack([features.transpose(1, 0, 2), cotangent.transpose(1, 0, 2)])
    all_weights = from_all_chan(weights)
    gathered = from_all_chan(values)
    local, to_b, face_a = call(
        rims_kernel, "rims", [send], [mask, gathered],
        [((2, 8, 8, 8, 128), F32), ((2, 80, 128), BF), ((2, 64, 128), BF)], [], 16,
    )
    from_bm, from_bp = passed_along(to_b[0], 1), passed_along(to_b[1], -1)
    to_am = jnp.concatenate([face_a[0], from_bm[64:72], from_bp[64:72]], axis=0)
    to_ap = jnp.concatenate([face_a[1], from_bm[72:80], from_bp[72:80]], axis=0)
    from_am, from_ap = passed_along(to_am, 4), passed_along(to_ap, -4)
    act, sent, own = call(
        main_kernel, "conv", [neighbours, chan, place],
        [mask, local, from_bm, from_bp, from_am, from_ap, gathered, all_weights, weights],
        [
            ((2, 32, 512), BF), ((GROUP * SENT, 128), BF), ((2, 8, 8, 8, 128), F32),
        ],
        [
            ((3, 10, 10, 16, 128), BF), ((12, 12, 16, 128), BF), ((10, 10, 16, 128), BF),
            ((2, 128, 512), BF), ((3, 2, 10, 10, 8, 128), F32), ((GROUP * SENT, 128), F32),
        ],
        40,
    )
    scale = 1.0 / math.sqrt(2 * lax.axis_size("space") * 512)
    direct = exchanged(sent, False)
    (sent,) = call(
        middle_kernel, "middle", [place], [direct], [((planes * ONWARD, 128), BF)],
        [((GROUP * SENT, 128), F32), ((planes * ONWARD, 128), F32)], 16,
    )
    onward = exchanged(sent, True)
    (sent,) = call(
        functools.partial(sum_kernel, scale), "sums", [], [onward], [((GROUP * PART, 128), BF)], [], 16
    )
    summed = exchanged(sent, False)
    grad_weights = summed[:864].astype(F32).reshape(27, 32, 128)
    (grad,) = call(
        final_kernel, "grad", [send, place], [mask, own, direct, onward],
        [((2, 32, 512), BF)],
        [((2, 8, 8, 8, 128), F32), ((GROUP * SENT, 128), F32), ((planes * ONWARD, 128), F32)], 16,
    )
    return act.transpose(1, 0, 2), grad.transpose(1, 0, 2), grad_weights


def solution(mesh):
    return jax.shard_map(
        on_device,
        mesh=mesh,
        in_specs=(
            P("chan", "space", None),
            P("space", None),
            P("space", None),
            P("space", None, None),
            P(None, "chan", None),
            P("chan", "space", None),
        ),
        out_specs=(P("chan", "space", None), P("chan", "space", None), P(None, "chan", None)),
        check_vma=False,
    )
```

```python
import functools
import math

import jax
import jax.numpy as jnp
from jax import lax
from jax.experimental import pallas as pl
from jax.experimental.pallas import tpu as pltpu
from jax.sharding import PartitionSpec as P

BF = jnp.bfloat16
F32 = jnp.float32
SIDE = {-1: slice(7, 8), 0: slice(0, 8), 1: slice(0, 1)}
RIM = {-1: slice(0, 1), 0: slice(1, 9), 1: slice(9, 10)}
PLANAR = [(a, b) for a in (-1, 0, 1) for b in (-1, 0, 1)]
MOVES = [m for m in PLANAR if m != (0, 0)]
STEPS = {(a, b): 4 * a + b for a, b in MOVES}
GROUP = 16
PART = 56
SENT = PART + 16
ONWARD = PART + 24


def slot_of(dx, dy, dz):
    linear = (dx + 1) * 9 + (dy + 1) * 3 + dz + 1
    return linear if linear < 13 else linear - 1


def planar_slots(dx, dy):
    return [None if (dx, dy, dz) == (0, 0, 0) else slot_of(dx, dy, dz) for dz in (-1, 0, 1)]


def tiles(ref_or_value, dx, dy):
    part = ref_or_value[SIDE[dx], SIDE[dy]]
    return part.reshape(-1, 8, 128)


def packed(rim):
    if rim.shape[0] == 1:
        return jnp.concatenate([rim[0], jnp.zeros((8, 128), F32)], axis=0)
    lane = lax.broadcasted_iota(jnp.int32, (8, 128), 1)
    halves = []
    for first in (0, 4):
        value = rim[first]
        for j in (1, 2, 3):
            value = jnp.where(lane < 32 * j, value, pltpu.roll(rim[first + j], 32 * j, 1))
        halves.append(value)
    return jnp.concatenate(halves, axis=0)


def unpacked(rows, count):
    pieces = []
    for i in range(count):
        value = rows[8 * (i // 4) : 8 * (i // 4) + 8]
        pieces.append(pltpu.roll(value, 128 - 32 * (i % 4), 1) if i % 4 else value)
    return jnp.stack(pieces)


def rows_of(index, stride, first, count):
    return pl.ds(pl.multiple_of(index * stride + first, 8), count)


def rims_kernel(send, mask, gathered, local, to_b, face_a):
    for brick in range(2):
        rows = gathered[:, brick].reshape(128, 512).astype(F32) * mask[brick : brick + 1, :]
        local[brick] = rows.T.reshape(8, 8, 8, 128)

    def chosen(move):
        s = send[MOVES.index(move)]
        first, second = (tiles(local[brick], *move) for brick in range(2))
        return jnp.where(s == 0, first, jnp.where(s == 1, second, 0.0))

    for i, b in enumerate((-1, 1)):
        parts = [chosen((0, b)), chosen((-1, b)), chosen((1, b))]
        to_b[i] = jnp.concatenate(parts, axis=0).reshape(80, 128).astype(BF)
    for i, a in enumerate((-1, 1)):
        face_a[i] = chosen((a, 0)).reshape(64, 128).astype(BF)


def main_kernel(
    near, chan, place, mask, local, from_bm, from_bp, from_am, from_ap, extra0, extra1, extra2, extra3,
    act_out, sent, own_out,
    blocks, grads, own_block, act_all, terms, stage, extra,
):
    z = lax.broadcasted_iota(jnp.int32, (1, 8, 128), 1)
    from_b = {-1: from_bm, 1: from_bp}
    from_a = {-1: from_am, 1: from_ap}
    own_weights = extra0
    for by, part in enumerate((extra0, extra1, extra2, extra3)):
        extra[lax.rem(chan[0] - by + 4, 4)] = part[...]

    def arrived(dx, dy):
        if dx == 0:
            return from_b[dy][0:64].astype(F32).reshape(8, 8, 128)
        if dy == 0:
            return from_a[dx][0:64].astype(F32).reshape(8, 8, 128)
        edges = from_a[dx][64:80].astype(F32).reshape(2, 8, 128)
        return edges[0:1] if dy == -1 else edges[1:2]

    for dx, dy in PLANAR:
        options = [tiles(local[0], dx, dy), tiles(local[1], dx, dy)]
        rows = [0, 1]
        if (dx, dy) != (0, 0):
            options.append(arrived(dx, dy))
            rows.append(2 + MOVES.index((dx, dy)))

        def pick(r):
            value = 0.0
            for row, option in zip(rows, options):
                value = jnp.where(r == row, option, value)
            return value

        shifted = [[], [], []]
        for brick in range(2):
            below, level, above = planar_slots(dx, dy)
            center = options[brick] if level is None else pick(near[brick, level])
            under, over = pick(near[brick, below]), pick(near[brick, above])
            shifted[0].append(pltpu.roll(jnp.where(z == 7, under, center), 1, 1))
            shifted[1].append(center)
            shifted[2].append(pltpu.roll(jnp.where(z == 0, over, center), 7, 1))
        for i in range(3):
            both = jnp.stack(shifted[i], axis=1)
            count = both.shape[0]
            nx = 8 if dx == 0 else 1
            blocks[i, RIM[dx], RIM[dy]] = both.reshape(nx, count // nx, 16, 128).astype(BF)

    pre = jnp.zeros((1024, 128), F32)
    for dx in range(3):
        left = jnp.concatenate(
            [
                blocks[dz, dx : dx + 8, dy : dy + 8].reshape(1024, 128)
                for dy in range(3)
                for dz in range(3)
            ],
            axis=1,
        )
        right = jnp.concatenate([extra[:, 9 * dx + o].reshape(128, 128) for o in range(9)], axis=0)
        pre = pre + jnp.dot(left, right, preferred_element_type=F32)
    pre = pre.reshape(64, 2, 8, 128)

    back = []
    for brick in range(2):
        on = mask[brick : brick + 1, :]
        pre_act = pre[:, brick].reshape(512, 128).T * on
        gate = jax.nn.sigmoid(pre_act)
        act_all[brick] = (pre_act * gate).astype(BF)
        cotangent = jnp.concatenate(
            [extra[:, 27 + 4 * brick + i].reshape(128, 128).astype(F32) for i in range(4)], axis=1
        )
        grad = cotangent * on * gate * (1.0 + pre_act * (1.0 - gate))
        back.append(grad.T.reshape(64, 8, 128))
    start = pl.multiple_of(chan[0] * 32, 32)
    for brick in range(2):
        act_out[brick] = act_all[brick, pl.ds(start, 32), :]
    back = jnp.stack(back, axis=1).reshape(1024, 128)
    grads[...] = jnp.zeros(grads.shape, BF)
    grads[2:10, 2:10] = back.astype(BF).reshape(8, 8, 16, 128)
    back_t = back.T.astype(BF)

    row = lax.broadcasted_iota(jnp.int32, (384, 128), 0)
    column = lax.broadcasted_iota(jnp.int32, (384, 128), 1)
    wanted = (row >> 7 == column >> 5) & ((row & 127) == chan[0] * 32 + (column & 31))
    select = jnp.where(wanted, 1.0, 0.0).astype(BF)
    stacked = jnp.concatenate([blocks[dz].reshape(1600, 128) for dz in range(3)], axis=1)
    own_block[...] = (
        jnp.dot(stacked, select, preferred_element_type=F32).astype(BF).reshape(10, 10, 16, 128)
    )

    def put_part(tile, value):
        first = tile // 7 * SENT + tile % 7 * 8
        stage[first : first + 8] = value

    for i, (dx, dy) in enumerate(PLANAR):
        window = own_block[dx + 1 : dx + 9, dy + 1 : dy + 9].reshape(1024, 128)
        product = jnp.dot(back_t, window, preferred_element_type=F32)
        product = product.T
        for tile in range(12):
            put_part(12 * i + tile, product[8 * tile : 8 * tile + 8])
    for tile in range(108, 112):
        put_part(tile, jnp.zeros((8, 128), F32))
    for j in range(GROUP):
        stage[j * SENT + PART : (j + 1) * SENT] = jnp.zeros((16, 128), F32)

    spread = jnp.zeros((1600, 128), F32)
    for dx in (-1, 0, 1):
        left = jnp.concatenate(
            [
                grads[1 - dx : 11 - dx, 1 - dy : 11 - dy].reshape(1600, 128)
                for dy in (-1, 0, 1)
            ],
            axis=1,
        )
        rights = []
        for dy in (-1, 0, 1):
            first = (dx + 1) * 9 + (dy + 1) * 3
            piece = own_weights[first : first + 3].reshape(96, 128).astype(F32)
            piece = jnp.concatenate([piece, jnp.zeros((32, 128), F32)], axis=0)
            rights.append(piece.T.astype(BF))
        spread = spread + jnp.dot(left, jnp.concatenate(rights, axis=0), preferred_element_type=F32)
    spread = spread.reshape(100, 2, 8, 128)
    for brick in range(2):
        part = spread[:, brick]
        up = pltpu.roll(part, 7, 1)
        down = pltpu.roll(pltpu.roll(part, 64, 2), 1, 1)
        center = (
            pltpu.roll(part, 96, 2) + jnp.where(z < 7, up, 0.0) + jnp.where(z > 0, down, 0.0)
        )
        terms[0, brick] = jnp.where(z == 7, up, 0.0).reshape(10, 10, 8, 128)
        terms[1, brick] = center.reshape(10, 10, 8, 128)
        terms[2, brick] = jnp.where(z == 0, down, 0.0).reshape(10, 10, 8, 128)
    for brick in range(2):
        own_out[brick] = terms[1, brick, 1:9, 1:9]
    for dx, dy in PLANAR:
        pieces = [
            (near[brick, slot], terms[i, brick, RIM[dx], RIM[dy]])
            for brick in range(2)
            for i, slot in enumerate(planar_slots(dx, dy))
            if slot is not None
        ]

        def collected(target):
            total = 0.0
            for r, piece in pieces:
                total = total + jnp.where(r == target, piece, 0.0)
            return total

        for brick in range(2):
            own_out[brick, SIDE[dx], SIDE[dy]] += collected(brick)
        if (dx, dy) != (0, 0):
            rim = collected(2 + MOVES.index((dx, dy))).reshape(-1, 8, 128)
            target = lax.rem(place[0] + STEPS[dx, dy] + GROUP, GROUP)
            stage[rows_of(target, SENT, PART, 16)] = packed(rim)
    sent[...] = stage[...].astype(BF)


def middle_kernel(place, arrived, sent, held, stage):
    held[...] = arrived[...].astype(F32)
    total = held[0:PART]
    for j in range(1, GROUP):
        total = total + held[j * SENT : j * SENT + PART]
    planes = stage.shape[0] // ONWARD
    for j in range(planes):
        stage[j * ONWARD : j * ONWARD + PART] = total
        stage[j * ONWARD + PART : (j + 1) * ONWARD] = jnp.zeros((24, 128), F32)
    lane = lax.broadcasted_iota(jnp.int32, (8, 128), 1)
    for a in (-1, 1):
        rims = {
            b: held[rows_of(lax.rem(place[0] - STEPS[a, b] + GROUP, GROUP), SENT, PART, 16 if b == 0 else 8)]
            for b in (-1, 0, 1)
        }
        edges = jnp.where(lane < 32, rims[-1], pltpu.roll(rims[1], 32, 1))
        target = place[1] + a

        @pl.when((target >= 0) & (target < planes))
        def _():
            stage[rows_of(target, ONWARD, PART, 24)] = jnp.concatenate([rims[0], edges], axis=0)

    sent[...] = stage[...].astype(BF)


def sum_kernel(scale, arrived, sent):
    values = arrived[...].astype(F32)
    total = values[0:PART]
    for j in range(1, values.shape[0] // ONWARD):
        total = total + values[j * ONWARD : j * ONWARD + PART]
    sent[...] = jnp.concatenate([total * scale] * GROUP, axis=0).astype(BF)


def final_kernel(send, place, mask, own, direct, onward, out, total, held, passed):
    total[...] = own[...]
    held[...] = direct[...].astype(F32)
    passed[...] = onward[...].astype(F32)
    inner, outer = place[0], place[1]
    for dx, dy in MOVES:
        s = send[MOVES.index((dx, dy))]
        origin = inner - STEPS[dx, dy]
        size = 8 if dx and dy else 16
        rows = held[rows_of(lax.rem(origin + GROUP, GROUP), SENT, PART, size)]
        if dx:
            passer = jnp.clip(outer - dx, 0, passed.shape[0] // ONWARD - 1)
            other = passed[rows_of(passer, ONWARD, PART + 16 if dy else PART, size)]
            if dy == 1:
                other = pltpu.roll(other, 96, 1)
            rows = jnp.where((origin >= 0) & (origin < GROUP), rows, other)
        piece = unpacked(rows, 1 if dx and dy else 8)
        nx = 8 if dx == 0 else 1
        piece = piece.reshape(nx, piece.shape[0] // nx, 8, 128)
        for brick in range(2):
            total[brick, SIDE[dx], SIDE[dy]] += jnp.where(s == brick, piece, 0.0)
    for brick in range(2):
        rows = total[brick].reshape(512, 128).T[0:32] * mask[brick : brick + 1, :]
        out[brick] = rows.astype(BF)


SMEM = pl.BlockSpec(memory_space=pltpu.SMEM)
VMEM = pl.BlockSpec(memory_space=pltpu.VMEM)


def call(kernel, name, smem, vmem, outs, scratch, limit):
    shapes = [jax.ShapeDtypeStruct(s, d) for s, d in outs]
    return pl.pallas_call(
        kernel,
        out_shape=shapes,
        in_specs=[SMEM] * len(smem) + [VMEM] * len(vmem),
        out_specs=[VMEM] * len(outs),
        scratch_shapes=[pltpu.VMEM(s, d) for s, d in scratch],
        compiler_params=pltpu.CompilerParams(vmem_limit_bytes=limit << 20),
        name=name,
    )(*smem, *vmem)


def passed_along(shard, by):
    count = lax.axis_size("space")
    pairs = [(i, i + by) for i in range(count) if 0 <= i + by < count]
    if abs(by) == 1:
        pairs = [(i, j) for i, j in pairs if i // 4 == j // 4]
    return lax.ppermute(shard, "space", pairs)


def unpack_mask(packed):
    shifts = jnp.arange(32, dtype=jnp.int32)
    bits = lax.shift_right_logical(packed[:, :, None], shifts[None, None, :]) & 1
    return bits.reshape(packed.shape[0], packed.shape[1] * 32).astype(F32)


def exchanged(values, far):
    count = lax.axis_size("space")
    planes = count // GROUP
    groups = [[j * GROUP + i for i in range(GROUP)] for j in range(planes)]
    if far:
        groups = [list(members) for members in zip(*groups)]
    return lax.all_to_all(values, "space", 0, 0, tiled=True, axis_index_groups=groups)


def round_chan(shard, by):
    count = lax.axis_size("chan")
    return lax.ppermute(shard, "chan", [(i, (i + by) % count) for i in range(count)])


def from_all_chan(part):
    count = lax.axis_size("chan")
    copies = jnp.broadcast_to(part[None], (count,) + part.shape)
    return lax.all_to_all(copies, "chan", 0, 0, tiled=True)


def on_device(features, mask_packed, neighbours, send_list, weights, cotangent):
    chan = lax.axis_index("chan").astype(jnp.int32).reshape(1)
    send = send_list.reshape(8)
    where = lax.axis_index("space").astype(jnp.int32)
    place = jnp.stack([where % GROUP, where // GROUP])
    planes = lax.axis_size("space") // GROUP
    mask = unpack_mask(mask_packed)
    gathered = from_all_chan(features.transpose(1, 0, 2))
    by_lanes = cotangent.reshape(32, 8, 128).transpose(1, 0, 2)
    extra = jnp.concatenate([weights, by_lanes], axis=0)
    extras = [extra] + [round_chan(extra, by) for by in (1, 2, 3)]
    local, to_b, face_a = call(
        rims_kernel, "rims", [send], [mask, gathered],
        [((2, 8, 8, 8, 128), F32), ((2, 80, 128), BF), ((2, 64, 128), BF)], [], 16,
    )
    from_bm, from_bp = passed_along(to_b[0], 1), passed_along(to_b[1], -1)
    to_am = jnp.concatenate([face_a[0], from_bm[64:72], from_bp[64:72]], axis=0)
    to_ap = jnp.concatenate([face_a[1], from_bm[72:80], from_bp[72:80]], axis=0)
    from_am, from_ap = passed_along(to_am, 4), passed_along(to_ap, -4)
    act, sent, own = call(
        main_kernel, "conv", [neighbours, chan, place],
        [mask, local, from_bm, from_bp, from_am, from_ap, *extras],
        [
            ((2, 32, 512), BF), ((GROUP * SENT, 128), BF), ((2, 8, 8, 8, 128), F32),
        ],
        [
            ((3, 10, 10, 16, 128), BF), ((12, 12, 16, 128), BF), ((10, 10, 16, 128), BF),
            ((2, 128, 512), BF), ((3, 2, 10, 10, 8, 128), F32), ((GROUP * SENT, 128), F32),
            ((4, 35, 32, 128), BF),
        ],
        40,
    )
    scale = 1.0 / math.sqrt(2 * lax.axis_size("space") * 512)
    direct = exchanged(sent, False)
    (sent,) = call(
        middle_kernel, "middle", [place], [direct], [((planes * ONWARD, 128), BF)],
        [((GROUP * SENT, 128), F32), ((planes * ONWARD, 128), F32)], 16,
    )
    onward = exchanged(sent, True)
    (sent,) = call(
        functools.partial(sum_kernel, scale), "sums", [], [onward], [((GROUP * PART, 128), BF)], [], 16
    )
    summed = exchanged(sent, False)
    grad_weights = summed[:864].astype(F32).reshape(27, 32, 128)
    (grad,) = call(
        final_kernel, "grad", [send, place], [mask, own, direct, onward],
        [((2, 32, 512), BF)],
        [((2, 8, 8, 8, 128), F32), ((GROUP * SENT, 128), F32), ((planes * ONWARD, 128), F32)], 16,
    )
    return act.transpose(1, 0, 2), grad.transpose(1, 0, 2), grad_weights


def solution(mesh):
    return jax.shard_map(
        on_device,
        mesh=mesh,
        in_specs=(
            P("chan", "space", None),
            P("space", None),
            P("space", None),
            P("space", None, None),
            P(None, "chan", None),
            P("chan", "space", None),
        ),
        out_specs=(P("chan", "space", None), P("chan", "space", None), P(None, "chan", None)),
        check_vma=False,
    )
```

```python
import functools
import math

import jax
import jax.numpy as jnp
from jax import lax
from jax.experimental import pallas as pl
from jax.experimental.pallas import tpu as pltpu
from jax.sharding import PartitionSpec as P

BF = jnp.bfloat16
F32 = jnp.float32
SIDE = {-1: slice(7, 8), 0: slice(0, 8), 1: slice(0, 1)}
RIM = {-1: slice(0, 1), 0: slice(1, 9), 1: slice(9, 10)}
PLANAR = [(a, b) for a in (-1, 0, 1) for b in (-1, 0, 1)]
MOVES = [m for m in PLANAR if m != (0, 0)]
STEPS = {(a, b): 4 * a + b for a, b in MOVES}
GROUP = 16
PART = 56
SENT = PART + 16
ONWARD = PART + 24


def slot_of(dx, dy, dz):
    linear = (dx + 1) * 9 + (dy + 1) * 3 + dz + 1
    return linear if linear < 13 else linear - 1


def planar_slots(dx, dy):
    return [None if (dx, dy, dz) == (0, 0, 0) else slot_of(dx, dy, dz) for dz in (-1, 0, 1)]


def tiles(ref_or_value, dx, dy):
    part = ref_or_value[SIDE[dx], SIDE[dy]]
    return part.reshape(-1, 8, 128)


def packed(rim):
    if rim.shape[0] == 1:
        return jnp.concatenate([rim[0], jnp.zeros((8, 128), F32)], axis=0)
    lane = lax.broadcasted_iota(jnp.int32, (8, 128), 1)
    halves = []
    for first in (0, 4):
        value = rim[first]
        for j in (1, 2, 3):
            value = jnp.where(lane < 32 * j, value, pltpu.roll(rim[first + j], 32 * j, 1))
        halves.append(value)
    return jnp.concatenate(halves, axis=0)


def unpacked(rows, count):
    pieces = []
    for i in range(count):
        value = rows[8 * (i // 4) : 8 * (i // 4) + 8]
        pieces.append(pltpu.roll(value, 128 - 32 * (i % 4), 1) if i % 4 else value)
    return jnp.stack(pieces)


def rows_of(index, stride, first, count):
    return pl.ds(pl.multiple_of(index * stride + first, 8), count)


def rims_kernel(send, mask, gathered, local, to_b, face_a):
    for brick in range(2):
        rows = gathered[:, brick].reshape(128, 512).astype(F32) * mask[brick : brick + 1, :]
        local[brick] = rows.T.reshape(8, 8, 8, 128)

    def chosen(move):
        s = send[MOVES.index(move)]
        first, second = (tiles(local[brick], *move) for brick in range(2))
        return jnp.where(s == 0, first, jnp.where(s == 1, second, 0.0))

    for i, b in enumerate((-1, 1)):
        parts = [chosen((0, b)), chosen((-1, b)), chosen((1, b))]
        to_b[i] = jnp.concatenate(parts, axis=0).reshape(80, 128).astype(BF)
    for i, a in enumerate((-1, 1)):
        face_a[i] = chosen((a, 0)).reshape(64, 128).astype(BF)


def main_kernel(
    near, chan, place, mask, local, from_bm, from_bp, from_am, from_ap, extra, own_weights,
    act_out, sent, own_out,
    blocks, grads, own_block, act_all, terms, stage,
):
    z = lax.broadcasted_iota(jnp.int32, (1, 8, 128), 1)
    from_b = {-1: from_bm, 1: from_bp}
    from_a = {-1: from_am, 1: from_ap}

    def arrived(dx, dy):
        if dx == 0:
            return from_b[dy][0:64].astype(F32).reshape(8, 8, 128)
        if dy == 0:
            return from_a[dx][0:64].astype(F32).reshape(8, 8, 128)
        edges = from_a[dx][64:80].astype(F32).reshape(2, 8, 128)
        return edges[0:1] if dy == -1 else edges[1:2]

    for dx, dy in PLANAR:
        options = [tiles(local[0], dx, dy), tiles(local[1], dx, dy)]
        rows = [0, 1]
        if (dx, dy) != (0, 0):
            options.append(arrived(dx, dy))
            rows.append(2 + MOVES.index((dx, dy)))

        def pick(r):
            value = 0.0
            for row, option in zip(rows, options):
                value = jnp.where(r == row, option, value)
            return value

        shifted = [[], [], []]
        for brick in range(2):
            below, level, above = planar_slots(dx, dy)
            center = options[brick] if level is None else pick(near[brick, level])
            under, over = pick(near[brick, below]), pick(near[brick, above])
            shifted[0].append(pltpu.roll(jnp.where(z == 7, under, center), 1, 1))
            shifted[1].append(center)
            shifted[2].append(pltpu.roll(jnp.where(z == 0, over, center), 7, 1))
        for i in range(3):
            both = jnp.stack(shifted[i], axis=1)
            count = both.shape[0]
            nx = 8 if dx == 0 else 1
            blocks[i, RIM[dx], RIM[dy]] = both.reshape(nx, count // nx, 16, 128).astype(BF)

    pre = jnp.zeros((1024, 128), F32)
    for dx in range(3):
        left = jnp.concatenate(
            [
                blocks[dz, dx : dx + 8, dy : dy + 8].reshape(1024, 128)
                for dy in range(3)
                for dz in range(3)
            ],
            axis=1,
        )
        right = jnp.concatenate([extra[:, 9 * dx + o].reshape(128, 128) for o in range(9)], axis=0)
        pre = pre + jnp.dot(left, right, preferred_element_type=F32)
    pre = pre.reshape(64, 2, 8, 128)

    back = []
    for brick in range(2):
        on = mask[brick : brick + 1, :]
        pre_act = pre[:, brick].reshape(512, 128).T * on
        gate = jax.nn.sigmoid(pre_act)
        act_all[brick] = (pre_act * gate).astype(BF)
        cotangent = jnp.concatenate(
            [extra[:, 27 + 4 * brick + i].reshape(128, 128).astype(F32) for i in range(4)], axis=1
        )
        grad = cotangent * on * gate * (1.0 + pre_act * (1.0 - gate))
        back.append(grad.T.reshape(64, 8, 128))
    start = pl.multiple_of(chan[0] * 32, 32)
    for brick in range(2):
        act_out[brick] = act_all[brick, pl.ds(start, 32), :]
    back = jnp.stack(back, axis=1).reshape(1024, 128)
    grads[...] = jnp.zeros(grads.shape, BF)
    grads[2:10, 2:10] = back.astype(BF).reshape(8, 8, 16, 128)
    back_t = back.T.astype(BF)

    row = lax.broadcasted_iota(jnp.int32, (384, 128), 0)
    column = lax.broadcasted_iota(jnp.int32, (384, 128), 1)
    wanted = (row >> 7 == column >> 5) & ((row & 127) == chan[0] * 32 + (column & 31))
    select = jnp.where(wanted, 1.0, 0.0).astype(BF)
    stacked = jnp.concatenate([blocks[dz].reshape(1600, 128) for dz in range(3)], axis=1)
    own_block[...] = (
        jnp.dot(stacked, select, preferred_element_type=F32).astype(BF).reshape(10, 10, 16, 128)
    )

    def put_part(tile, value):
        first = tile // 7 * SENT + tile % 7 * 8
        stage[first : first + 8] = value

    for i, (dx, dy) in enumerate(PLANAR):
        window = own_block[dx + 1 : dx + 9, dy + 1 : dy + 9].reshape(1024, 128)
        product = jnp.dot(back_t, window, preferred_element_type=F32)
        product = product.T
        for tile in range(12):
            put_part(12 * i + tile, product[8 * tile : 8 * tile + 8])
    for tile in range(108, 112):
        put_part(tile, jnp.zeros((8, 128), F32))
    for j in range(GROUP):
        stage[j * SENT + PART : (j + 1) * SENT] = jnp.zeros((16, 128), F32)

    spread = jnp.zeros((1600, 128), F32)
    for dx in (-1, 0, 1):
        left = jnp.concatenate(
            [
                grads[1 - dx : 11 - dx, 1 - dy : 11 - dy].reshape(1600, 128)
                for dy in (-1, 0, 1)
            ],
            axis=1,
        )
        rights = []
        for dy in (-1, 0, 1):
            first = (dx + 1) * 9 + (dy + 1) * 3
            piece = own_weights[first : first + 3].reshape(96, 128).astype(F32)
            piece = jnp.concatenate([piece, jnp.zeros((32, 128), F32)], axis=0)
            rights.append(piece.T.astype(BF))
        spread = spread + jnp.dot(left, jnp.concatenate(rights, axis=0), preferred_element_type=F32)
    spread = spread.reshape(100, 2, 8, 128)
    for brick in range(2):
        part = spread[:, brick]
        up = pltpu.roll(part, 7, 1)
        down = pltpu.roll(pltpu.roll(part, 64, 2), 1, 1)
        center = (
            pltpu.roll(part, 96, 2) + jnp.where(z < 7, up, 0.0) + jnp.where(z > 0, down, 0.0)
        )
        terms[0, brick] = jnp.where(z == 7, up, 0.0).reshape(10, 10, 8, 128)
        terms[1, brick] = center.reshape(10, 10, 8, 128)
        terms[2, brick] = jnp.where(z == 0, down, 0.0).reshape(10, 10, 8, 128)
    for brick in range(2):
        own_out[brick] = terms[1, brick, 1:9, 1:9]
    for dx, dy in PLANAR:
        pieces = [
            (near[brick, slot], terms[i, brick, RIM[dx], RIM[dy]])
            for brick in range(2)
            for i, slot in enumerate(planar_slots(dx, dy))
            if slot is not None
        ]

        def collected(target):
            total = 0.0
            for r, piece in pieces:
                total = total + jnp.where(r == target, piece, 0.0)
            return total

        for brick in range(2):
            own_out[brick, SIDE[dx], SIDE[dy]] += collected(brick)
        if (dx, dy) != (0, 0):
            rim = collected(2 + MOVES.index((dx, dy))).reshape(-1, 8, 128)
            target = lax.rem(place[0] + STEPS[dx, dy] + GROUP, GROUP)
            stage[rows_of(target, SENT, PART, 16)] = packed(rim)
    sent[...] = stage[...].astype(BF)


def middle_kernel(place, arrived, sent, held, stage):
    held[...] = arrived[...].astype(F32)
    total = held[0:PART]
    for j in range(1, GROUP):
        total = total + held[j * SENT : j * SENT + PART]
    planes = stage.shape[0] // ONWARD
    for j in range(planes):
        stage[j * ONWARD : j * ONWARD + PART] = total
        stage[j * ONWARD + PART : (j + 1) * ONWARD] = jnp.zeros((24, 128), F32)
    lane = lax.broadcasted_iota(jnp.int32, (8, 128), 1)
    for a in (-1, 1):
        rims = {
            b: held[rows_of(lax.rem(place[0] - STEPS[a, b] + GROUP, GROUP), SENT, PART, 16 if b == 0 else 8)]
            for b in (-1, 0, 1)
        }
        edges = jnp.where(lane < 32, rims[-1], pltpu.roll(rims[1], 32, 1))
        target = place[1] + a

        @pl.when((target >= 0) & (target < planes))
        def _():
            stage[rows_of(target, ONWARD, PART, 24)] = jnp.concatenate([rims[0], edges], axis=0)

    sent[...] = stage[...].astype(BF)


def sum_kernel(scale, arrived, sent):
    values = arrived[...].astype(F32)
    total = values[0:PART]
    for j in range(1, values.shape[0] // ONWARD):
        total = total + values[j * ONWARD : j * ONWARD + PART]
    sent[...] = jnp.concatenate([total * scale] * GROUP, axis=0).astype(BF)


def final_kernel(send, place, mask, own, direct, onward, out, total, held, passed):
    total[...] = own[...]
    held[...] = direct[...].astype(F32)
    passed[...] = onward[...].astype(F32)
    inner, outer = place[0], place[1]
    for dx, dy in MOVES:
        s = send[MOVES.index((dx, dy))]
        origin = inner - STEPS[dx, dy]
        size = 8 if dx and dy else 16
        rows = held[rows_of(lax.rem(origin + GROUP, GROUP), SENT, PART, size)]
        if dx:
            passer = jnp.clip(outer - dx, 0, passed.shape[0] // ONWARD - 1)
            other = passed[rows_of(passer, ONWARD, PART + 16 if dy else PART, size)]
            if dy == 1:
                other = pltpu.roll(other, 96, 1)
            rows = jnp.where((origin >= 0) & (origin < GROUP), rows, other)
        piece = unpacked(rows, 1 if dx and dy else 8)
        nx = 8 if dx == 0 else 1
        piece = piece.reshape(nx, piece.shape[0] // nx, 8, 128)
        for brick in range(2):
            total[brick, SIDE[dx], SIDE[dy]] += jnp.where(s == brick, piece, 0.0)
    for brick in range(2):
        rows = total[brick].reshape(512, 128).T[0:32] * mask[brick : brick + 1, :]
        out[brick] = rows.astype(BF)


SMEM = pl.BlockSpec(memory_space=pltpu.SMEM)
VMEM = pl.BlockSpec(memory_space=pltpu.VMEM)


def call(kernel, name, smem, vmem, outs, scratch, limit):
    shapes = [jax.ShapeDtypeStruct(s, d) for s, d in outs]
    return pl.pallas_call(
        kernel,
        out_shape=shapes,
        in_specs=[SMEM] * len(smem) + [VMEM] * len(vmem),
        out_specs=[VMEM] * len(outs),
        scratch_shapes=[pltpu.VMEM(s, d) for s, d in scratch],
        compiler_params=pltpu.CompilerParams(vmem_limit_bytes=limit << 20),
        name=name,
    )(*smem, *vmem)


def passed_along(shard, by):
    count = lax.axis_size("space")
    pairs = [(i, i + by) for i in range(count) if 0 <= i + by < count]
    if abs(by) == 1:
        pairs = [(i, j) for i, j in pairs if i // 4 == j // 4]
    return lax.ppermute(shard, "space", pairs)


def unpack_mask(packed):
    shifts = jnp.arange(32, dtype=jnp.int32)
    bits = lax.shift_right_logical(packed[:, :, None], shifts[None, None, :]) & 1
    return bits.reshape(packed.shape[0], packed.shape[1] * 32).astype(F32)


def exchanged(values, far):
    count = lax.axis_size("space")
    planes = count // GROUP
    groups = [[j * GROUP + i for i in range(GROUP)] for j in range(planes)]
    if far:
        groups = [list(members) for members in zip(*groups)]
    return lax.all_to_all(values, "space", 0, 0, tiled=True, axis_index_groups=groups)


def from_all_chan(part):
    count = lax.axis_size("chan")
    copies = jnp.broadcast_to(part[None], (count,) + part.shape)
    return lax.all_to_all(copies, "chan", 0, 0, tiled=True)


def on_device(features, mask_packed, neighbours, send_list, weights, cotangent):
    chan = lax.axis_index("chan").astype(jnp.int32).reshape(1)
    send = send_list.reshape(8)
    where = lax.axis_index("space").astype(jnp.int32)
    place = jnp.stack([where % GROUP, where // GROUP])
    planes = lax.axis_size("space") // GROUP
    mask = unpack_mask(mask_packed)
    gathered = from_all_chan(features.transpose(1, 0, 2))
    by_lanes = cotangent.reshape(32, 8, 128).transpose(1, 0, 2)
    extra = jnp.concatenate([weights, by_lanes], axis=0)
    extra = from_all_chan(extra)
    local, to_b, face_a = call(
        rims_kernel, "rims", [send], [mask, gathered],
        [((2, 8, 8, 8, 128), F32), ((2, 80, 128), BF), ((2, 64, 128), BF)], [], 16,
    )
    from_bm, from_bp = passed_along(to_b[0], 1), passed_along(to_b[1], -1)
    to_am = jnp.concatenate([face_a[0], from_bm[64:72], from_bp[64:72]], axis=0)
    to_ap = jnp.concatenate([face_a[1], from_bm[72:80], from_bp[72:80]], axis=0)
    from_am, from_ap = passed_along(to_am, 4), passed_along(to_ap, -4)
    act, sent, own = call(
        main_kernel, "conv", [neighbours, chan, place],
        [mask, local, from_bm, from_bp, from_am, from_ap, extra, weights],
        [
            ((2, 32, 512), BF), ((GROUP * SENT, 128), BF), ((2, 8, 8, 8, 128), F32),
        ],
        [
            ((3, 10, 10, 16, 128), BF), ((12, 12, 16, 128), BF), ((10, 10, 16, 128), BF),
            ((2, 128, 512), BF), ((3, 2, 10, 10, 8, 128), F32), ((GROUP * SENT, 128), F32),
        ],
        40,
    )
    scale = 1.0 / math.sqrt(2 * lax.axis_size("space") * 512)
    direct = exchanged(sent, False)
    (sent,) = call(
        middle_kernel, "middle", [place], [direct], [((planes * ONWARD, 128), BF)],
        [((GROUP * SENT, 128), F32), ((planes * ONWARD, 128), F32)], 16,
    )
    onward = exchanged(sent, True)
    (sent,) = call(
        functools.partial(sum_kernel, scale), "sums", [], [onward], [((GROUP * PART, 128), BF)], [], 16
    )
    summed = exchanged(sent, False)
    grad_weights = summed[:864].astype(F32).reshape(27, 32, 128)
    (grad,) = call(
        final_kernel, "grad", [send, place], [mask, own, direct, onward],
        [((2, 32, 512), BF)],
        [((2, 8, 8, 8, 128), F32), ((GROUP * SENT, 128), F32), ((planes * ONWARD, 128), F32)], 16,
    )
    return act.transpose(1, 0, 2), grad.transpose(1, 0, 2), grad_weights


def solution(mesh):
    return jax.shard_map(
        on_device,
        mesh=mesh,
        in_specs=(
            P("chan", "space", None),
            P("space", None),
            P("space", None),
            P("space", None, None),
            P(None, "chan", None),
            P("chan", "space", None),
        ),
        out_specs=(P("chan", "space", None), P("chan", "space", None), P(None, "chan", None)),
        check_vma=False,
    )
```

```python
import functools
import math

import jax
import jax.numpy as jnp
from jax import lax
from jax.experimental import pallas as pl
from jax.experimental.pallas import tpu as pltpu
from jax.sharding import PartitionSpec as P

BF = jnp.bfloat16
F32 = jnp.float32
SIDE = {-1: slice(7, 8), 0: slice(0, 8), 1: slice(0, 1)}
RIM = {-1: slice(0, 1), 0: slice(1, 9), 1: slice(9, 10)}
PLANAR = [(a, b) for a in (-1, 0, 1) for b in (-1, 0, 1)]
MOVES = [m for m in PLANAR if m != (0, 0)]
STEPS = {(a, b): 4 * a + b for a, b in MOVES}
GROUP = 16
PART = 56
SENT = PART + 16
ONWARD = PART + 24


def slot_of(dx, dy, dz):
    linear = (dx + 1) * 9 + (dy + 1) * 3 + dz + 1
    return linear if linear < 13 else linear - 1


def planar_slots(dx, dy):
    return [None if (dx, dy, dz) == (0, 0, 0) else slot_of(dx, dy, dz) for dz in (-1, 0, 1)]


def tiles(ref_or_value, dx, dy):
    part = ref_or_value[SIDE[dx], SIDE[dy]]
    return part.reshape(-1, 8, 128)


def packed(rim):
    if rim.shape[0] == 1:
        return jnp.concatenate([rim[0], jnp.zeros((8, 128), F32)], axis=0)
    lane = lax.broadcasted_iota(jnp.int32, (8, 128), 1)
    halves = []
    for first in (0, 4):
        value = rim[first]
        for j in (1, 2, 3):
            value = jnp.where(lane < 32 * j, value, pltpu.roll(rim[first + j], 32 * j, 1))
        halves.append(value)
    return jnp.concatenate(halves, axis=0)


def unpacked(rows, count):
    pieces = []
    for i in range(count):
        value = rows[8 * (i // 4) : 8 * (i // 4) + 8]
        pieces.append(pltpu.roll(value, 128 - 32 * (i % 4), 1) if i % 4 else value)
    return jnp.stack(pieces)


def rows_of(index, stride, first, count):
    return pl.ds(pl.multiple_of(index * stride + first, 8), count)


def rims_kernel(send, mask, gathered, local, to_b, face_a):
    for brick in range(2):
        rows = gathered[:, brick].reshape(128, 512).astype(F32) * mask[brick : brick + 1, :]
        local[brick] = rows.T.reshape(8, 8, 8, 128)

    def chosen(move):
        s = send[MOVES.index(move)]
        first, second = (tiles(local[brick], *move) for brick in range(2))
        return jnp.where(s == 0, first, jnp.where(s == 1, second, 0.0))

    for i, b in enumerate((-1, 1)):
        parts = [chosen((0, b)), chosen((-1, b)), chosen((1, b))]
        to_b[i] = jnp.concatenate(parts, axis=0).reshape(80, 128).astype(BF)
    for i, a in enumerate((-1, 1)):
        face_a[i] = chosen((a, 0)).reshape(64, 128).astype(BF)


def main_kernel(
    near, chan, place, mask, local, from_bm, from_bp, from_am, from_ap, extra, own_weights,
    act_out, sent, own_out,
    blocks, grads, own_block, act_all, terms, stage,
):
    z = lax.broadcasted_iota(jnp.int32, (1, 8, 128), 1)
    from_b = {-1: from_bm, 1: from_bp}
    from_a = {-1: from_am, 1: from_ap}

    def arrived(dx, dy):
        if dx == 0:
            return from_b[dy][0:64].astype(F32).reshape(8, 8, 128)
        if dy == 0:
            return from_a[dx][0:64].astype(F32).reshape(8, 8, 128)
        edges = from_a[dx][64:80].astype(F32).reshape(2, 8, 128)
        return edges[0:1] if dy == -1 else edges[1:2]

    for dx, dy in PLANAR:
        options = [tiles(local[0], dx, dy), tiles(local[1], dx, dy)]
        rows = [0, 1]
        if (dx, dy) != (0, 0):
            options.append(arrived(dx, dy))
            rows.append(2 + MOVES.index((dx, dy)))

        def pick(r):
            value = 0.0
            for row, option in zip(rows, options):
                value = jnp.where(r == row, option, value)
            return value

        shifted = [[], [], []]
        for brick in range(2):
            below, level, above = planar_slots(dx, dy)
            center = options[brick] if level is None else pick(near[brick, level])
            under, over = pick(near[brick, below]), pick(near[brick, above])
            shifted[0].append(pltpu.roll(jnp.where(z == 7, under, center), 1, 1))
            shifted[1].append(center)
            shifted[2].append(pltpu.roll(jnp.where(z == 0, over, center), 7, 1))
        for i in range(3):
            both = jnp.stack(shifted[i], axis=1)
            count = both.shape[0]
            nx = 8 if dx == 0 else 1
            blocks[i, RIM[dx], RIM[dy]] = both.reshape(nx, count // nx, 16, 128).astype(BF)

    pre = jnp.zeros((1024, 128), F32)
    for dx in range(3):
        left = jnp.concatenate(
            [
                blocks[dz, dx : dx + 8, dy : dy + 8].reshape(1024, 128)
                for dy in range(3)
                for dz in range(3)
            ],
            axis=1,
        )
        right = jnp.concatenate([extra[:, 9 * dx + o].reshape(128, 128) for o in range(9)], axis=0)
        pre = pre + jnp.dot(left, right, preferred_element_type=F32)
    pre = pre.reshape(64, 2, 8, 128)

    back = []
    for brick in range(2):
        on = mask[brick : brick + 1, :]
        pre_act = pre[:, brick].reshape(512, 128).T * on
        gate = jax.nn.sigmoid(pre_act)
        act_all[brick] = (pre_act * gate).astype(BF)
        cotangent = jnp.concatenate(
            [extra[:, 27 + 4 * brick + i].reshape(128, 128).astype(F32) for i in range(4)], axis=1
        )
        grad = cotangent * on * gate * (1.0 + pre_act * (1.0 - gate))
        back.append(grad.T.reshape(64, 8, 128))
    start = pl.multiple_of(chan[0] * 32, 32)
    for brick in range(2):
        act_out[brick] = act_all[brick, pl.ds(start, 32), :]
    back = jnp.stack(back, axis=1).reshape(1024, 128)
    grads[...] = jnp.zeros(grads.shape, BF)
    grads[2:10, 2:10] = back.astype(BF).reshape(8, 8, 16, 128)
    back_t = back.T.astype(BF)

    row = lax.broadcasted_iota(jnp.int32, (384, 128), 0)
    column = lax.broadcasted_iota(jnp.int32, (384, 128), 1)
    wanted = (row >> 7 == column >> 5) & ((row & 127) == chan[0] * 32 + (column & 31))
    select = jnp.where(wanted, 1.0, 0.0).astype(BF)
    stacked = jnp.concatenate([blocks[dz].reshape(1600, 128) for dz in range(3)], axis=1)
    own_block[...] = (
        jnp.dot(stacked, select, preferred_element_type=F32).astype(BF).reshape(10, 10, 16, 128)
    )

    def put_part(tile, value):
        first = tile // 7 * SENT + tile % 7 * 8
        stage[first : first + 8] = value

    for i, (dx, dy) in enumerate(PLANAR):
        window = own_block[dx + 1 : dx + 9, dy + 1 : dy + 9].reshape(1024, 128)
        product = jnp.dot(back_t, window, preferred_element_type=F32)
        product = product.T
        for tile in range(12):
            put_part(12 * i + tile, product[8 * tile : 8 * tile + 8])
    for tile in range(108, 112):
        put_part(tile, jnp.zeros((8, 128), F32))
    for j in range(GROUP):
        stage[j * SENT + PART : (j + 1) * SENT] = jnp.zeros((16, 128), F32)

    spread = jnp.zeros((1600, 128), F32)
    for dx in (-1, 0, 1):
        left = jnp.concatenate(
            [
                grads[1 - dx : 11 - dx, 1 - dy : 11 - dy].reshape(1600, 128)
                for dy in (-1, 0, 1)
            ],
            axis=1,
        )
        rights = []
        for dy in (-1, 0, 1):
            first = (dx + 1) * 9 + (dy + 1) * 3
            piece = own_weights[first : first + 3].reshape(96, 128).astype(F32)
            piece = jnp.concatenate([piece, jnp.zeros((32, 128), F32)], axis=0)
            rights.append(piece.T.astype(BF))
        spread = spread + jnp.dot(left, jnp.concatenate(rights, axis=0), preferred_element_type=F32)
    spread = spread.reshape(100, 2, 8, 128)
    for brick in range(2):
        part = spread[:, brick]
        up = pltpu.roll(part, 7, 1)
        down = pltpu.roll(pltpu.roll(part, 64, 2), 1, 1)
        center = (
            pltpu.roll(part, 96, 2) + jnp.where(z < 7, up, 0.0) + jnp.where(z > 0, down, 0.0)
        )
        terms[0, brick] = jnp.where(z == 7, up, 0.0).reshape(10, 10, 8, 128)
        terms[1, brick] = center.reshape(10, 10, 8, 128)
        terms[2, brick] = jnp.where(z == 0, down, 0.0).reshape(10, 10, 8, 128)
    for brick in range(2):
        own_out[brick] = terms[1, brick, 1:9, 1:9]
    for dx, dy in PLANAR:
        pieces = [
            (near[brick, slot], terms[i, brick, RIM[dx], RIM[dy]])
            for brick in range(2)
            for i, slot in enumerate(planar_slots(dx, dy))
            if slot is not None
        ]

        def collected(target):
            total = 0.0
            for r, piece in pieces:
                total = total + jnp.where(r == target, piece, 0.0)
            return total

        for brick in range(2):
            own_out[brick, SIDE[dx], SIDE[dy]] += collected(brick)
        if (dx, dy) != (0, 0):
            rim = collected(2 + MOVES.index((dx, dy))).reshape(-1, 8, 128)
            target = lax.rem(place[0] + STEPS[dx, dy] + GROUP, GROUP)
            stage[rows_of(target, SENT, PART, 16)] = packed(rim)
    sent[...] = stage[...].astype(BF)


def middle_kernel(place, arrived, sent, held, stage):
    held[...] = arrived[...].astype(F32)
    total = held[0:PART]
    for j in range(1, GROUP):
        total = total + held[j * SENT : j * SENT + PART]
    planes = stage.shape[0] // ONWARD
    for j in range(planes):
        stage[j * ONWARD : j * ONWARD + PART] = total
        stage[j * ONWARD + PART : (j + 1) * ONWARD] = jnp.zeros((24, 128), F32)
    lane = lax.broadcasted_iota(jnp.int32, (8, 128), 1)
    for a in (-1, 1):
        rims = {
            b: held[rows_of(lax.rem(place[0] - STEPS[a, b] + GROUP, GROUP), SENT, PART, 16 if b == 0 else 8)]
            for b in (-1, 0, 1)
        }
        edges = jnp.where(lane < 32, rims[-1], pltpu.roll(rims[1], 32, 1))
        target = place[1] + a

        @pl.when((target >= 0) & (target < planes))
        def _():
            stage[rows_of(target, ONWARD, PART, 24)] = jnp.concatenate([rims[0], edges], axis=0)

    sent[...] = stage[...].astype(BF)


def sum_kernel(scale, arrived, sent):
    values = arrived[...].astype(F32)
    total = values[0:PART]
    for j in range(1, values.shape[0] // ONWARD):
        total = total + values[j * ONWARD : j * ONWARD + PART]
    sent[...] = jnp.concatenate([total * scale] * GROUP, axis=0).astype(BF)


def final_kernel(send, place, mask, own, direct, onward, out, total, held, passed):
    total[...] = own[...]
    held[...] = direct[...].astype(F32)
    passed[...] = onward[...].astype(F32)
    inner, outer = place[0], place[1]
    for dx, dy in MOVES:
        s = send[MOVES.index((dx, dy))]
        origin = inner - STEPS[dx, dy]
        size = 8 if dx and dy else 16
        rows = held[rows_of(lax.rem(origin + GROUP, GROUP), SENT, PART, size)]
        if dx:
            passer = jnp.clip(outer - dx, 0, passed.shape[0] // ONWARD - 1)
            other = passed[rows_of(passer, ONWARD, PART + 16 if dy else PART, size)]
            if dy == 1:
                other = pltpu.roll(other, 96, 1)
            rows = jnp.where((origin >= 0) & (origin < GROUP), rows, other)
        piece = unpacked(rows, 1 if dx and dy else 8)
        nx = 8 if dx == 0 else 1
        piece = piece.reshape(nx, piece.shape[0] // nx, 8, 128)
        for brick in range(2):
            total[brick, SIDE[dx], SIDE[dy]] += jnp.where(s == brick, piece, 0.0)
    for brick in range(2):
        rows = total[brick].reshape(512, 128).T[0:32] * mask[brick : brick + 1, :]
        out[brick] = rows.astype(BF)


SMEM = pl.BlockSpec(memory_space=pltpu.SMEM)
VMEM = pl.BlockSpec(memory_space=pltpu.VMEM)


def call(kernel, name, smem, vmem, outs, scratch, limit):
    shapes = [jax.ShapeDtypeStruct(s, d) for s, d in outs]
    return pl.pallas_call(
        kernel,
        out_shape=shapes,
        in_specs=[SMEM] * len(smem) + [VMEM] * len(vmem),
        out_specs=[VMEM] * len(outs),
        scratch_shapes=[pltpu.VMEM(s, d) for s, d in scratch],
        compiler_params=pltpu.CompilerParams(vmem_limit_bytes=limit << 20),
        name=name,
    )(*smem, *vmem)


def passed_along(shard, by):
    count = lax.axis_size("space")
    pairs = [(i, i + by) for i in range(count) if 0 <= i + by < count]
    if abs(by) == 1:
        pairs = [(i, j) for i, j in pairs if i // 4 == j // 4]
    return lax.ppermute(shard, "space", pairs)


def unpack_mask(packed):
    shifts = jnp.arange(32, dtype=jnp.int32)
    bits = lax.shift_right_logical(packed[:, :, None], shifts[None, None, :]) & 1
    return bits.reshape(packed.shape[0], packed.shape[1] * 32).astype(F32)


def exchanged(values, far):
    count = lax.axis_size("space")
    planes = count // GROUP
    groups = [[j * GROUP + i for i in range(GROUP)] for j in range(planes)]
    if far:
        groups = [list(members) for members in zip(*groups)]
    return lax.all_to_all(values, "space", 0, 0, tiled=True, axis_index_groups=groups)


def from_all_chan(part):
    count = lax.axis_size("chan")
    copies = jnp.broadcast_to(part[None], (count,) + part.shape)
    return lax.all_to_all(copies, "chan", 0, 0, tiled=True)


def on_device(features, mask_packed, neighbours, send_list, weights, cotangent):
    chan = lax.axis_index("chan").astype(jnp.int32).reshape(1)
    send = send_list.reshape(8)
    where = lax.axis_index("space").astype(jnp.int32)
    place = jnp.stack([where % GROUP, where // GROUP])
    planes = lax.axis_size("space") // GROUP
    mask = unpack_mask(mask_packed)
    gathered = from_all_chan(features.transpose(1, 0, 2))
    by_lanes = cotangent.reshape(32, 8, 128).transpose(1, 0, 2)
    extra = jnp.concatenate([weights, by_lanes], axis=0)
    extra = lax.all_gather(extra, "chan", axis=0)
    local, to_b, face_a = call(
        rims_kernel, "rims", [send], [mask, gathered],
        [((2, 8, 8, 8, 128), F32), ((2, 80, 128), BF), ((2, 64, 128), BF)], [], 16,
    )
    from_bm, from_bp = passed_along(to_b[0], 1), passed_along(to_b[1], -1)
    to_am = jnp.concatenate([face_a[0], from_bm[64:72], from_bp[64:72]], axis=0)
    to_ap = jnp.concatenate([face_a[1], from_bm[72:80], from_bp[72:80]], axis=0)
    from_am, from_ap = passed_along(to_am, 4), passed_along(to_ap, -4)
    act, sent, own = call(
        main_kernel, "conv", [neighbours, chan, place],
        [mask, local, from_bm, from_bp, from_am, from_ap, extra, weights],
        [
            ((2, 32, 512), BF), ((GROUP * SENT, 128), BF), ((2, 8, 8, 8, 128), F32),
        ],
        [
            ((3, 10, 10, 16, 128), BF), ((12, 12, 16, 128), BF), ((10, 10, 16, 128), BF),
            ((2, 128, 512), BF), ((3, 2, 10, 10, 8, 128), F32), ((GROUP * SENT, 128), F32),
        ],
        40,
    )
    scale = 1.0 / math.sqrt(2 * lax.axis_size("space") * 512)
    direct = exchanged(sent, False)
    (sent,) = call(
        middle_kernel, "middle", [place], [direct], [((planes * ONWARD, 128), BF)],
        [((GROUP * SENT, 128), F32), ((planes * ONWARD, 128), F32)], 16,
    )
    onward = exchanged(sent, True)
    (sent,) = call(
        functools.partial(sum_kernel, scale), "sums", [], [onward], [((GROUP * PART, 128), BF)], [], 16
    )
    summed = exchanged(sent, False)
    grad_weights = summed[:864].astype(F32).reshape(27, 32, 128)
    (grad,) = call(
        final_kernel, "grad", [send, place], [mask, own, direct, onward],
        [((2, 32, 512), BF)],
        [((2, 8, 8, 8, 128), F32), ((GROUP * SENT, 128), F32), ((planes * ONWARD, 128), F32)], 16,
    )
    return act.transpose(1, 0, 2), grad.transpose(1, 0, 2), grad_weights


def solution(mesh):
    return jax.shard_map(
        on_device,
        mesh=mesh,
        in_specs=(
            P("chan", "space", None),
            P("space", None),
            P("space", None),
            P("space", None, None),
            P(None, "chan", None),
            P("chan", "space", None),
        ),
        out_specs=(P("chan", "space", None), P("chan", "space", None), P(None, "chan", None)),
        check_vma=False,
    )
```

```python
import functools
import math

import jax
import jax.numpy as jnp
from jax import lax
from jax.experimental import pallas as pl
from jax.experimental.pallas import tpu as pltpu
from jax.sharding import PartitionSpec as P

BF = jnp.bfloat16
F32 = jnp.float32
SIDE = {-1: slice(7, 8), 0: slice(0, 8), 1: slice(0, 1)}
RIM = {-1: slice(0, 1), 0: slice(1, 9), 1: slice(9, 10)}
PLANAR = [(a, b) for a in (-1, 0, 1) for b in (-1, 0, 1)]
MOVES = [m for m in PLANAR if m != (0, 0)]
STEPS = {(a, b): 4 * a + b for a, b in MOVES}
GROUP = 16
PART = 56
SENT = PART + 16
ONWARD = PART + 24


def slot_of(dx, dy, dz):
    linear = (dx + 1) * 9 + (dy + 1) * 3 + dz + 1
    return linear if linear < 13 else linear - 1


def planar_slots(dx, dy):
    return [None if (dx, dy, dz) == (0, 0, 0) else slot_of(dx, dy, dz) for dz in (-1, 0, 1)]


def tiles(ref_or_value, dx, dy):
    part = ref_or_value[SIDE[dx], SIDE[dy]]
    return part.reshape(-1, 8, 128)


def packed(rim):
    if rim.shape[0] == 1:
        return jnp.concatenate([rim[0], jnp.zeros((8, 128), F32)], axis=0)
    lane = lax.broadcasted_iota(jnp.int32, (8, 128), 1)
    halves = []
    for first in (0, 4):
        value = rim[first]
        for j in (1, 2, 3):
            value = jnp.where(lane < 32 * j, value, pltpu.roll(rim[first + j], 32 * j, 1))
        halves.append(value)
    return jnp.concatenate(halves, axis=0)


def unpacked(rows, count):
    pieces = []
    for i in range(count):
        value = rows[8 * (i // 4) : 8 * (i // 4) + 8]
        pieces.append(pltpu.roll(value, 128 - 32 * (i % 4), 1) if i % 4 else value)
    return jnp.stack(pieces)


def rows_of(index, stride, first, count):
    return pl.ds(pl.multiple_of(index * stride + first, 8), count)


def rims_kernel(send, mask, gathered, local, to_b, face_a):
    for brick in range(2):
        rows = gathered[:, brick].reshape(128, 512).astype(F32) * mask[brick : brick + 1, :]
        local[brick] = rows.T.reshape(8, 8, 8, 128)

    def chosen(move):
        s = send[MOVES.index(move)]
        first, second = (tiles(local[brick], *move) for brick in range(2))
        return jnp.where(s == 0, first, jnp.where(s == 1, second, 0.0))

    for i, b in enumerate((-1, 1)):
        parts = [chosen((0, b)), chosen((-1, b)), chosen((1, b))]
        to_b[i] = jnp.concatenate(parts, axis=0).reshape(80, 128).astype(BF)
    for i, a in enumerate((-1, 1)):
        face_a[i] = chosen((a, 0)).reshape(64, 128).astype(BF)


def main_kernel(
    near, chan, place, mask, local, from_bm, from_bp, from_am, from_ap, extra, own_weights,
    act_out, sent, own_out,
    blocks, grads, own_block, act_all, terms, stage,
):
    z = lax.broadcasted_iota(jnp.int32, (1, 8, 128), 1)
    from_b = {-1: from_bm, 1: from_bp}
    from_a = {-1: from_am, 1: from_ap}

    def arrived(dx, dy):
        if dx == 0:
            return from_b[dy][0:64].astype(F32).reshape(8, 8, 128)
        if dy == 0:
            return from_a[dx][0:64].astype(F32).reshape(8, 8, 128)
        edges = from_a[dx][64:80].astype(F32).reshape(2, 8, 128)
        return edges[0:1] if dy == -1 else edges[1:2]

    for dx, dy in PLANAR:
        options = [tiles(local[0], dx, dy), tiles(local[1], dx, dy)]
        rows = [0, 1]
        if (dx, dy) != (0, 0):
            options.append(arrived(dx, dy))
            rows.append(2 + MOVES.index((dx, dy)))

        def pick(r):
            value = 0.0
            for row, option in zip(rows, options):
                value = jnp.where(r == row, option, value)
            return value

        shifted = [[], [], []]
        for brick in range(2):
            below, level, above = planar_slots(dx, dy)
            center = options[brick] if level is None else pick(near[brick, level])
            under, over = pick(near[brick, below]), pick(near[brick, above])
            shifted[0].append(pltpu.roll(jnp.where(z == 7, under, center), 1, 1))
            shifted[1].append(center)
            shifted[2].append(pltpu.roll(jnp.where(z == 0, over, center), 7, 1))
        for i in range(3):
            both = jnp.stack(shifted[i], axis=1)
            count = both.shape[0]
            nx = 8 if dx == 0 else 1
            blocks[i, RIM[dx], RIM[dy]] = both.reshape(nx, count // nx, 16, 128).astype(BF)

    def lefts(first, count):
        return jnp.concatenate(
            [
                blocks[dz, dx : dx + 8, first : first + count].reshape(128 * count, 128)
                for dx in range(3)
                for dz in range(3)
            ],
            axis=1,
        )

    def rights(dy):
        return jnp.concatenate(
            [
                extra[:, 9 * dx + 3 * dy + dz].reshape(128, 128)
                for dx in range(3)
                for dz in range(3)
            ],
            axis=0,
        )

    pair = jnp.concatenate([rights(0), rights(1)], axis=1)
    pair = jnp.dot(lefts(0, 9), pair, preferred_element_type=F32).reshape(8, 9, 16, 256)
    pre = jnp.dot(lefts(2, 8), rights(2), preferred_element_type=F32).reshape(8, 8, 16, 128)
    pre = pre + pair[:, 0:8, :, 0:128] + pair[:, 1:9, :, 128:256]
    pre = pre.reshape(64, 2, 8, 128)

    back = []
    for brick in range(2):
        on = mask[brick : brick + 1, :]
        pre_act = pre[:, brick].reshape(512, 128).T * on
        gate = jax.nn.sigmoid(pre_act)
        act_all[brick] = (pre_act * gate).astype(BF)
        cotangent = jnp.concatenate(
            [extra[:, 27 + 4 * brick + i].reshape(128, 128).astype(F32) for i in range(4)], axis=1
        )
        grad = cotangent * on * gate * (1.0 + pre_act * (1.0 - gate))
        back.append(grad.T.reshape(64, 8, 128))
    start = pl.multiple_of(chan[0] * 32, 32)
    for brick in range(2):
        act_out[brick] = act_all[brick, pl.ds(start, 32), :]
    back = jnp.stack(back, axis=1).reshape(1024, 128)
    grads[...] = jnp.zeros(grads.shape, BF)
    grads[2:10, 2:10] = back.astype(BF).reshape(8, 8, 16, 128)
    back_t = back.T.astype(BF)

    row = lax.broadcasted_iota(jnp.int32, (384, 128), 0)
    column = lax.broadcasted_iota(jnp.int32, (384, 128), 1)
    wanted = (row >> 7 == column >> 5) & ((row & 127) == chan[0] * 32 + (column & 31))
    select = jnp.where(wanted, 1.0, 0.0).astype(BF)
    stacked = jnp.concatenate([blocks[dz].reshape(1600, 128) for dz in range(3)], axis=1)
    own_block[...] = (
        jnp.dot(stacked, select, preferred_element_type=F32).astype(BF).reshape(10, 10, 16, 128)
    )

    def put_part(tile, value):
        first = tile // 7 * SENT + tile % 7 * 8
        stage[first : first + 8] = value

    for first in range(0, 9, 2):
        windows = [
            own_block[dx + 1 : dx + 9, dy + 1 : dy + 9].reshape(1024, 128)
            for dx, dy in PLANAR[first : first + 2]
        ]
        product = jnp.dot(back_t, jnp.concatenate(windows, axis=1), preferred_element_type=F32)
        for i in range(len(windows)):
            turned = product[:, 128 * i : 128 * i + 128].T
            for tile in range(12):
                put_part(12 * (first + i) + tile, turned[8 * tile : 8 * tile + 8])
    for tile in range(108, 112):
        put_part(tile, jnp.zeros((8, 128), F32))
    for j in range(GROUP):
        stage[j * SENT + PART : (j + 1) * SENT] = jnp.zeros((16, 128), F32)

    def grad_lefts(first, count):
        return jnp.concatenate(
            [
                grads[1 - dx : 11 - dx, first : first + count].reshape(160 * count, 128)
                for dx in (-1, 0, 1)
            ],
            axis=1,
        )

    def grad_rights(dy):
        pieces = []
        for dx in (-1, 0, 1):
            first = (dx + 1) * 9 + (dy + 1) * 3
            piece = own_weights[first : first + 3].reshape(96, 128).astype(F32)
            piece = jnp.concatenate([piece, jnp.zeros((32, 128), F32)], axis=0)
            pieces.append(piece.T.astype(BF))
        return jnp.concatenate(pieces, axis=0)

    pair = jnp.concatenate([grad_rights(1), grad_rights(0)], axis=1)
    pair = jnp.dot(grad_lefts(0, 11), pair, preferred_element_type=F32).reshape(10, 11, 16, 256)
    spread = jnp.dot(grad_lefts(2, 10), grad_rights(-1), preferred_element_type=F32)
    spread = spread.reshape(10, 10, 16, 128)
    spread = spread + pair[:, 0:10, :, 0:128] + pair[:, 1:11, :, 128:256]
    spread = spread.reshape(100, 2, 8, 128)
    for brick in range(2):
        part = spread[:, brick]
        up = pltpu.roll(part, 7, 1)
        down = pltpu.roll(pltpu.roll(part, 64, 2), 1, 1)
        center = (
            pltpu.roll(part, 96, 2) + jnp.where(z < 7, up, 0.0) + jnp.where(z > 0, down, 0.0)
        )
        terms[0, brick] = jnp.where(z == 7, up, 0.0).reshape(10, 10, 8, 128)
        terms[1, brick] = center.reshape(10, 10, 8, 128)
        terms[2, brick] = jnp.where(z == 0, down, 0.0).reshape(10, 10, 8, 128)
    for brick in range(2):
        own_out[brick] = terms[1, brick, 1:9, 1:9]
    for dx, dy in PLANAR:
        pieces = [
            (near[brick, slot], terms[i, brick, RIM[dx], RIM[dy]])
            for brick in range(2)
            for i, slot in enumerate(planar_slots(dx, dy))
            if slot is not None
        ]

        def collected(target):
            total = 0.0
            for r, piece in pieces:
                total = total + jnp.where(r == target, piece, 0.0)
            return total

        for brick in range(2):
            own_out[brick, SIDE[dx], SIDE[dy]] += collected(brick)
        if (dx, dy) != (0, 0):
            rim = collected(2 + MOVES.index((dx, dy))).reshape(-1, 8, 128)
            target = lax.rem(place[0] + STEPS[dx, dy] + GROUP, GROUP)
            stage[rows_of(target, SENT, PART, 16)] = packed(rim)
    sent[...] = stage[...].astype(BF)


def middle_kernel(place, arrived, sent, held, stage):
    held[...] = arrived[...].astype(F32)
    total = held[0:PART]
    for j in range(1, GROUP):
        total = total + held[j * SENT : j * SENT + PART]
    planes = stage.shape[0] // ONWARD
    for j in range(planes):
        stage[j * ONWARD : j * ONWARD + PART] = total
        stage[j * ONWARD + PART : (j + 1) * ONWARD] = jnp.zeros((24, 128), F32)
    lane = lax.broadcasted_iota(jnp.int32, (8, 128), 1)
    for a in (-1, 1):
        rims = {
            b: held[rows_of(lax.rem(place[0] - STEPS[a, b] + GROUP, GROUP), SENT, PART, 16 if b == 0 else 8)]
            for b in (-1, 0, 1)
        }
        edges = jnp.where(lane < 32, rims[-1], pltpu.roll(rims[1], 32, 1))
        target = place[1] + a

        @pl.when((target >= 0) & (target < planes))
        def _():
            stage[rows_of(target, ONWARD, PART, 24)] = jnp.concatenate([rims[0], edges], axis=0)

    sent[...] = stage[...].astype(BF)


def sum_kernel(scale, arrived, sent):
    values = arrived[...].astype(F32)
    total = values[0:PART]
    for j in range(1, values.shape[0] // ONWARD):
        total = total + values[j * ONWARD : j * ONWARD + PART]
    sent[...] = jnp.concatenate([total * scale] * GROUP, axis=0).astype(BF)


def final_kernel(send, place, mask, own, direct, onward, out, total, held, passed):
    total[...] = own[...]
    held[...] = direct[...].astype(F32)
    passed[...] = onward[...].astype(F32)
    inner, outer = place[0], place[1]
    for dx, dy in MOVES:
        s = send[MOVES.index((dx, dy))]
        origin = inner - STEPS[dx, dy]
        size = 8 if dx and dy else 16
        rows = held[rows_of(lax.rem(origin + GROUP, GROUP), SENT, PART, size)]
        if dx:
            passer = jnp.clip(outer - dx, 0, passed.shape[0] // ONWARD - 1)
            other = passed[rows_of(passer, ONWARD, PART + 16 if dy else PART, size)]
            if dy == 1:
                other = pltpu.roll(other, 96, 1)
            rows = jnp.where((origin >= 0) & (origin < GROUP), rows, other)
        piece = unpacked(rows, 1 if dx and dy else 8)
        nx = 8 if dx == 0 else 1
        piece = piece.reshape(nx, piece.shape[0] // nx, 8, 128)
        for brick in range(2):
            total[brick, SIDE[dx], SIDE[dy]] += jnp.where(s == brick, piece, 0.0)
    for brick in range(2):
        rows = total[brick].reshape(512, 128).T[0:32] * mask[brick : brick + 1, :]
        out[brick] = rows.astype(BF)


SMEM = pl.BlockSpec(memory_space=pltpu.SMEM)
VMEM = pl.BlockSpec(memory_space=pltpu.VMEM)


def call(kernel, name, smem, vmem, outs, scratch, limit):
    shapes = [jax.ShapeDtypeStruct(s, d) for s, d in outs]
    return pl.pallas_call(
        kernel,
        out_shape=shapes,
        in_specs=[SMEM] * len(smem) + [VMEM] * len(vmem),
        out_specs=[VMEM] * len(outs),
        scratch_shapes=[pltpu.VMEM(s, d) for s, d in scratch],
        compiler_params=pltpu.CompilerParams(vmem_limit_bytes=limit << 20),
        name=name,
    )(*smem, *vmem)


def passed_along(shard, by):
    count = lax.axis_size("space")
    pairs = [(i, i + by) for i in range(count) if 0 <= i + by < count]
    if abs(by) == 1:
        pairs = [(i, j) for i, j in pairs if i // 4 == j // 4]
    return lax.ppermute(shard, "space", pairs)


def unpack_mask(packed):
    shifts = jnp.arange(32, dtype=jnp.int32)
    bits = lax.shift_right_logical(packed[:, :, None], shifts[None, None, :]) & 1
    return bits.reshape(packed.shape[0], packed.shape[1] * 32).astype(F32)


def exchanged(values, far):
    count = lax.axis_size("space")
    planes = count // GROUP
    groups = [[j * GROUP + i for i in range(GROUP)] for j in range(planes)]
    if far:
        groups = [list(members) for members in zip(*groups)]
    return lax.all_to_all(values, "space", 0, 0, tiled=True, axis_index_groups=groups)


def from_all_chan(part):
    count = lax.axis_size("chan")
    copies = jnp.broadcast_to(part[None], (count,) + part.shape)
    return lax.all_to_all(copies, "chan", 0, 0, tiled=True)


def on_device(features, mask_packed, neighbours, send_list, weights, cotangent):
    chan = lax.axis_index("chan").astype(jnp.int32).reshape(1)
    send = send_list.reshape(8)
    where = lax.axis_index("space").astype(jnp.int32)
    place = jnp.stack([where % GROUP, where // GROUP])
    planes = lax.axis_size("space") // GROUP
    mask = unpack_mask(mask_packed)
    gathered = from_all_chan(features.transpose(1, 0, 2))
    by_lanes = cotangent.reshape(32, 8, 128).transpose(1, 0, 2)
    extra = jnp.concatenate([weights, by_lanes], axis=0)
    extra = from_all_chan(extra)
    local, to_b, face_a = call(
        rims_kernel, "rims", [send], [mask, gathered],
        [((2, 8, 8, 8, 128), F32), ((2, 80, 128), BF), ((2, 64, 128), BF)], [], 16,
    )
    from_bm, from_bp = passed_along(to_b[0], 1), passed_along(to_b[1], -1)
    to_am = jnp.concatenate([face_a[0], from_bm[64:72], from_bp[64:72]], axis=0)
    to_ap = jnp.concatenate([face_a[1], from_bm[72:80], from_bp[72:80]], axis=0)
    from_am, from_ap = passed_along(to_am, 4), passed_along(to_ap, -4)
    act, sent, own = call(
        main_kernel, "conv", [neighbours, chan, place],
        [mask, local, from_bm, from_bp, from_am, from_ap, extra, weights],
        [
            ((2, 32, 512), BF), ((GROUP * SENT, 128), BF), ((2, 8, 8, 8, 128), F32),
        ],
        [
            ((3, 10, 10, 16, 128), BF), ((12, 12, 16, 128), BF), ((10, 10, 16, 128), BF),
            ((2, 128, 512), BF), ((3, 2, 10, 10, 8, 128), F32), ((GROUP * SENT, 128), F32),
        ],
        40,
    )
    scale = 1.0 / math.sqrt(2 * lax.axis_size("space") * 512)
    direct = exchanged(sent, False)
    (sent,) = call(
        middle_kernel, "middle", [place], [direct], [((planes * ONWARD, 128), BF)],
        [((GROUP * SENT, 128), F32), ((planes * ONWARD, 128), F32)], 16,
    )
    onward = exchanged(sent, True)
    (sent,) = call(
        functools.partial(sum_kernel, scale), "sums", [], [onward], [((GROUP * PART, 128), BF)], [], 16
    )
    summed = exchanged(sent, False)
    grad_weights = summed[:864].astype(F32).reshape(27, 32, 128)
    (grad,) = call(
        final_kernel, "grad", [send, place], [mask, own, direct, onward],
        [((2, 32, 512), BF)],
        [((2, 8, 8, 8, 128), F32), ((GROUP * SENT, 128), F32), ((planes * ONWARD, 128), F32)], 16,
    )
    return act.transpose(1, 0, 2), grad.transpose(1, 0, 2), grad_weights


def solution(mesh):
    return jax.shard_map(
        on_device,
        mesh=mesh,
        in_specs=(
            P("chan", "space", None),
            P("space", None),
            P("space", None),
            P("space", None, None),
            P(None, "chan", None),
            P("chan", "space", None),
        ),
        out_specs=(P("chan", "space", None), P("chan", "space", None), P(None, "chan", None)),
        check_vma=False,
    )
```

```python
import functools
import math

import jax
import jax.numpy as jnp
from jax import lax
from jax.experimental import pallas as pl
from jax.experimental.pallas import tpu as pltpu
from jax.sharding import PartitionSpec as P

BF = jnp.bfloat16
F32 = jnp.float32
SIDE = {-1: slice(7, 8), 0: slice(0, 8), 1: slice(0, 1)}
RIM = {-1: slice(0, 1), 0: slice(1, 9), 1: slice(9, 10)}
PLANAR = [(a, b) for a in (-1, 0, 1) for b in (-1, 0, 1)]
MOVES = [m for m in PLANAR if m != (0, 0)]
STEPS = {(a, b): 4 * a + b for a, b in MOVES}
GROUP = 16
PART = 56
SENT = PART + 16
ONWARD = PART + 24


def slot_of(dx, dy, dz):
    linear = (dx + 1) * 9 + (dy + 1) * 3 + dz + 1
    return linear if linear < 13 else linear - 1


def planar_slots(dx, dy):
    return [None if (dx, dy, dz) == (0, 0, 0) else slot_of(dx, dy, dz) for dz in (-1, 0, 1)]


def tiles(ref_or_value, dx, dy):
    part = ref_or_value[SIDE[dx], SIDE[dy]]
    return part.reshape(-1, 8, 128)


def packed(rim):
    if rim.shape[0] == 1:
        return jnp.concatenate([rim[0], jnp.zeros((8, 128), F32)], axis=0)
    lane = lax.broadcasted_iota(jnp.int32, (8, 128), 1)
    halves = []
    for first in (0, 4):
        value = rim[first]
        for j in (1, 2, 3):
            value = jnp.where(lane < 32 * j, value, pltpu.roll(rim[first + j], 32 * j, 1))
        halves.append(value)
    return jnp.concatenate(halves, axis=0)


def unpacked(rows, count):
    pieces = []
    for i in range(count):
        value = rows[8 * (i // 4) : 8 * (i // 4) + 8]
        pieces.append(pltpu.roll(value, 128 - 32 * (i % 4), 1) if i % 4 else value)
    return jnp.stack(pieces)


def rows_of(index, stride, first, count):
    return pl.ds(pl.multiple_of(index * stride + first, 8), count)


def rims_kernel(send, mask, gathered, local, to_b, face_a):
    for brick in range(2):
        rows = gathered[:, brick].reshape(128, 512).astype(F32) * mask[brick : brick + 1, :]
        local[brick] = rows.T.reshape(8, 8, 8, 128)

    def chosen(move):
        s = send[MOVES.index(move)]
        first, second = (tiles(local[brick], *move) for brick in range(2))
        return jnp.where(s == 0, first, jnp.where(s == 1, second, 0.0))

    for i, b in enumerate((-1, 1)):
        parts = [chosen((0, b)), chosen((-1, b)), chosen((1, b))]
        to_b[i] = jnp.concatenate(parts, axis=0).reshape(80, 128).astype(BF)
    for i, a in enumerate((-1, 1)):
        face_a[i] = chosen((a, 0)).reshape(64, 128).astype(BF)


def block_tiles(near, local, arrived, dx, dy):
    z = lax.broadcasted_iota(jnp.int32, (1, 8, 128), 1)
    options = [tiles(local[0], dx, dy), tiles(local[1], dx, dy)]
    rows = [0, 1]
    if (dx, dy) != (0, 0):
        options.append(arrived)
        rows.append(2 + MOVES.index((dx, dy)))

    def pick(r):
        value = 0.0
        for row, option in zip(rows, options):
            value = jnp.where(r == row, option, value)
        return value

    shifted = [[], [], []]
    for brick in range(2):
        below, level, above = planar_slots(dx, dy)
        center = options[brick] if level is None else pick(near[brick, level])
        under, over = pick(near[brick, below]), pick(near[brick, above])
        shifted[0].append(pltpu.roll(jnp.where(z == 7, under, center), 1, 1))
        shifted[1].append(center)
        shifted[2].append(pltpu.roll(jnp.where(z == 0, over, center), 7, 1))
    return [jnp.stack(pair, axis=1).reshape(-1, 16, 128).astype(BF) for pair in shifted]


def selection(chan):
    row = lax.broadcasted_iota(jnp.int32, (384, 128), 0)
    column = lax.broadcasted_iota(jnp.int32, (384, 128), 1)
    wanted = (row >> 7 == column >> 5) & ((row & 127) == chan * 32 + (column & 31))
    return jnp.where(wanted, 1.0, 0.0).astype(BF)


def center_kernel(near, chan, local, from_bm, from_bp, extra, pre_out, own_out, blocks):
    for i in range(3):
        for plane in (0, 9):
            blocks[i, plane] = jnp.zeros((10, 16, 128), BF)
    for dy, part in ((-1, from_bm), (0, None), (1, from_bp)):
        arrived = None if part is None else part[0:64].astype(F32).reshape(8, 8, 128)
        for i, value in enumerate(block_tiles(near, local, arrived, 0, dy)):
            blocks[i, 1:9, RIM[dy]] = value.reshape(8, -1, 16, 128)

    def lefts(first, count):
        return jnp.concatenate(
            [
                blocks[dz, dx : dx + 8, first : first + count].reshape(128 * count, 128)
                for dx in range(3)
                for dz in range(3)
            ],
            axis=1,
        )

    def rights(dy):
        return jnp.concatenate(
            [
                extra[:, 9 * dx + 3 * dy + dz].reshape(128, 128)
                for dx in range(3)
                for dz in range(3)
            ],
            axis=0,
        )

    pair = jnp.concatenate([rights(0), rights(1)], axis=1)
    pair = jnp.dot(lefts(0, 9), pair, preferred_element_type=F32).reshape(8, 9, 16, 256)
    pre = jnp.dot(lefts(2, 8), rights(2), preferred_element_type=F32).reshape(8, 8, 16, 128)
    pre_out[...] = pre + pair[:, 0:8, :, 0:128] + pair[:, 1:9, :, 128:256]
    stacked = jnp.concatenate([blocks[dz, 1:9].reshape(1280, 128) for dz in range(3)], axis=1)
    own = jnp.dot(stacked, selection(chan[0]), preferred_element_type=F32).astype(BF)
    own_out[...] = own.reshape(8, 10, 16, 128)


def main_kernel(
    near, chan, place, mask, local, from_am, from_ap, center_pre, center_own, extra, own_weights,
    act_out, sent, own_out,
    rim, grads, own_block, act_all, terms, stage,
):
    z = lax.broadcasted_iota(jnp.int32, (1, 8, 128), 1)
    own_block[1:9] = center_own[...]
    edges = []
    for side, (dx, part) in enumerate(((-1, from_am), (1, from_ap))):
        corner = part[64:80].astype(F32).reshape(2, 8, 128)
        face = part[0:64].astype(F32).reshape(8, 8, 128)
        for dy, arrived in ((-1, corner[0:1]), (0, face), (1, corner[1:2])):
            for i, value in enumerate(block_tiles(near, local, arrived, dx, dy)):
                rim[side, i, RIM[dy]] = value
        left = jnp.concatenate(
            [rim[side, dz, dy : dy + 8].reshape(128, 128) for dy in range(3) for dz in range(3)],
            axis=1,
        )
        right = jnp.concatenate(
            [extra[:, 9 * (dx + 1) + o].reshape(128, 128) for o in range(9)], axis=0
        )
        edges.append(jnp.dot(left, right, preferred_element_type=F32).reshape(1, 8, 16, 128))
        stacked = jnp.concatenate([rim[side, dz].reshape(160, 128) for dz in range(3)], axis=1)
        own = jnp.dot(stacked, selection(chan[0]), preferred_element_type=F32).astype(BF)
        own_block[9 * side] = own.reshape(10, 16, 128)
    pre = center_pre[...]
    pre = jnp.concatenate([pre[0:1] + edges[0], pre[1:7], pre[7:8] + edges[1]], axis=0)
    pre = pre.reshape(64, 2, 8, 128)

    back = []
    for brick in range(2):
        on = mask[brick : brick + 1, :]
        pre_act = pre[:, brick].reshape(512, 128).T * on
        gate = jax.nn.sigmoid(pre_act)
        act_all[brick] = (pre_act * gate).astype(BF)
        cotangent = jnp.concatenate(
            [extra[:, 27 + 4 * brick + i].reshape(128, 128).astype(F32) for i in range(4)], axis=1
        )
        grad = cotangent * on * gate * (1.0 + pre_act * (1.0 - gate))
        back.append(grad.T.reshape(64, 8, 128))
    start = pl.multiple_of(chan[0] * 32, 32)
    for brick in range(2):
        act_out[brick] = act_all[brick, pl.ds(start, 32), :]
    back = jnp.stack(back, axis=1).reshape(1024, 128)
    grads[...] = jnp.zeros(grads.shape, BF)
    grads[2:10, 2:10] = back.astype(BF).reshape(8, 8, 16, 128)
    back_t = back.T.astype(BF)

    def put_part(tile, value):
        first = tile // 7 * SENT + tile % 7 * 8
        stage[first : first + 8] = value

    for first in range(0, 9, 2):
        windows = [
            own_block[dx + 1 : dx + 9, dy + 1 : dy + 9].reshape(1024, 128)
            for dx, dy in PLANAR[first : first + 2]
        ]
        product = jnp.dot(back_t, jnp.concatenate(windows, axis=1), preferred_element_type=F32)
        for i in range(len(windows)):
            turned = product[:, 128 * i : 128 * i + 128].T
            for tile in range(12):
                put_part(12 * (first + i) + tile, turned[8 * tile : 8 * tile + 8])
    for tile in range(108, 112):
        put_part(tile, jnp.zeros((8, 128), F32))
    for j in range(GROUP):
        stage[j * SENT + PART : (j + 1) * SENT] = jnp.zeros((16, 128), F32)

    def grad_lefts(first, count):
        return jnp.concatenate(
            [
                grads[1 - dx : 11 - dx, first : first + count].reshape(160 * count, 128)
                for dx in (-1, 0, 1)
            ],
            axis=1,
        )

    def grad_rights(dy):
        pieces = []
        for dx in (-1, 0, 1):
            first = (dx + 1) * 9 + (dy + 1) * 3
            piece = own_weights[first : first + 3].reshape(96, 128).astype(F32)
            piece = jnp.concatenate([piece, jnp.zeros((32, 128), F32)], axis=0)
            pieces.append(piece.T.astype(BF))
        return jnp.concatenate(pieces, axis=0)

    pair = jnp.concatenate([grad_rights(1), grad_rights(0)], axis=1)
    pair = jnp.dot(grad_lefts(0, 11), pair, preferred_element_type=F32).reshape(10, 11, 16, 256)
    spread = jnp.dot(grad_lefts(2, 10), grad_rights(-1), preferred_element_type=F32)
    spread = spread.reshape(10, 10, 16, 128)
    spread = spread + pair[:, 0:10, :, 0:128] + pair[:, 1:11, :, 128:256]
    spread = spread.reshape(100, 2, 8, 128)
    for brick in range(2):
        part = spread[:, brick]
        up = pltpu.roll(part, 7, 1)
        down = pltpu.roll(pltpu.roll(part, 64, 2), 1, 1)
        center = (
            pltpu.roll(part, 96, 2) + jnp.where(z < 7, up, 0.0) + jnp.where(z > 0, down, 0.0)
        )
        terms[0, brick] = jnp.where(z == 7, up, 0.0).reshape(10, 10, 8, 128)
        terms[1, brick] = center.reshape(10, 10, 8, 128)
        terms[2, brick] = jnp.where(z == 0, down, 0.0).reshape(10, 10, 8, 128)
    for brick in range(2):
        own_out[brick] = terms[1, brick, 1:9, 1:9]
    for dx, dy in PLANAR:
        pieces = [
            (near[brick, slot], terms[i, brick, RIM[dx], RIM[dy]])
            for brick in range(2)
            for i, slot in enumerate(planar_slots(dx, dy))
            if slot is not None
        ]

        def collected(target):
            total = 0.0
            for r, piece in pieces:
                total = total + jnp.where(r == target, piece, 0.0)
            return total

        for brick in range(2):
            own_out[brick, SIDE[dx], SIDE[dy]] += collected(brick)
        if (dx, dy) != (0, 0):
            rim = collected(2 + MOVES.index((dx, dy))).reshape(-1, 8, 128)
            target = lax.rem(place[0] + STEPS[dx, dy] + GROUP, GROUP)
            stage[rows_of(target, SENT, PART, 16)] = packed(rim)
    sent[...] = stage[...].astype(BF)


def middle_kernel(place, arrived, sent, held, stage):
    held[...] = arrived[...].astype(F32)
    total = held[0:PART]
    for j in range(1, GROUP):
        total = total + held[j * SENT : j * SENT + PART]
    planes = stage.shape[0] // ONWARD
    for j in range(planes):
        stage[j * ONWARD : j * ONWARD + PART] = total
        stage[j * ONWARD + PART : (j + 1) * ONWARD] = jnp.zeros((24, 128), F32)
    lane = lax.broadcasted_iota(jnp.int32, (8, 128), 1)
    for a in (-1, 1):
        rims = {
            b: held[rows_of(lax.rem(place[0] - STEPS[a, b] + GROUP, GROUP), SENT, PART, 16 if b == 0 else 8)]
            for b in (-1, 0, 1)
        }
        edges = jnp.where(lane < 32, rims[-1], pltpu.roll(rims[1], 32, 1))
        target = place[1] + a

        @pl.when((target >= 0) & (target < planes))
        def _():
            stage[rows_of(target, ONWARD, PART, 24)] = jnp.concatenate([rims[0], edges], axis=0)

    sent[...] = stage[...].astype(BF)


def sum_kernel(scale, arrived, sent):
    values = arrived[...].astype(F32)
    total = values[0:PART]
    for j in range(1, values.shape[0] // ONWARD):
        total = total + values[j * ONWARD : j * ONWARD + PART]
    sent[...] = jnp.concatenate([total * scale] * GROUP, axis=0).astype(BF)


def final_kernel(send, place, mask, own, direct, onward, out, total, held, passed):
    total[...] = own[...]
    held[...] = direct[...].astype(F32)
    passed[...] = onward[...].astype(F32)
    inner, outer = place[0], place[1]
    for dx, dy in MOVES:
        s = send[MOVES.index((dx, dy))]
        origin = inner - STEPS[dx, dy]
        size = 8 if dx and dy else 16
        rows = held[rows_of(lax.rem(origin + GROUP, GROUP), SENT, PART, size)]
        if dx:
            passer = jnp.clip(outer - dx, 0, passed.shape[0] // ONWARD - 1)
            other = passed[rows_of(passer, ONWARD, PART + 16 if dy else PART, size)]
            if dy == 1:
                other = pltpu.roll(other, 96, 1)
            rows = jnp.where((origin >= 0) & (origin < GROUP), rows, other)
        piece = unpacked(rows, 1 if dx and dy else 8)
        nx = 8 if dx == 0 else 1
        piece = piece.reshape(nx, piece.shape[0] // nx, 8, 128)
        for brick in range(2):
            total[brick, SIDE[dx], SIDE[dy]] += jnp.where(s == brick, piece, 0.0)
    for brick in range(2):
        rows = total[brick].reshape(512, 128).T[0:32] * mask[brick : brick + 1, :]
        out[brick] = rows.astype(BF)


SMEM = pl.BlockSpec(memory_space=pltpu.SMEM)
VMEM = pl.BlockSpec(memory_space=pltpu.VMEM)


def call(kernel, name, smem, vmem, outs, scratch, limit, cost=None):
    shapes = [jax.ShapeDtypeStruct(s, d) for s, d in outs]
    return pl.pallas_call(
        kernel,
        out_shape=shapes,
        in_specs=[SMEM] * len(smem) + [VMEM] * len(vmem),
        out_specs=[VMEM] * len(outs),
        scratch_shapes=[pltpu.VMEM(s, d) for s, d in scratch],
        compiler_params=pltpu.CompilerParams(vmem_limit_bytes=limit << 20),
        cost_estimate=cost,
        name=name,
    )(*smem, *vmem)


def passed_along(shard, by):
    count = lax.axis_size("space")
    pairs = [(i, i + by) for i in range(count) if 0 <= i + by < count]
    if abs(by) == 1:
        pairs = [(i, j) for i, j in pairs if i // 4 == j // 4]
    return lax.ppermute(shard, "space", pairs)


def unpack_mask(packed):
    shifts = jnp.arange(32, dtype=jnp.int32)
    bits = lax.shift_right_logical(packed[:, :, None], shifts[None, None, :]) & 1
    return bits.reshape(packed.shape[0], packed.shape[1] * 32).astype(F32)


def exchanged(values, far):
    count = lax.axis_size("space")
    planes = count // GROUP
    groups = [[j * GROUP + i for i in range(GROUP)] for j in range(planes)]
    if far:
        groups = [list(members) for members in zip(*groups)]
    return lax.all_to_all(values, "space", 0, 0, tiled=True, axis_index_groups=groups)


def from_all_chan(part):
    count = lax.axis_size("chan")
    copies = jnp.broadcast_to(part[None], (count,) + part.shape)
    return lax.all_to_all(copies, "chan", 0, 0, tiled=True)


def on_device(features, mask_packed, neighbours, send_list, weights, cotangent):
    chan = lax.axis_index("chan").astype(jnp.int32).reshape(1)
    send = send_list.reshape(8)
    where = lax.axis_index("space").astype(jnp.int32)
    place = jnp.stack([where % GROUP, where // GROUP])
    planes = lax.axis_size("space") // GROUP
    mask = unpack_mask(mask_packed)
    gathered = from_all_chan(features.transpose(1, 0, 2))
    by_lanes = cotangent.reshape(32, 8, 128).transpose(1, 0, 2)
    extra = jnp.concatenate([weights, by_lanes], axis=0)
    extra = from_all_chan(extra)
    local, to_b, face_a = call(
        rims_kernel, "rims", [send], [mask, gathered],
        [((2, 8, 8, 8, 128), F32), ((2, 80, 128), BF), ((2, 64, 128), BF)], [], 16,
    )
    from_bm, from_bp = passed_along(to_b[0], 1), passed_along(to_b[1], -1)
    to_am = jnp.concatenate([face_a[0], from_bm[64:72], from_bp[64:72]], axis=0)
    to_ap = jnp.concatenate([face_a[1], from_bm[72:80], from_bp[72:80]], axis=0)
    from_am, from_ap = passed_along(to_am, 4), passed_along(to_ap, -4)
    center_pre, center_own = call(
        center_kernel, "center", [neighbours, chan], [local, from_bm, from_bp, extra],
        [((8, 8, 16, 128), F32), ((8, 10, 16, 128), BF)], [((3, 10, 10, 16, 128), BF)], 24,
        pl.CostEstimate(flops=1 << 30, bytes_accessed=3 << 20, transcendentals=0),
    )
    act, sent, own = call(
        main_kernel, "conv", [neighbours, chan, place],
        [mask, local, from_am, from_ap, center_pre, center_own, extra, weights],
        [
            ((2, 32, 512), BF), ((GROUP * SENT, 128), BF), ((2, 8, 8, 8, 128), F32),
        ],
        [
            ((2, 3, 10, 16, 128), BF), ((12, 12, 16, 128), BF), ((10, 10, 16, 128), BF),
            ((2, 128, 512), BF), ((3, 2, 10, 10, 8, 128), F32), ((GROUP * SENT, 128), F32),
        ],
        32,
    )
    scale = 1.0 / math.sqrt(2 * lax.axis_size("space") * 512)
    direct = exchanged(sent, False)
    (sent,) = call(
        middle_kernel, "middle", [place], [direct], [((planes * ONWARD, 128), BF)],
        [((GROUP * SENT, 128), F32), ((planes * ONWARD, 128), F32)], 16,
    )
    onward = exchanged(sent, True)
    (sent,) = call(
        functools.partial(sum_kernel, scale), "sums", [], [onward], [((GROUP * PART, 128), BF)], [], 16
    )
    summed = exchanged(sent, False)
    grad_weights = summed[:864].astype(F32).reshape(27, 32, 128)
    (grad,) = call(
        final_kernel, "grad", [send, place], [mask, own, direct, onward],
        [((2, 32, 512), BF)],
        [((2, 8, 8, 8, 128), F32), ((GROUP * SENT, 128), F32), ((planes * ONWARD, 128), F32)], 16,
    )
    return act.transpose(1, 0, 2), grad.transpose(1, 0, 2), grad_weights


def solution(mesh):
    return jax.shard_map(
        on_device,
        mesh=mesh,
        in_specs=(
            P("chan", "space", None),
            P("space", None),
            P("space", None),
            P("space", None, None),
            P(None, "chan", None),
            P("chan", "space", None),
        ),
        out_specs=(P("chan", "space", None), P("chan", "space", None), P(None, "chan", None)),
        check_vma=False,
    )
```

```python
import functools
import math

import jax
import jax.numpy as jnp
from jax import lax
from jax.experimental import pallas as pl
from jax.experimental.pallas import tpu as pltpu
from jax.sharding import PartitionSpec as P

BF = jnp.bfloat16
F32 = jnp.float32
SIDE = {-1: slice(7, 8), 0: slice(0, 8), 1: slice(0, 1)}
RIM = {-1: slice(0, 1), 0: slice(1, 9), 1: slice(9, 10)}
PLANAR = [(a, b) for a in (-1, 0, 1) for b in (-1, 0, 1)]
MOVES = [m for m in PLANAR if m != (0, 0)]
STEPS = {(a, b): 4 * a + b for a, b in MOVES}
GROUP = 16
PART = 56
SENT = PART + 16
ONWARD = PART + 24


def slot_of(dx, dy, dz):
    linear = (dx + 1) * 9 + (dy + 1) * 3 + dz + 1
    return linear if linear < 13 else linear - 1


def planar_slots(dx, dy):
    return [None if (dx, dy, dz) == (0, 0, 0) else slot_of(dx, dy, dz) for dz in (-1, 0, 1)]


def tiles(ref_or_value, dx, dy):
    part = ref_or_value[SIDE[dx], SIDE[dy]]
    return part.reshape(-1, 8, 128)


def packed(rim):
    if rim.shape[0] == 1:
        return jnp.concatenate([rim[0], jnp.zeros((8, 128), F32)], axis=0)
    lane = lax.broadcasted_iota(jnp.int32, (8, 128), 1)
    halves = []
    for first in (0, 4):
        value = rim[first]
        for j in (1, 2, 3):
            value = jnp.where(lane < 32 * j, value, pltpu.roll(rim[first + j], 32 * j, 1))
        halves.append(value)
    return jnp.concatenate(halves, axis=0)


def unpacked(rows, count):
    pieces = []
    for i in range(count):
        value = rows[8 * (i // 4) : 8 * (i // 4) + 8]
        pieces.append(pltpu.roll(value, 128 - 32 * (i % 4), 1) if i % 4 else value)
    return jnp.stack(pieces)


def rows_of(index, stride, first, count):
    return pl.ds(pl.multiple_of(index * stride + first, 8), count)


def copies_kernel(weights, by_lanes, out):
    for i in range(out.shape[0]):
        out[i, 0:27] = weights[...]
        out[i, 27:35] = by_lanes[...]


def rims_kernel(send, mask, gathered, local, to_b, face_a):
    for brick in range(2):
        rows = gathered[:, brick].reshape(128, 512).astype(F32) * mask[brick : brick + 1, :]
        local[brick] = rows.T.reshape(8, 8, 8, 128)

    def chosen(move):
        s = send[MOVES.index(move)]
        first, second = (tiles(local[brick], *move) for brick in range(2))
        return jnp.where(s == 0, first, jnp.where(s == 1, second, 0.0))

    for i, b in enumerate((-1, 1)):
        parts = [chosen((0, b)), chosen((-1, b)), chosen((1, b))]
        to_b[i] = jnp.concatenate(parts, axis=0).reshape(80, 128).astype(BF)
    for i, a in enumerate((-1, 1)):
        face_a[i] = chosen((a, 0)).reshape(64, 128).astype(BF)


def block_tiles(near, local, arrived, dx, dy):
    z = lax.broadcasted_iota(jnp.int32, (1, 8, 128), 1)
    options = [tiles(local[0], dx, dy), tiles(local[1], dx, dy)]
    rows = [0, 1]
    if (dx, dy) != (0, 0):
        options.append(arrived)
        rows.append(2 + MOVES.index((dx, dy)))

    def pick(r):
        value = 0.0
        for row, option in zip(rows, options):
            value = jnp.where(r == row, option, value)
        return value

    shifted = [[], [], []]
    for brick in range(2):
        below, level, above = planar_slots(dx, dy)
        center = options[brick] if level is None else pick(near[brick, level])
        under, over = pick(near[brick, below]), pick(near[brick, above])
        shifted[0].append(pltpu.roll(jnp.where(z == 7, under, center), 1, 1))
        shifted[1].append(center)
        shifted[2].append(pltpu.roll(jnp.where(z == 0, over, center), 7, 1))
    return [jnp.stack(pair, axis=1).reshape(-1, 16, 128).astype(BF) for pair in shifted]


def selection(chan):
    row = lax.broadcasted_iota(jnp.int32, (384, 128), 0)
    column = lax.broadcasted_iota(jnp.int32, (384, 128), 1)
    wanted = (row >> 7 == column >> 5) & ((row & 127) == chan * 32 + (column & 31))
    return jnp.where(wanted, 1.0, 0.0).astype(BF)


def center_kernel(near, chan, local, from_bm, from_bp, extra, pre_out, own_out, blocks):
    for i in range(3):
        for plane in (0, 9):
            blocks[i, plane] = jnp.zeros((10, 16, 128), BF)
    for dy, part in ((-1, from_bm), (0, None), (1, from_bp)):
        arrived = None if part is None else part[0:64].astype(F32).reshape(8, 8, 128)
        for i, value in enumerate(block_tiles(near, local, arrived, 0, dy)):
            blocks[i, 1:9, RIM[dy]] = value.reshape(8, -1, 16, 128)

    def lefts(first, count):
        return jnp.concatenate(
            [
                blocks[dz, dx : dx + 8, first : first + count].reshape(128 * count, 128)
                for dx in range(3)
                for dz in range(3)
            ],
            axis=1,
        )

    def rights(dy):
        return jnp.concatenate(
            [
                extra[:, 9 * dx + 3 * dy + dz].reshape(128, 128)
                for dx in range(3)
                for dz in range(3)
            ],
            axis=0,
        )

    pair = jnp.concatenate([rights(0), rights(1)], axis=1)
    pair = jnp.dot(lefts(0, 9), pair, preferred_element_type=F32).reshape(8, 9, 16, 256)
    pre = jnp.dot(lefts(2, 8), rights(2), preferred_element_type=F32).reshape(8, 8, 16, 128)
    pre_out[...] = pre + pair[:, 0:8, :, 0:128] + pair[:, 1:9, :, 128:256]
    stacked = jnp.concatenate([blocks[dz, 1:9].reshape(1280, 128) for dz in range(3)], axis=1)
    own = jnp.dot(stacked, selection(chan[0]), preferred_element_type=F32).astype(BF)
    own_out[...] = own.reshape(8, 10, 16, 128)


def main_kernel(
    near, chan, place, mask, local, from_am, from_ap, center_pre, center_own, extra, own_weights,
    act_out, sent, own_out,
    rim, grads, own_block, act_all, terms, stage,
):
    z = lax.broadcasted_iota(jnp.int32, (1, 8, 128), 1)
    own_block[1:9] = center_own[...]
    edges = []
    for side, (dx, part) in enumerate(((-1, from_am), (1, from_ap))):
        corner = part[64:80].astype(F32).reshape(2, 8, 128)
        face = part[0:64].astype(F32).reshape(8, 8, 128)
        for dy, arrived in ((-1, corner[0:1]), (0, face), (1, corner[1:2])):
            for i, value in enumerate(block_tiles(near, local, arrived, dx, dy)):
                rim[side, i, RIM[dy]] = value
        left = jnp.concatenate(
            [rim[side, dz, dy : dy + 8].reshape(128, 128) for dy in range(3) for dz in range(3)],
            axis=1,
        )
        right = jnp.concatenate(
            [extra[:, 9 * (dx + 1) + o].reshape(128, 128) for o in range(9)], axis=0
        )
        edges.append(jnp.dot(left, right, preferred_element_type=F32).reshape(1, 8, 16, 128))
        stacked = jnp.concatenate([rim[side, dz].reshape(160, 128) for dz in range(3)], axis=1)
        own = jnp.dot(stacked, selection(chan[0]), preferred_element_type=F32).astype(BF)
        own_block[9 * side] = own.reshape(10, 16, 128)
    pre = center_pre[...]
    pre = jnp.concatenate([pre[0:1] + edges[0], pre[1:7], pre[7:8] + edges[1]], axis=0)
    pre = pre.reshape(64, 2, 8, 128)

    back = []
    for brick in range(2):
        on = mask[brick : brick + 1, :]
        pre_act = pre[:, brick].reshape(512, 128).T * on
        gate = jax.nn.sigmoid(pre_act)
        act_all[brick] = (pre_act * gate).astype(BF)
        cotangent = jnp.concatenate(
            [extra[:, 27 + 4 * brick + i].reshape(128, 128).astype(F32) for i in range(4)], axis=1
        )
        grad = cotangent * on * gate * (1.0 + pre_act * (1.0 - gate))
        back.append(grad.T.reshape(64, 8, 128))
    start = pl.multiple_of(chan[0] * 32, 32)
    for brick in range(2):
        act_out[brick] = act_all[brick, pl.ds(start, 32), :]
    back = jnp.stack(back, axis=1).reshape(1024, 128)
    grads[...] = jnp.zeros(grads.shape, BF)
    grads[2:10, 2:10] = back.astype(BF).reshape(8, 8, 16, 128)
    back_t = back.T.astype(BF)

    def put_part(tile, value):
        first = tile // 7 * SENT + tile % 7 * 8
        stage[first : first + 8] = value

    for first in range(0, 9, 2):
        windows = [
            own_block[dx + 1 : dx + 9, dy + 1 : dy + 9].reshape(1024, 128)
            for dx, dy in PLANAR[first : first + 2]
        ]
        product = jnp.dot(back_t, jnp.concatenate(windows, axis=1), preferred_element_type=F32)
        for i in range(len(windows)):
            turned = product[:, 128 * i : 128 * i + 128].T
            for tile in range(12):
                put_part(12 * (first + i) + tile, turned[8 * tile : 8 * tile + 8])
    for tile in range(108, 112):
        put_part(tile, jnp.zeros((8, 128), F32))
    for j in range(GROUP):
        stage[j * SENT + PART : (j + 1) * SENT] = jnp.zeros((16, 128), F32)

    def grad_lefts(first, count):
        return jnp.concatenate(
            [
                grads[1 - dx : 11 - dx, first : first + count].reshape(160 * count, 128)
                for dx in (-1, 0, 1)
            ],
            axis=1,
        )

    def grad_rights(dy):
        pieces = []
        for dx in (-1, 0, 1):
            first = (dx + 1) * 9 + (dy + 1) * 3
            piece = own_weights[first : first + 3].reshape(96, 128).astype(F32)
            piece = jnp.concatenate([piece, jnp.zeros((32, 128), F32)], axis=0)
            pieces.append(piece.T.astype(BF))
        return jnp.concatenate(pieces, axis=0)

    pair = jnp.concatenate([grad_rights(1), grad_rights(0)], axis=1)
    pair = jnp.dot(grad_lefts(0, 11), pair, preferred_element_type=F32).reshape(10, 11, 16, 256)
    spread = jnp.dot(grad_lefts(2, 10), grad_rights(-1), preferred_element_type=F32)
    spread = spread.reshape(10, 10, 16, 128)
    spread = spread + pair[:, 0:10, :, 0:128] + pair[:, 1:11, :, 128:256]
    spread = spread.reshape(100, 2, 8, 128)
    for brick in range(2):
        part = spread[:, brick]
        up = pltpu.roll(part, 7, 1)
        down = pltpu.roll(pltpu.roll(part, 64, 2), 1, 1)
        center = (
            pltpu.roll(part, 96, 2) + jnp.where(z < 7, up, 0.0) + jnp.where(z > 0, down, 0.0)
        )
        terms[0, brick] = jnp.where(z == 7, up, 0.0).reshape(10, 10, 8, 128)
        terms[1, brick] = center.reshape(10, 10, 8, 128)
        terms[2, brick] = jnp.where(z == 0, down, 0.0).reshape(10, 10, 8, 128)
    for brick in range(2):
        own_out[brick] = terms[1, brick, 1:9, 1:9]
    for dx, dy in PLANAR:
        pieces = [
            (near[brick, slot], terms[i, brick, RIM[dx], RIM[dy]])
            for brick in range(2)
            for i, slot in enumerate(planar_slots(dx, dy))
            if slot is not None
        ]

        def collected(target):
            total = 0.0
            for r, piece in pieces:
                total = total + jnp.where(r == target, piece, 0.0)
            return total

        for brick in range(2):
            own_out[brick, SIDE[dx], SIDE[dy]] += collected(brick)
        if (dx, dy) != (0, 0):
            rim = collected(2 + MOVES.index((dx, dy))).reshape(-1, 8, 128)
            target = lax.rem(place[0] + STEPS[dx, dy] + GROUP, GROUP)
            stage[rows_of(target, SENT, PART, 16)] = packed(rim)
    sent[...] = stage[...].astype(BF)


def middle_kernel(place, arrived, sent, held, stage):
    held[...] = arrived[...].astype(F32)
    total = held[0:PART]
    for j in range(1, GROUP):
        total = total + held[j * SENT : j * SENT + PART]
    planes = stage.shape[0] // ONWARD
    for j in range(planes):
        stage[j * ONWARD : j * ONWARD + PART] = total
        stage[j * ONWARD + PART : (j + 1) * ONWARD] = jnp.zeros((24, 128), F32)
    lane = lax.broadcasted_iota(jnp.int32, (8, 128), 1)
    for a in (-1, 1):
        rims = {
            b: held[rows_of(lax.rem(place[0] - STEPS[a, b] + GROUP, GROUP), SENT, PART, 16 if b == 0 else 8)]
            for b in (-1, 0, 1)
        }
        edges = jnp.where(lane < 32, rims[-1], pltpu.roll(rims[1], 32, 1))
        target = place[1] + a

        @pl.when((target >= 0) & (target < planes))
        def _():
            stage[rows_of(target, ONWARD, PART, 24)] = jnp.concatenate([rims[0], edges], axis=0)

    sent[...] = stage[...].astype(BF)


def sum_kernel(scale, arrived, sent):
    values = arrived[...].astype(F32)
    total = values[0:PART]
    for j in range(1, values.shape[0] // ONWARD):
        total = total + values[j * ONWARD : j * ONWARD + PART]
    sent[...] = jnp.concatenate([total * scale] * GROUP, axis=0).astype(BF)


def final_kernel(send, place, mask, own, direct, onward, out, total, held, passed):
    total[...] = own[...]
    held[...] = direct[...].astype(F32)
    passed[...] = onward[...].astype(F32)
    inner, outer = place[0], place[1]
    for dx, dy in MOVES:
        s = send[MOVES.index((dx, dy))]
        origin = inner - STEPS[dx, dy]
        size = 8 if dx and dy else 16
        rows = held[rows_of(lax.rem(origin + GROUP, GROUP), SENT, PART, size)]
        if dx:
            passer = jnp.clip(outer - dx, 0, passed.shape[0] // ONWARD - 1)
            other = passed[rows_of(passer, ONWARD, PART + 16 if dy else PART, size)]
            if dy == 1:
                other = pltpu.roll(other, 96, 1)
            rows = jnp.where((origin >= 0) & (origin < GROUP), rows, other)
        piece = unpacked(rows, 1 if dx and dy else 8)
        nx = 8 if dx == 0 else 1
        piece = piece.reshape(nx, piece.shape[0] // nx, 8, 128)
        for brick in range(2):
            total[brick, SIDE[dx], SIDE[dy]] += jnp.where(s == brick, piece, 0.0)
    for brick in range(2):
        rows = total[brick].reshape(512, 128).T[0:32] * mask[brick : brick + 1, :]
        out[brick] = rows.astype(BF)


SMEM = pl.BlockSpec(memory_space=pltpu.SMEM)
VMEM = pl.BlockSpec(memory_space=pltpu.VMEM)


def call(kernel, name, smem, vmem, outs, scratch, limit, cost=None):
    shapes = [jax.ShapeDtypeStruct(s, d) for s, d in outs]
    return pl.pallas_call(
        kernel,
        out_shape=shapes,
        in_specs=[SMEM] * len(smem) + [VMEM] * len(vmem),
        out_specs=[VMEM] * len(outs),
        scratch_shapes=[pltpu.VMEM(s, d) for s, d in scratch],
        compiler_params=pltpu.CompilerParams(vmem_limit_bytes=limit << 20),
        cost_estimate=cost,
        name=name,
    )(*smem, *vmem)


def passed_along(shard, by):
    count = lax.axis_size("space")
    pairs = [(i, i + by) for i in range(count) if 0 <= i + by < count]
    if abs(by) == 1:
        pairs = [(i, j) for i, j in pairs if i // 4 == j // 4]
    return lax.ppermute(shard, "space", pairs)


def unpack_mask(packed):
    shifts = jnp.arange(32, dtype=jnp.int32)
    bits = lax.shift_right_logical(packed[:, :, None], shifts[None, None, :]) & 1
    return bits.reshape(packed.shape[0], packed.shape[1] * 32).astype(F32)


def exchanged(values, far):
    count = lax.axis_size("space")
    planes = count // GROUP
    groups = [[j * GROUP + i for i in range(GROUP)] for j in range(planes)]
    if far:
        groups = [list(members) for members in zip(*groups)]
    return lax.all_to_all(values, "space", 0, 0, tiled=True, axis_index_groups=groups)


def from_all_chan(part):
    count = lax.axis_size("chan")
    copies = jnp.broadcast_to(part[None], (count,) + part.shape)
    return lax.all_to_all(copies, "chan", 0, 0, tiled=True)


def on_device(features, mask_packed, neighbours, send_list, weights, cotangent):
    chan = lax.axis_index("chan").astype(jnp.int32).reshape(1)
    send = send_list.reshape(8)
    where = lax.axis_index("space").astype(jnp.int32)
    place = jnp.stack([where % GROUP, where // GROUP])
    planes = lax.axis_size("space") // GROUP
    mask = unpack_mask(mask_packed)
    gathered = from_all_chan(features.transpose(1, 0, 2))
    by_lanes = cotangent.reshape(32, 8, 128).transpose(1, 0, 2)
    (extra,) = call(
        copies_kernel, "copies", [], [weights, by_lanes], [((4, 35, 32, 128), BF)], [], 16,
        pl.CostEstimate(flops=0, bytes_accessed=8 << 20, transcendentals=0),
    )
    extra = lax.all_to_all(extra, "chan", 0, 0, tiled=True)
    local, to_b, face_a = call(
        rims_kernel, "rims", [send], [mask, gathered],
        [((2, 8, 8, 8, 128), F32), ((2, 80, 128), BF), ((2, 64, 128), BF)], [], 16,
    )
    from_bm, from_bp = passed_along(to_b[0], 1), passed_along(to_b[1], -1)
    to_am = jnp.concatenate([face_a[0], from_bm[64:72], from_bp[64:72]], axis=0)
    to_ap = jnp.concatenate([face_a[1], from_bm[72:80], from_bp[72:80]], axis=0)
    from_am, from_ap = passed_along(to_am, 4), passed_along(to_ap, -4)
    center_pre, center_own = call(
        center_kernel, "center", [neighbours, chan], [local, from_bm, from_bp, extra],
        [((8, 8, 16, 128), F32), ((8, 10, 16, 128), BF)], [((3, 10, 10, 16, 128), BF)], 24,
        pl.CostEstimate(flops=1 << 30, bytes_accessed=3 << 20, transcendentals=0),
    )
    act, sent, own = call(
        main_kernel, "conv", [neighbours, chan, place],
        [mask, local, from_am, from_ap, center_pre, center_own, extra, weights],
        [
            ((2, 32, 512), BF), ((GROUP * SENT, 128), BF), ((2, 8, 8, 8, 128), F32),
        ],
        [
            ((2, 3, 10, 16, 128), BF), ((12, 12, 16, 128), BF), ((10, 10, 16, 128), BF),
            ((2, 128, 512), BF), ((3, 2, 10, 10, 8, 128), F32), ((GROUP * SENT, 128), F32),
        ],
        32,
    )
    scale = 1.0 / math.sqrt(2 * lax.axis_size("space") * 512)
    direct = exchanged(sent, False)
    (sent,) = call(
        middle_kernel, "middle", [place], [direct], [((planes * ONWARD, 128), BF)],
        [((GROUP * SENT, 128), F32), ((planes * ONWARD, 128), F32)], 16,
    )
    onward = exchanged(sent, True)
    (sent,) = call(
        functools.partial(sum_kernel, scale), "sums", [], [onward], [((GROUP * PART, 128), BF)], [], 16
    )
    summed = exchanged(sent, False)
    grad_weights = summed[:864].astype(F32).reshape(27, 32, 128)
    (grad,) = call(
        final_kernel, "grad", [send, place], [mask, own, direct, onward],
        [((2, 32, 512), BF)],
        [((2, 8, 8, 8, 128), F32), ((GROUP * SENT, 128), F32), ((planes * ONWARD, 128), F32)], 16,
    )
    return act.transpose(1, 0, 2), grad.transpose(1, 0, 2), grad_weights


def solution(mesh):
    return jax.shard_map(
        on_device,
        mesh=mesh,
        in_specs=(
            P("chan", "space", None),
            P("space", None),
            P("space", None),
            P("space", None, None),
            P(None, "chan", None),
            P("chan", "space", None),
        ),
        out_specs=(P("chan", "space", None), P("chan", "space", None), P(None, "chan", None)),
        check_vma=False,
    )
```

```python
import functools
import math

import jax
import jax.numpy as jnp
from jax import lax
from jax.experimental import pallas as pl
from jax.experimental.pallas import tpu as pltpu
from jax.sharding import PartitionSpec as P

BF = jnp.bfloat16
F32 = jnp.float32
SIDE = {-1: slice(7, 8), 0: slice(0, 8), 1: slice(0, 1)}
RIM = {-1: slice(0, 1), 0: slice(1, 9), 1: slice(9, 10)}
PLANAR = [(a, b) for a in (-1, 0, 1) for b in (-1, 0, 1)]
MOVES = [m for m in PLANAR if m != (0, 0)]
STEPS = {(a, b): 4 * a + b for a, b in MOVES}
GROUP = 16
PART = 56
SENT = PART + 16
ONWARD = PART + 24


def slot_of(dx, dy, dz):
    linear = (dx + 1) * 9 + (dy + 1) * 3 + dz + 1
    return linear if linear < 13 else linear - 1


def planar_slots(dx, dy):
    return [None if (dx, dy, dz) == (0, 0, 0) else slot_of(dx, dy, dz) for dz in (-1, 0, 1)]


def tiles(ref_or_value, dx, dy):
    part = ref_or_value[SIDE[dx], SIDE[dy]]
    return part.reshape(-1, 8, 128)


def packed(rim):
    if rim.shape[0] == 1:
        return jnp.concatenate([rim[0], jnp.zeros((8, 128), F32)], axis=0)
    lane = lax.broadcasted_iota(jnp.int32, (8, 128), 1)
    halves = []
    for first in (0, 4):
        value = rim[first]
        for j in (1, 2, 3):
            value = jnp.where(lane < 32 * j, value, pltpu.roll(rim[first + j], 32 * j, 1))
        halves.append(value)
    return jnp.concatenate(halves, axis=0)


def unpacked(rows, count):
    pieces = []
    for i in range(count):
        value = rows[8 * (i // 4) : 8 * (i // 4) + 8]
        pieces.append(pltpu.roll(value, 128 - 32 * (i % 4), 1) if i % 4 else value)
    return jnp.stack(pieces)


def rows_of(index, stride, first, count):
    return pl.ds(pl.multiple_of(index * stride + first, 8), count)


def copies_kernel(weights, by_lanes, out):
    for i in range(out.shape[0]):
        out[i, 0:27] = weights[...]
        out[i, 27:35] = by_lanes[...]


def rims_kernel(send, mask, gathered, local, to_b, face_a):
    both = gathered[...].reshape(128, 2, 512).astype(F32)
    for brick in range(2):
        rows = both[:, brick] * mask[brick : brick + 1, :]
        local[brick] = rows.T.reshape(8, 8, 8, 128)

    def chosen(move):
        s = send[MOVES.index(move)]
        first, second = (tiles(local[brick], *move) for brick in range(2))
        return jnp.where(s == 0, first, jnp.where(s == 1, second, 0.0))

    for i, b in enumerate((-1, 1)):
        parts = [chosen((0, b)), chosen((-1, b)), chosen((1, b))]
        to_b[i] = jnp.concatenate(parts, axis=0).reshape(80, 128).astype(BF)
    for i, a in enumerate((-1, 1)):
        face_a[i] = chosen((a, 0)).reshape(64, 128).astype(BF)


def block_tiles(near, local, arrived, dx, dy):
    z = lax.broadcasted_iota(jnp.int32, (1, 8, 128), 1)
    options = [tiles(local[0], dx, dy), tiles(local[1], dx, dy)]
    rows = [0, 1]
    if (dx, dy) != (0, 0):
        options.append(arrived)
        rows.append(2 + MOVES.index((dx, dy)))

    def pick(r):
        value = 0.0
        for row, option in zip(rows, options):
            value = jnp.where(r == row, option, value)
        return value

    shifted = [[], [], []]
    for brick in range(2):
        below, level, above = planar_slots(dx, dy)
        center = options[brick] if level is None else pick(near[brick, level])
        under, over = pick(near[brick, below]), pick(near[brick, above])
        shifted[0].append(pltpu.roll(jnp.where(z == 7, under, center), 1, 1))
        shifted[1].append(center)
        shifted[2].append(pltpu.roll(jnp.where(z == 0, over, center), 7, 1))
    return [jnp.stack(pair, axis=1).reshape(-1, 16, 128).astype(BF) for pair in shifted]


def selection(chan):
    row = lax.broadcasted_iota(jnp.int32, (384, 128), 0)
    column = lax.broadcasted_iota(jnp.int32, (384, 128), 1)
    wanted = (row >> 7 == column >> 5) & ((row & 127) == chan * 32 + (column & 31))
    return jnp.where(wanted, 1.0, 0.0).astype(BF)


def center_kernel(near, chan, local, from_bm, from_bp, extra, pre_out, own_out, blocks):
    for i in range(3):
        for plane in (0, 9):
            blocks[i, plane] = jnp.zeros((10, 16, 128), BF)
    for dy, part in ((-1, from_bm), (0, None), (1, from_bp)):
        arrived = None if part is None else part[0:64].astype(F32).reshape(8, 8, 128)
        for i, value in enumerate(block_tiles(near, local, arrived, 0, dy)):
            blocks[i, 1:9, RIM[dy]] = value.reshape(8, -1, 16, 128)

    def lefts(first, count):
        return jnp.concatenate(
            [
                blocks[dz, dx : dx + 8, first : first + count].reshape(128 * count, 128)
                for dx in range(3)
                for dz in range(3)
            ],
            axis=1,
        )

    def rights(dy):
        return jnp.concatenate(
            [
                extra[:, 9 * dx + 3 * dy + dz].reshape(128, 128)
                for dx in range(3)
                for dz in range(3)
            ],
            axis=0,
        )

    pair = jnp.concatenate([rights(0), rights(1)], axis=1)
    pair = jnp.dot(lefts(0, 9), pair, preferred_element_type=F32).reshape(8, 9, 16, 256)
    pre = jnp.dot(lefts(2, 8), rights(2), preferred_element_type=F32).reshape(8, 8, 16, 128)
    pre_out[...] = pre + pair[:, 0:8, :, 0:128] + pair[:, 1:9, :, 128:256]
    stacked = jnp.concatenate([blocks[dz, 1:9].reshape(1280, 128) for dz in range(3)], axis=1)
    own = jnp.dot(stacked, selection(chan[0]), preferred_element_type=F32).astype(BF)
    own_out[...] = own.reshape(8, 10, 16, 128)


def main_kernel(
    near, chan, place, mask, local, from_am, from_ap, center_pre, center_own, extra, own_weights,
    act_out, sent, own_out,
    rim, grads, own_block, act_all, terms, stage,
):
    z = lax.broadcasted_iota(jnp.int32, (1, 8, 128), 1)
    own_block[1:9] = center_own[...]
    edges = []
    for side, (dx, part) in enumerate(((-1, from_am), (1, from_ap))):
        corner = part[64:80].astype(F32).reshape(2, 8, 128)
        face = part[0:64].astype(F32).reshape(8, 8, 128)
        for dy, arrived in ((-1, corner[0:1]), (0, face), (1, corner[1:2])):
            for i, value in enumerate(block_tiles(near, local, arrived, dx, dy)):
                rim[side, i, RIM[dy]] = value
        left = jnp.concatenate(
            [rim[side, dz, dy : dy + 8].reshape(128, 128) for dy in range(3) for dz in range(3)],
            axis=1,
        )
        right = jnp.concatenate(
            [extra[:, 9 * (dx + 1) + o].reshape(128, 128) for o in range(9)], axis=0
        )
        edges.append(jnp.dot(left, right, preferred_element_type=F32).reshape(1, 8, 16, 128))
        stacked = jnp.concatenate([rim[side, dz].reshape(160, 128) for dz in range(3)], axis=1)
        own = jnp.dot(stacked, selection(chan[0]), preferred_element_type=F32).astype(BF)
        own_block[9 * side] = own.reshape(10, 16, 128)
    pre = center_pre[...]
    pre = jnp.concatenate([pre[0:1] + edges[0], pre[1:7], pre[7:8] + edges[1]], axis=0)
    pre = pre.reshape(64, 2, 8, 128)

    back = []
    for brick in range(2):
        on = mask[brick : brick + 1, :]
        pre_act = pre[:, brick].reshape(512, 128).T * on
        gate = jax.nn.sigmoid(pre_act)
        act_all[brick] = (pre_act * gate).astype(BF)
        cotangent = jnp.concatenate(
            [extra[:, 27 + 4 * brick + i].reshape(128, 128).astype(F32) for i in range(4)], axis=1
        )
        grad = cotangent * on * gate * (1.0 + pre_act * (1.0 - gate))
        back.append(grad.T.reshape(64, 8, 128))
    start = pl.multiple_of(chan[0] * 32, 32)
    for brick in range(2):
        act_out[brick] = act_all[brick, pl.ds(start, 32), :]
    back = jnp.stack(back, axis=1).reshape(1024, 128)
    grads[...] = jnp.zeros(grads.shape, BF)
    grads[2:10, 2:10] = back.astype(BF).reshape(8, 8, 16, 128)
    back_t = back.T.astype(BF)

    def put_part(tile, value):
        first = tile // 7 * SENT + tile % 7 * 8
        stage[first : first + 8] = value

    for first in range(0, 9, 2):
        windows = [
            own_block[dx + 1 : dx + 9, dy + 1 : dy + 9].reshape(1024, 128)
            for dx, dy in PLANAR[first : first + 2]
        ]
        product = jnp.dot(back_t, jnp.concatenate(windows, axis=1), preferred_element_type=F32)
        for i in range(len(windows)):
            turned = product[:, 128 * i : 128 * i + 128].T
            for tile in range(12):
                put_part(12 * (first + i) + tile, turned[8 * tile : 8 * tile + 8])
    for tile in range(108, 112):
        put_part(tile, jnp.zeros((8, 128), F32))
    for j in range(GROUP):
        stage[j * SENT + PART : (j + 1) * SENT] = jnp.zeros((16, 128), F32)

    def grad_lefts(first, count):
        return jnp.concatenate(
            [
                grads[1 - dx : 11 - dx, first : first + count].reshape(160 * count, 128)
                for dx in (-1, 0, 1)
            ],
            axis=1,
        )

    def grad_rights(dy):
        pieces = []
        for dx in (-1, 0, 1):
            first = (dx + 1) * 9 + (dy + 1) * 3
            piece = own_weights[first : first + 3].reshape(96, 128).astype(F32)
            piece = jnp.concatenate([piece, jnp.zeros((32, 128), F32)], axis=0)
            pieces.append(piece.T.astype(BF))
        return jnp.concatenate(pieces, axis=0)

    pair = jnp.concatenate([grad_rights(1), grad_rights(0)], axis=1)
    pair = jnp.dot(grad_lefts(0, 11), pair, preferred_element_type=F32).reshape(10, 11, 16, 256)
    spread = jnp.dot(grad_lefts(2, 10), grad_rights(-1), preferred_element_type=F32)
    spread = spread.reshape(10, 10, 16, 128)
    spread = spread + pair[:, 0:10, :, 0:128] + pair[:, 1:11, :, 128:256]
    spread = spread.reshape(100, 2, 8, 128)
    for brick in range(2):
        part = spread[:, brick]
        up = pltpu.roll(part, 7, 1)
        down = pltpu.roll(pltpu.roll(part, 64, 2), 1, 1)
        center = (
            pltpu.roll(part, 96, 2) + jnp.where(z < 7, up, 0.0) + jnp.where(z > 0, down, 0.0)
        )
        terms[0, brick] = jnp.where(z == 7, up, 0.0).reshape(10, 10, 8, 128)
        terms[1, brick] = center.reshape(10, 10, 8, 128)
        terms[2, brick] = jnp.where(z == 0, down, 0.0).reshape(10, 10, 8, 128)
    for brick in range(2):
        own_out[brick] = terms[1, brick, 1:9, 1:9]
    for dx, dy in PLANAR:
        pieces = [
            (near[brick, slot], terms[i, brick, RIM[dx], RIM[dy]])
            for brick in range(2)
            for i, slot in enumerate(planar_slots(dx, dy))
            if slot is not None
        ]

        def collected(target):
            total = 0.0
            for r, piece in pieces:
                total = total + jnp.where(r == target, piece, 0.0)
            return total

        for brick in range(2):
            own_out[brick, SIDE[dx], SIDE[dy]] += collected(brick)
        if (dx, dy) != (0, 0):
            rim = collected(2 + MOVES.index((dx, dy))).reshape(-1, 8, 128)
            target = lax.rem(place[0] + STEPS[dx, dy] + GROUP, GROUP)
            stage[rows_of(target, SENT, PART, 16)] = packed(rim)
    sent[...] = stage[...].astype(BF)


def middle_kernel(place, arrived, sent, held, stage):
    held[...] = arrived[...].astype(F32)
    total = held[0:PART]
    for j in range(1, GROUP):
        total = total + held[j * SENT : j * SENT + PART]
    planes = stage.shape[0] // ONWARD
    for j in range(planes):
        stage[j * ONWARD : j * ONWARD + PART] = total
        stage[j * ONWARD + PART : (j + 1) * ONWARD] = jnp.zeros((24, 128), F32)
    lane = lax.broadcasted_iota(jnp.int32, (8, 128), 1)
    for a in (-1, 1):
        rims = {
            b: held[rows_of(lax.rem(place[0] - STEPS[a, b] + GROUP, GROUP), SENT, PART, 16 if b == 0 else 8)]
            for b in (-1, 0, 1)
        }
        edges = jnp.where(lane < 32, rims[-1], pltpu.roll(rims[1], 32, 1))
        target = place[1] + a

        @pl.when((target >= 0) & (target < planes))
        def _():
            stage[rows_of(target, ONWARD, PART, 24)] = jnp.concatenate([rims[0], edges], axis=0)

    sent[...] = stage[...].astype(BF)


def sum_kernel(scale, arrived, sent):
    values = arrived[...].astype(F32)
    total = values[0:PART]
    for j in range(1, values.shape[0] // ONWARD):
        total = total + values[j * ONWARD : j * ONWARD + PART]
    sent[...] = jnp.concatenate([total * scale] * GROUP, axis=0).astype(BF)


def final_kernel(send, place, mask, own, direct, onward, out, total, held, passed):
    total[...] = own[...]
    held[...] = direct[...].astype(F32)
    passed[...] = onward[...].astype(F32)
    inner, outer = place[0], place[1]
    for dx, dy in MOVES:
        s = send[MOVES.index((dx, dy))]
        origin = inner - STEPS[dx, dy]
        size = 8 if dx and dy else 16
        rows = held[rows_of(lax.rem(origin + GROUP, GROUP), SENT, PART, size)]
        if dx:
            passer = jnp.clip(outer - dx, 0, passed.shape[0] // ONWARD - 1)
            other = passed[rows_of(passer, ONWARD, PART + 16 if dy else PART, size)]
            if dy == 1:
                other = pltpu.roll(other, 96, 1)
            rows = jnp.where((origin >= 0) & (origin < GROUP), rows, other)
        piece = unpacked(rows, 1 if dx and dy else 8)
        nx = 8 if dx == 0 else 1
        piece = piece.reshape(nx, piece.shape[0] // nx, 8, 128)
        for brick in range(2):
            total[brick, SIDE[dx], SIDE[dy]] += jnp.where(s == brick, piece, 0.0)
    for brick in range(2):
        rows = total[brick].reshape(512, 128).T[0:32] * mask[brick : brick + 1, :]
        out[brick] = rows.astype(BF)


SMEM = pl.BlockSpec(memory_space=pltpu.SMEM)
VMEM = pl.BlockSpec(memory_space=pltpu.VMEM)


def call(kernel, name, smem, vmem, outs, scratch, limit, cost=None):
    shapes = [jax.ShapeDtypeStruct(s, d) for s, d in outs]
    return pl.pallas_call(
        kernel,
        out_shape=shapes,
        in_specs=[SMEM] * len(smem) + [VMEM] * len(vmem),
        out_specs=[VMEM] * len(outs),
        scratch_shapes=[pltpu.VMEM(s, d) for s, d in scratch],
        compiler_params=pltpu.CompilerParams(vmem_limit_bytes=limit << 20),
        cost_estimate=cost,
        name=name,
    )(*smem, *vmem)


def passed_along(shard, by):
    count = lax.axis_size("space")
    pairs = [(i, i + by) for i in range(count) if 0 <= i + by < count]
    if abs(by) == 1:
        pairs = [(i, j) for i, j in pairs if i // 4 == j // 4]
    return lax.ppermute(shard, "space", pairs)


def unpack_mask(packed):
    shifts = jnp.arange(32, dtype=jnp.int32)
    bits = lax.shift_right_logical(packed[:, :, None], shifts[None, None, :]) & 1
    return bits.reshape(packed.shape[0], packed.shape[1] * 32).astype(F32)


def exchanged(values, far):
    count = lax.axis_size("space")
    planes = count // GROUP
    groups = [[j * GROUP + i for i in range(GROUP)] for j in range(planes)]
    if far:
        groups = [list(members) for members in zip(*groups)]
    return lax.all_to_all(values, "space", 0, 0, tiled=True, axis_index_groups=groups)


def from_all_chan(part):
    count = lax.axis_size("chan")
    copies = jnp.broadcast_to(part[None], (count,) + part.shape)
    return lax.all_to_all(copies, "chan", 0, 0, tiled=True)


def on_device(features, mask_packed, neighbours, send_list, weights, cotangent):
    chan = lax.axis_index("chan").astype(jnp.int32).reshape(1)
    send = send_list.reshape(8)
    where = lax.axis_index("space").astype(jnp.int32)
    place = jnp.stack([where % GROUP, where // GROUP])
    planes = lax.axis_size("space") // GROUP
    mask = unpack_mask(mask_packed)
    gathered = from_all_chan(features)
    by_lanes = cotangent.reshape(32, 8, 128).transpose(1, 0, 2)
    (extra,) = call(
        copies_kernel, "copies", [], [weights, by_lanes], [((4, 35, 32, 128), BF)], [], 16,
        pl.CostEstimate(flops=0, bytes_accessed=8 << 20, transcendentals=0),
    )
    extra = lax.all_to_all(extra, "chan", 0, 0, tiled=True)
    local, to_b, face_a = call(
        rims_kernel, "rims", [send], [mask, gathered],
        [((2, 8, 8, 8, 128), F32), ((2, 80, 128), BF), ((2, 64, 128), BF)], [], 16,
    )
    from_bm, from_bp = passed_along(to_b[0], 1), passed_along(to_b[1], -1)
    to_am = jnp.concatenate([face_a[0], from_bm[64:72], from_bp[64:72]], axis=0)
    to_ap = jnp.concatenate([face_a[1], from_bm[72:80], from_bp[72:80]], axis=0)
    from_am, from_ap = passed_along(to_am, 4), passed_along(to_ap, -4)
    center_pre, center_own = call(
        center_kernel, "center", [neighbours, chan], [local, from_bm, from_bp, extra],
        [((8, 8, 16, 128), F32), ((8, 10, 16, 128), BF)], [((3, 10, 10, 16, 128), BF)], 24,
        pl.CostEstimate(flops=1 << 30, bytes_accessed=3 << 20, transcendentals=0),
    )
    act, sent, own = call(
        main_kernel, "conv", [neighbours, chan, place],
        [mask, local, from_am, from_ap, center_pre, center_own, extra, weights],
        [
            ((2, 32, 512), BF), ((GROUP * SENT, 128), BF), ((2, 8, 8, 8, 128), F32),
        ],
        [
            ((2, 3, 10, 16, 128), BF), ((12, 12, 16, 128), BF), ((10, 10, 16, 128), BF),
            ((2, 128, 512), BF), ((3, 2, 10, 10, 8, 128), F32), ((GROUP * SENT, 128), F32),
        ],
        32,
    )
    scale = 1.0 / math.sqrt(2 * lax.axis_size("space") * 512)
    direct = exchanged(sent, False)
    (sent,) = call(
        middle_kernel, "middle", [place], [direct], [((planes * ONWARD, 128), BF)],
        [((GROUP * SENT, 128), F32), ((planes * ONWARD, 128), F32)], 16,
    )
    onward = exchanged(sent, True)
    (sent,) = call(
        functools.partial(sum_kernel, scale), "sums", [], [onward], [((GROUP * PART, 128), BF)], [], 16
    )
    summed = exchanged(sent, False)
    grad_weights = summed[:864].astype(F32).reshape(27, 32, 128)
    (grad,) = call(
        final_kernel, "grad", [send, place], [mask, own, direct, onward],
        [((2, 32, 512), BF)],
        [((2, 8, 8, 8, 128), F32), ((GROUP * SENT, 128), F32), ((planes * ONWARD, 128), F32)], 16,
    )
    return act.transpose(1, 0, 2), grad.transpose(1, 0, 2), grad_weights


def solution(mesh):
    return jax.shard_map(
        on_device,
        mesh=mesh,
        in_specs=(
            P("chan", "space", None),
            P("space", None),
            P("space", None),
            P("space", None, None),
            P(None, "chan", None),
            P("chan", "space", None),
        ),
        out_specs=(P("chan", "space", None), P("chan", "space", None), P(None, "chan", None)),
        check_vma=False,
    )
```

```python
import functools
import math

import jax
import jax.numpy as jnp
from jax import lax
from jax.experimental import pallas as pl
from jax.experimental.pallas import tpu as pltpu
from jax.sharding import PartitionSpec as P

BF = jnp.bfloat16
F32 = jnp.float32
SIDE = {-1: slice(7, 8), 0: slice(0, 8), 1: slice(0, 1)}
RIM = {-1: slice(0, 1), 0: slice(1, 9), 1: slice(9, 10)}
PLANAR = [(a, b) for a in (-1, 0, 1) for b in (-1, 0, 1)]
MOVES = [m for m in PLANAR if m != (0, 0)]
STEPS = {(a, b): 4 * a + b for a, b in MOVES}
GROUP = 16
PART = 56
SENT = PART + 16
ONWARD = PART + 24


def slot_of(dx, dy, dz):
    linear = (dx + 1) * 9 + (dy + 1) * 3 + dz + 1
    return linear if linear < 13 else linear - 1


def planar_slots(dx, dy):
    return [None if (dx, dy, dz) == (0, 0, 0) else slot_of(dx, dy, dz) for dz in (-1, 0, 1)]


def tiles(ref_or_value, dx, dy):
    part = ref_or_value[SIDE[dx], SIDE[dy]]
    return part.reshape(-1, 8, 128)


def packed(rim):
    if rim.shape[0] == 1:
        return jnp.concatenate([rim[0], jnp.zeros((8, 128), F32)], axis=0)
    lane = lax.broadcasted_iota(jnp.int32, (8, 128), 1)
    halves = []
    for first in (0, 4):
        value = rim[first]
        for j in (1, 2, 3):
            value = jnp.where(lane < 32 * j, value, pltpu.roll(rim[first + j], 32 * j, 1))
        halves.append(value)
    return jnp.concatenate(halves, axis=0)


def unpacked(rows, count):
    pieces = []
    for i in range(count):
        value = rows[8 * (i // 4) : 8 * (i // 4) + 8]
        pieces.append(pltpu.roll(value, 128 - 32 * (i % 4), 1) if i % 4 else value)
    return jnp.stack(pieces)


def rows_of(index, stride, first, count):
    return pl.ds(pl.multiple_of(index * stride + first, 8), count)


def feature_copies_kernel(features, out):
    value = features[...]
    for i in range(out.shape[0]):
        out[i] = value


def copies_kernel(weights, by_lanes, out):
    for i in range(out.shape[0]):
        out[i, 0:27] = weights[...]
        out[i, 27:35] = by_lanes[...]


def rims_kernel(send, mask, gathered, local, to_b, face_a):
    both = gathered[...].reshape(128, 2, 512).astype(F32)
    for brick in range(2):
        rows = both[:, brick] * mask[brick : brick + 1, :]
        local[brick] = rows.T.reshape(8, 8, 8, 128)

    def chosen(move):
        s = send[MOVES.index(move)]
        first, second = (tiles(local[brick], *move) for brick in range(2))
        return jnp.where(s == 0, first, jnp.where(s == 1, second, 0.0))

    for i, b in enumerate((-1, 1)):
        parts = [chosen((0, b)), chosen((-1, b)), chosen((1, b))]
        to_b[i] = jnp.concatenate(parts, axis=0).reshape(80, 128).astype(BF)
    for i, a in enumerate((-1, 1)):
        face_a[i] = chosen((a, 0)).reshape(64, 128).astype(BF)


def block_tiles(near, local, arrived, dx, dy):
    z = lax.broadcasted_iota(jnp.int32, (1, 8, 128), 1)
    options = [tiles(local[0], dx, dy), tiles(local[1], dx, dy)]
    rows = [0, 1]
    if (dx, dy) != (0, 0):
        options.append(arrived)
        rows.append(2 + MOVES.index((dx, dy)))

    def pick(r):
        value = 0.0
        for row, option in zip(rows, options):
            value = jnp.where(r == row, option, value)
        return value

    shifted = [[], [], []]
    for brick in range(2):
        below, level, above = planar_slots(dx, dy)
        center = options[brick] if level is None else pick(near[brick, level])
        under, over = pick(near[brick, below]), pick(near[brick, above])
        shifted[0].append(pltpu.roll(jnp.where(z == 7, under, center), 1, 1))
        shifted[1].append(center)
        shifted[2].append(pltpu.roll(jnp.where(z == 0, over, center), 7, 1))
    return [jnp.stack(pair, axis=1).reshape(-1, 16, 128).astype(BF) for pair in shifted]


def selection(chan):
    row = lax.broadcasted_iota(jnp.int32, (384, 128), 0)
    column = lax.broadcasted_iota(jnp.int32, (384, 128), 1)
    wanted = (row >> 7 == column >> 5) & ((row & 127) == chan * 32 + (column & 31))
    return jnp.where(wanted, 1.0, 0.0).astype(BF)


def center_kernel(near, chan, local, from_bm, from_bp, extra, pre_out, own_out, blocks):
    for i in range(3):
        for plane in (0, 9):
            blocks[i, plane] = jnp.zeros((10, 16, 128), BF)
    for dy, part in ((-1, from_bm), (0, None), (1, from_bp)):
        arrived = None if part is None else part[0:64].astype(F32).reshape(8, 8, 128)
        for i, value in enumerate(block_tiles(near, local, arrived, 0, dy)):
            blocks[i, 1:9, RIM[dy]] = value.reshape(8, -1, 16, 128)

    def lefts(first, count):
        return jnp.concatenate(
            [
                blocks[dz, dx : dx + 8, first : first + count].reshape(128 * count, 128)
                for dx in range(3)
                for dz in range(3)
            ],
            axis=1,
        )

    def rights(dy):
        return jnp.concatenate(
            [
                extra[:, 9 * dx + 3 * dy + dz].reshape(128, 128)
                for dx in range(3)
                for dz in range(3)
            ],
            axis=0,
        )

    pair = jnp.concatenate([rights(0), rights(1)], axis=1)
    pair = jnp.dot(lefts(0, 9), pair, preferred_element_type=F32).reshape(8, 9, 16, 256)
    pre = jnp.dot(lefts(2, 8), rights(2), preferred_element_type=F32).reshape(8, 8, 16, 128)
    pre_out[...] = pre + pair[:, 0:8, :, 0:128] + pair[:, 1:9, :, 128:256]
    stacked = jnp.concatenate([blocks[dz, 1:9].reshape(1280, 128) for dz in range(3)], axis=1)
    own = jnp.dot(stacked, selection(chan[0]), preferred_element_type=F32).astype(BF)
    own_out[...] = own.reshape(8, 10, 16, 128)


def main_kernel(
    near, chan, place, mask, local, from_am, from_ap, center_pre, center_own, extra, own_weights,
    act_out, sent, own_out,
    rim, grads, own_block, act_all, terms, stage,
):
    z = lax.broadcasted_iota(jnp.int32, (1, 8, 128), 1)
    own_block[1:9] = center_own[...]
    edges = []
    for side, (dx, part) in enumerate(((-1, from_am), (1, from_ap))):
        corner = part[64:80].astype(F32).reshape(2, 8, 128)
        face = part[0:64].astype(F32).reshape(8, 8, 128)
        for dy, arrived in ((-1, corner[0:1]), (0, face), (1, corner[1:2])):
            for i, value in enumerate(block_tiles(near, local, arrived, dx, dy)):
                rim[side, i, RIM[dy]] = value
        left = jnp.concatenate(
            [rim[side, dz, dy : dy + 8].reshape(128, 128) for dy in range(3) for dz in range(3)],
            axis=1,
        )
        right = jnp.concatenate(
            [extra[:, 9 * (dx + 1) + o].reshape(128, 128) for o in range(9)], axis=0
        )
        edges.append(jnp.dot(left, right, preferred_element_type=F32).reshape(1, 8, 16, 128))
        stacked = jnp.concatenate([rim[side, dz].reshape(160, 128) for dz in range(3)], axis=1)
        own = jnp.dot(stacked, selection(chan[0]), preferred_element_type=F32).astype(BF)
        own_block[9 * side] = own.reshape(10, 16, 128)
    pre = center_pre[...]
    pre = jnp.concatenate([pre[0:1] + edges[0], pre[1:7], pre[7:8] + edges[1]], axis=0)
    pre = pre.reshape(64, 2, 8, 128)

    back = []
    for brick in range(2):
        on = mask[brick : brick + 1, :]
        pre_act = pre[:, brick].reshape(512, 128).T * on
        gate = jax.nn.sigmoid(pre_act)
        act_all[brick] = (pre_act * gate).astype(BF)
        cotangent = jnp.concatenate(
            [extra[:, 27 + 4 * brick + i].reshape(128, 128).astype(F32) for i in range(4)], axis=1
        )
        grad = cotangent * on * gate * (1.0 + pre_act * (1.0 - gate))
        back.append(grad.T.reshape(64, 8, 128))
    start = pl.multiple_of(chan[0] * 32, 32)
    for brick in range(2):
        act_out[brick] = act_all[brick, pl.ds(start, 32), :]
    back = jnp.stack(back, axis=1).reshape(1024, 128)
    grads[...] = jnp.zeros(grads.shape, BF)
    grads[2:10, 2:10] = back.astype(BF).reshape(8, 8, 16, 128)
    back_t = back.T.astype(BF)

    def put_part(tile, value):
        first = tile // 7 * SENT + tile % 7 * 8
        stage[first : first + 8] = value

    for first in range(0, 9, 2):
        windows = [
            own_block[dx + 1 : dx + 9, dy + 1 : dy + 9].reshape(1024, 128)
            for dx, dy in PLANAR[first : first + 2]
        ]
        product = jnp.dot(back_t, jnp.concatenate(windows, axis=1), preferred_element_type=F32)
        for i in range(len(windows)):
            turned = product[:, 128 * i : 128 * i + 128].T
            for tile in range(12):
                put_part(12 * (first + i) + tile, turned[8 * tile : 8 * tile + 8])
    for tile in range(108, 112):
        put_part(tile, jnp.zeros((8, 128), F32))
    for j in range(GROUP):
        stage[j * SENT + PART : (j + 1) * SENT] = jnp.zeros((16, 128), F32)

    def grad_lefts(first, count):
        return jnp.concatenate(
            [
                grads[1 - dx : 11 - dx, first : first + count].reshape(160 * count, 128)
                for dx in (-1, 0, 1)
            ],
            axis=1,
        )

    def grad_rights(dy):
        pieces = []
        for dx in (-1, 0, 1):
            first = (dx + 1) * 9 + (dy + 1) * 3
            piece = own_weights[first : first + 3].reshape(96, 128).astype(F32)
            piece = jnp.concatenate([piece, jnp.zeros((32, 128), F32)], axis=0)
            pieces.append(piece.T.astype(BF))
        return jnp.concatenate(pieces, axis=0)

    pair = jnp.concatenate([grad_rights(1), grad_rights(0)], axis=1)
    pair = jnp.dot(grad_lefts(0, 11), pair, preferred_element_type=F32).reshape(10, 11, 16, 256)
    spread = jnp.dot(grad_lefts(2, 10), grad_rights(-1), preferred_element_type=F32)
    spread = spread.reshape(10, 10, 16, 128)
    spread = spread + pair[:, 0:10, :, 0:128] + pair[:, 1:11, :, 128:256]
    spread = spread.reshape(100, 2, 8, 128)
    for brick in range(2):
        part = spread[:, brick]
        up = pltpu.roll(part, 7, 1)
        down = pltpu.roll(pltpu.roll(part, 64, 2), 1, 1)
        center = (
            pltpu.roll(part, 96, 2) + jnp.where(z < 7, up, 0.0) + jnp.where(z > 0, down, 0.0)
        )
        terms[0, brick] = jnp.where(z == 7, up, 0.0).reshape(10, 10, 8, 128)
        terms[1, brick] = center.reshape(10, 10, 8, 128)
        terms[2, brick] = jnp.where(z == 0, down, 0.0).reshape(10, 10, 8, 128)
    for brick in range(2):
        own_out[brick] = terms[1, brick, 1:9, 1:9]
    for dx, dy in PLANAR:
        pieces = [
            (near[brick, slot], terms[i, brick, RIM[dx], RIM[dy]])
            for brick in range(2)
            for i, slot in enumerate(planar_slots(dx, dy))
            if slot is not None
        ]

        def collected(target):
            total = 0.0
            for r, piece in pieces:
                total = total + jnp.where(r == target, piece, 0.0)
            return total

        for brick in range(2):
            own_out[brick, SIDE[dx], SIDE[dy]] += collected(brick)
        if (dx, dy) != (0, 0):
            rim = collected(2 + MOVES.index((dx, dy))).reshape(-1, 8, 128)
            target = lax.rem(place[0] + STEPS[dx, dy] + GROUP, GROUP)
            stage[rows_of(target, SENT, PART, 16)] = packed(rim)
    sent[...] = stage[...].astype(BF)


def middle_kernel(place, arrived, sent, held, stage):
    held[...] = arrived[...].astype(F32)
    total = held[0:PART]
    for j in range(1, GROUP):
        total = total + held[j * SENT : j * SENT + PART]
    planes = stage.shape[0] // ONWARD
    for j in range(planes):
        stage[j * ONWARD : j * ONWARD + PART] = total
        stage[j * ONWARD + PART : (j + 1) * ONWARD] = jnp.zeros((24, 128), F32)
    lane = lax.broadcasted_iota(jnp.int32, (8, 128), 1)
    for a in (-1, 1):
        rims = {
            b: held[rows_of(lax.rem(place[0] - STEPS[a, b] + GROUP, GROUP), SENT, PART, 16 if b == 0 else 8)]
            for b in (-1, 0, 1)
        }
        edges = jnp.where(lane < 32, rims[-1], pltpu.roll(rims[1], 32, 1))
        target = place[1] + a

        @pl.when((target >= 0) & (target < planes))
        def _():
            stage[rows_of(target, ONWARD, PART, 24)] = jnp.concatenate([rims[0], edges], axis=0)

    sent[...] = stage[...].astype(BF)


def sum_kernel(scale, arrived, sent):
    values = arrived[...].astype(F32)
    total = values[0:PART]
    for j in range(1, values.shape[0] // ONWARD):
        total = total + values[j * ONWARD : j * ONWARD + PART]
    sent[...] = jnp.concatenate([total * scale] * GROUP, axis=0).astype(BF)


def final_kernel(send, place, mask, own, direct, onward, out, total, held, passed):
    total[...] = own[...]
    held[...] = direct[...].astype(F32)
    passed[...] = onward[...].astype(F32)
    inner, outer = place[0], place[1]
    for dx, dy in MOVES:
        s = send[MOVES.index((dx, dy))]
        origin = inner - STEPS[dx, dy]
        size = 8 if dx and dy else 16
        rows = held[rows_of(lax.rem(origin + GROUP, GROUP), SENT, PART, size)]
        if dx:
            passer = jnp.clip(outer - dx, 0, passed.shape[0] // ONWARD - 1)
            other = passed[rows_of(passer, ONWARD, PART + 16 if dy else PART, size)]
            if dy == 1:
                other = pltpu.roll(other, 96, 1)
            rows = jnp.where((origin >= 0) & (origin < GROUP), rows, other)
        piece = unpacked(rows, 1 if dx and dy else 8)
        nx = 8 if dx == 0 else 1
        piece = piece.reshape(nx, piece.shape[0] // nx, 8, 128)
        for brick in range(2):
            total[brick, SIDE[dx], SIDE[dy]] += jnp.where(s == brick, piece, 0.0)
    for brick in range(2):
        rows = total[brick].reshape(512, 128).T[0:32] * mask[brick : brick + 1, :]
        out[brick] = rows.astype(BF)


SMEM = pl.BlockSpec(memory_space=pltpu.SMEM)
VMEM = pl.BlockSpec(memory_space=pltpu.VMEM)


def call(kernel, name, smem, vmem, outs, scratch, limit, cost=None):
    shapes = [jax.ShapeDtypeStruct(s, d) for s, d in outs]
    return pl.pallas_call(
        kernel,
        out_shape=shapes,
        in_specs=[SMEM] * len(smem) + [VMEM] * len(vmem),
        out_specs=[VMEM] * len(outs),
        scratch_shapes=[pltpu.VMEM(s, d) for s, d in scratch],
        compiler_params=pltpu.CompilerParams(vmem_limit_bytes=limit << 20),
        cost_estimate=cost,
        name=name,
    )(*smem, *vmem)


def passed_along(shard, by):
    count = lax.axis_size("space")
    pairs = [(i, i + by) for i in range(count) if 0 <= i + by < count]
    if abs(by) == 1:
        pairs = [(i, j) for i, j in pairs if i // 4 == j // 4]
    return lax.ppermute(shard, "space", pairs)


def unpack_mask(packed):
    shifts = jnp.arange(32, dtype=jnp.int32)
    bits = lax.shift_right_logical(packed[:, :, None], shifts[None, None, :]) & 1
    return bits.reshape(packed.shape[0], packed.shape[1] * 32).astype(F32)


def exchanged(values, far):
    count = lax.axis_size("space")
    planes = count // GROUP
    groups = [[j * GROUP + i for i in range(GROUP)] for j in range(planes)]
    if far:
        groups = [list(members) for members in zip(*groups)]
    return lax.all_to_all(values, "space", 0, 0, tiled=True, axis_index_groups=groups)


def on_device(features, mask_packed, neighbours, send_list, weights, cotangent):
    chan = lax.axis_index("chan").astype(jnp.int32).reshape(1)
    send = send_list.reshape(8)
    where = lax.axis_index("space").astype(jnp.int32)
    place = jnp.stack([where % GROUP, where // GROUP])
    planes = lax.axis_size("space") // GROUP
    mask = unpack_mask(mask_packed)
    (copies,) = call(feature_copies_kernel, "sent", [], [features], [((4, 32, 2, 512), BF)], [], 16)
    gathered = lax.all_to_all(copies, "chan", 0, 0, tiled=True)
    by_lanes = cotangent.reshape(32, 8, 128).transpose(1, 0, 2)
    (extra,) = call(
        copies_kernel, "copies", [], [weights, by_lanes], [((4, 35, 32, 128), BF)], [], 16,
        pl.CostEstimate(flops=0, bytes_accessed=8 << 20, transcendentals=0),
    )
    extra = lax.all_to_all(extra, "chan", 0, 0, tiled=True)
    local, to_b, face_a = call(
        rims_kernel, "rims", [send], [mask, gathered],
        [((2, 8, 8, 8, 128), F32), ((2, 80, 128), BF), ((2, 64, 128), BF)], [], 16,
    )
    from_bm, from_bp = passed_along(to_b[0], 1), passed_along(to_b[1], -1)
    to_am = jnp.concatenate([face_a[0], from_bm[64:72], from_bp[64:72]], axis=0)
    to_ap = jnp.concatenate([face_a[1], from_bm[72:80], from_bp[72:80]], axis=0)
    from_am, from_ap = passed_along(to_am, 4), passed_along(to_ap, -4)
    center_pre, center_own = call(
        center_kernel, "center", [neighbours, chan], [local, from_bm, from_bp, extra],
        [((8, 8, 16, 128), F32), ((8, 10, 16, 128), BF)], [((3, 10, 10, 16, 128), BF)], 24,
        pl.CostEstimate(flops=1 << 30, bytes_accessed=3 << 20, transcendentals=0),
    )
    act, sent, own = call(
        main_kernel, "conv", [neighbours, chan, place],
        [mask, local, from_am, from_ap, center_pre, center_own, extra, weights],
        [
            ((2, 32, 512), BF), ((GROUP * SENT, 128), BF), ((2, 8, 8, 8, 128), F32),
        ],
        [
            ((2, 3, 10, 16, 128), BF), ((12, 12, 16, 128), BF), ((10, 10, 16, 128), BF),
            ((2, 128, 512), BF), ((3, 2, 10, 10, 8, 128), F32), ((GROUP * SENT, 128), F32),
        ],
        32,
    )
    scale = 1.0 / math.sqrt(2 * lax.axis_size("space") * 512)
    direct = exchanged(sent, False)
    (sent,) = call(
        middle_kernel, "middle", [place], [direct], [((planes * ONWARD, 128), BF)],
        [((GROUP * SENT, 128), F32), ((planes * ONWARD, 128), F32)], 16,
    )
    onward = exchanged(sent, True)
    (sent,) = call(
        functools.partial(sum_kernel, scale), "sums", [], [onward], [((GROUP * PART, 128), BF)], [], 16
    )
    summed = exchanged(sent, False)
    grad_weights = summed[:864].astype(F32).reshape(27, 32, 128)
    (grad,) = call(
        final_kernel, "grad", [send, place], [mask, own, direct, onward],
        [((2, 32, 512), BF)],
        [((2, 8, 8, 8, 128), F32), ((GROUP * SENT, 128), F32), ((planes * ONWARD, 128), F32)], 16,
    )
    return act.transpose(1, 0, 2), grad.transpose(1, 0, 2), grad_weights


def solution(mesh):
    return jax.shard_map(
        on_device,
        mesh=mesh,
        in_specs=(
            P("chan", "space", None),
            P("space", None),
            P("space", None),
            P("space", None, None),
            P(None, "chan", None),
            P("chan", "space", None),
        ),
        out_specs=(P("chan", "space", None), P("chan", "space", None), P(None, "chan", None)),
        check_vma=False,
    )
```

```python
import functools
import math

import jax
import jax.numpy as jnp
from jax import lax
from jax.experimental import pallas as pl
from jax.experimental.pallas import tpu as pltpu
from jax.sharding import PartitionSpec as P

BF = jnp.bfloat16
F32 = jnp.float32
SIDE = {-1: slice(7, 8), 0: slice(0, 8), 1: slice(0, 1)}
RIM = {-1: slice(0, 1), 0: slice(1, 9), 1: slice(9, 10)}
PLANAR = [(a, b) for a in (-1, 0, 1) for b in (-1, 0, 1)]
MOVES = [m for m in PLANAR if m != (0, 0)]
STEPS = {(a, b): 4 * a + b for a, b in MOVES}
GROUP = 16
PART = 56
SENT = PART + 16
ONWARD = PART + 24


def slot_of(dx, dy, dz):
    linear = (dx + 1) * 9 + (dy + 1) * 3 + dz + 1
    return linear if linear < 13 else linear - 1


def planar_slots(dx, dy):
    return [None if (dx, dy, dz) == (0, 0, 0) else slot_of(dx, dy, dz) for dz in (-1, 0, 1)]


def tiles(ref_or_value, dx, dy):
    part = ref_or_value[SIDE[dx], SIDE[dy]]
    return part.reshape(-1, 8, 128)


def packed(rim):
    if rim.shape[0] == 1:
        return jnp.concatenate([rim[0], jnp.zeros((8, 128), F32)], axis=0)
    lane = lax.broadcasted_iota(jnp.int32, (8, 128), 1)
    halves = []
    for first in (0, 4):
        value = rim[first]
        for j in (1, 2, 3):
            value = jnp.where(lane < 32 * j, value, pltpu.roll(rim[first + j], 32 * j, 1))
        halves.append(value)
    return jnp.concatenate(halves, axis=0)


def unpacked(rows, count):
    pieces = []
    for i in range(count):
        value = rows[8 * (i // 4) : 8 * (i // 4) + 8]
        pieces.append(pltpu.roll(value, 128 - 32 * (i % 4), 1) if i % 4 else value)
    return jnp.stack(pieces)


def rows_of(index, stride, first, count):
    return pl.ds(pl.multiple_of(index * stride + first, 8), count)


def feature_copies_kernel(features, out):
    value = features[...]
    for i in range(out.shape[0]):
        out[i] = value


def copies_kernel(weights, by_lanes, out):
    for i in range(out.shape[0]):
        out[i, 0:27] = weights[...]
        out[i, 27:35] = by_lanes[...]


def rims_kernel(send, mask, gathered, local, to_b, face_a):
    both = gathered[...].reshape(128, 2, 512).astype(F32)
    for brick in range(2):
        rows = both[:, brick] * mask[brick : brick + 1, :]
        local[brick] = rows.T.reshape(8, 8, 8, 128)

    def chosen(move):
        s = send[MOVES.index(move)]
        first, second = (tiles(local[brick], *move) for brick in range(2))
        return jnp.where(s == 0, first, jnp.where(s == 1, second, 0.0))

    for i, b in enumerate((-1, 1)):
        parts = [chosen((0, b)), chosen((-1, b)), chosen((1, b))]
        to_b[i] = jnp.concatenate(parts, axis=0).reshape(80, 128).astype(BF)
    for i, a in enumerate((-1, 1)):
        face_a[i] = chosen((a, 0)).reshape(64, 128).astype(BF)


def block_tiles(near, local, arrived, dx, dy):
    z = lax.broadcasted_iota(jnp.int32, (1, 8, 128), 1)
    options = [tiles(local[0], dx, dy), tiles(local[1], dx, dy)]
    rows = [0, 1]
    if (dx, dy) != (0, 0):
        options.append(arrived)
        rows.append(2 + MOVES.index((dx, dy)))

    def pick(r):
        value = 0.0
        for row, option in zip(rows, options):
            value = jnp.where(r == row, option, value)
        return value

    shifted = [[], [], []]
    for brick in range(2):
        below, level, above = planar_slots(dx, dy)
        center = options[brick] if level is None else pick(near[brick, level])
        under, over = pick(near[brick, below]), pick(near[brick, above])
        shifted[0].append(pltpu.roll(jnp.where(z == 7, under, center), 1, 1))
        shifted[1].append(center)
        shifted[2].append(pltpu.roll(jnp.where(z == 0, over, center), 7, 1))
    return [jnp.stack(pair, axis=1).reshape(-1, 16, 128).astype(BF) for pair in shifted]


def selection(chan):
    row = lax.broadcasted_iota(jnp.int32, (384, 128), 0)
    column = lax.broadcasted_iota(jnp.int32, (384, 128), 1)
    wanted = (row >> 7 == column >> 5) & ((row & 127) == chan * 32 + (column & 31))
    return jnp.where(wanted, 1.0, 0.0).astype(BF)


def center_kernel(near, chan, local, from_bm, from_bp, extra, pre_out, own_out, blocks):
    for i in range(3):
        for plane in (0, 9):
            blocks[i, plane] = jnp.zeros((10, 16, 128), BF)
    for dy, part in ((-1, from_bm), (0, None), (1, from_bp)):
        arrived = None if part is None else part[0:64].astype(F32).reshape(8, 8, 128)
        for i, value in enumerate(block_tiles(near, local, arrived, 0, dy)):
            blocks[i, 1:9, RIM[dy]] = value.reshape(8, -1, 16, 128)

    def lefts(first, count):
        return jnp.concatenate(
            [
                blocks[dz, dx : dx + 8, first : first + count].reshape(128 * count, 128)
                for dx in range(3)
                for dz in range(3)
            ],
            axis=1,
        )

    def rights(dy):
        return jnp.concatenate(
            [
                extra[:, 9 * dx + 3 * dy + dz].reshape(128, 128)
                for dx in range(3)
                for dz in range(3)
            ],
            axis=0,
        )

    pair = jnp.concatenate([rights(0), rights(1)], axis=1)
    pair = jnp.dot(lefts(0, 9), pair, preferred_element_type=F32).reshape(8, 9, 16, 256)
    pre = jnp.dot(lefts(2, 8), rights(2), preferred_element_type=F32).reshape(8, 8, 16, 128)
    pre_out[...] = pre + pair[:, 0:8, :, 0:128] + pair[:, 1:9, :, 128:256]
    stacked = jnp.concatenate([blocks[dz, 1:9].reshape(1280, 128) for dz in range(3)], axis=1)
    own = jnp.dot(stacked, selection(chan[0]), preferred_element_type=F32).astype(BF)
    own_out[...] = own.reshape(8, 10, 16, 128)


def main_kernel(
    near, chan, place, mask, local, from_am, from_ap, center_pre, center_own, extra, own_weights,
    act_out, sent, own_out,
    rim, grads, own_block, act_all, terms, stage,
):
    z = lax.broadcasted_iota(jnp.int32, (1, 8, 128), 1)
    own_block[1:9] = center_own[...]
    edges = []
    for side, (dx, part) in enumerate(((-1, from_am), (1, from_ap))):
        corner = part[64:80].astype(F32).reshape(2, 8, 128)
        face = part[0:64].astype(F32).reshape(8, 8, 128)
        for dy, arrived in ((-1, corner[0:1]), (0, face), (1, corner[1:2])):
            for i, value in enumerate(block_tiles(near, local, arrived, dx, dy)):
                rim[side, i, RIM[dy]] = value
        left = jnp.concatenate(
            [rim[side, dz, dy : dy + 8].reshape(128, 128) for dy in range(3) for dz in range(3)],
            axis=1,
        )
        right = jnp.concatenate(
            [extra[:, 9 * (dx + 1) + o].reshape(128, 128) for o in range(9)], axis=0
        )
        edges.append(jnp.dot(left, right, preferred_element_type=F32).reshape(1, 8, 16, 128))
        stacked = jnp.concatenate([rim[side, dz].reshape(160, 128) for dz in range(3)], axis=1)
        own = jnp.dot(stacked, selection(chan[0]), preferred_element_type=F32).astype(BF)
        own_block[9 * side] = own.reshape(10, 16, 128)
    pre = center_pre[...]
    pre = jnp.concatenate([pre[0:1] + edges[0], pre[1:7], pre[7:8] + edges[1]], axis=0)
    pre = pre.reshape(64, 2, 8, 128)

    back = []
    for brick in range(2):
        on = mask[brick : brick + 1, :]
        pre_act = pre[:, brick].reshape(512, 128).T * on
        gate = jax.nn.sigmoid(pre_act)
        act_all[brick] = (pre_act * gate).astype(BF)
        cotangent = jnp.concatenate(
            [extra[:, 27 + 4 * brick + i].reshape(128, 128).astype(F32) for i in range(4)], axis=1
        )
        grad = cotangent * on * gate * (1.0 + pre_act * (1.0 - gate))
        back.append(grad.T.reshape(64, 8, 128))
    start = pl.multiple_of(chan[0] * 32, 32)
    for brick in range(2):
        act_out[brick] = act_all[brick, pl.ds(start, 32), :]
    back = jnp.stack(back, axis=1).reshape(1024, 128)
    grads[...] = jnp.zeros(grads.shape, BF)
    grads[2:10, 2:10] = back.astype(BF).reshape(8, 8, 16, 128)
    back_t = back.T.astype(BF)

    def put_part(tile, value):
        first = tile // 7 * SENT + tile % 7 * 8
        stage[first : first + 8] = value

    for first in range(0, 9, 2):
        windows = [
            own_block[dx + 1 : dx + 9, dy + 1 : dy + 9].reshape(1024, 128)
            for dx, dy in PLANAR[first : first + 2]
        ]
        product = jnp.dot(back_t, jnp.concatenate(windows, axis=1), preferred_element_type=F32)
        for i in range(len(windows)):
            turned = product[:, 128 * i : 128 * i + 128].T
            for tile in range(12):
                put_part(12 * (first + i) + tile, turned[8 * tile : 8 * tile + 8])
    for tile in range(108, 112):
        put_part(tile, jnp.zeros((8, 128), F32))
    for j in range(GROUP):
        stage[j * SENT + PART : (j + 1) * SENT] = jnp.zeros((16, 128), F32)

    def grad_lefts(first, count):
        return jnp.concatenate(
            [
                grads[1 - dx : 11 - dx, first : first + count].reshape(160 * count, 128)
                for dx in (-1, 0, 1)
            ],
            axis=1,
        )

    def grad_rights(dy):
        pieces = []
        for dx in (-1, 0, 1):
            first = (dx + 1) * 9 + (dy + 1) * 3
            piece = own_weights[first : first + 3].reshape(96, 128).astype(F32)
            piece = jnp.concatenate([piece, jnp.zeros((32, 128), F32)], axis=0)
            pieces.append(piece.T.astype(BF))
        return jnp.concatenate(pieces, axis=0)

    pair = jnp.concatenate([grad_rights(1), grad_rights(0)], axis=1)
    pair = jnp.dot(grad_lefts(0, 11), pair, preferred_element_type=F32).reshape(10, 11, 16, 256)
    spread = jnp.dot(grad_lefts(2, 10), grad_rights(-1), preferred_element_type=F32)
    spread = spread.reshape(10, 10, 16, 128)
    spread = spread + pair[:, 0:10, :, 0:128] + pair[:, 1:11, :, 128:256]
    spread = spread.reshape(100, 2, 8, 128)
    for brick in range(2):
        part = spread[:, brick]
        up = pltpu.roll(part, 7, 1)
        down = pltpu.roll(pltpu.roll(part, 64, 2), 1, 1)
        center = (
            pltpu.roll(part, 96, 2) + jnp.where(z < 7, up, 0.0) + jnp.where(z > 0, down, 0.0)
        )
        terms[0, brick] = jnp.where(z == 7, up, 0.0).reshape(10, 10, 8, 128)
        terms[1, brick] = center.reshape(10, 10, 8, 128)
        terms[2, brick] = jnp.where(z == 0, down, 0.0).reshape(10, 10, 8, 128)
    for brick in range(2):
        own_out[brick] = terms[1, brick, 1:9, 1:9]
    for dx, dy in PLANAR:
        pieces = [
            (near[brick, slot], terms[i, brick, RIM[dx], RIM[dy]])
            for brick in range(2)
            for i, slot in enumerate(planar_slots(dx, dy))
            if slot is not None
        ]

        def collected(target):
            total = 0.0
            for r, piece in pieces:
                total = total + jnp.where(r == target, piece, 0.0)
            return total

        for brick in range(2):
            own_out[brick, SIDE[dx], SIDE[dy]] += collected(brick)
        if (dx, dy) != (0, 0):
            rim = collected(2 + MOVES.index((dx, dy))).reshape(-1, 8, 128)
            target = lax.rem(place[0] + STEPS[dx, dy] + GROUP, GROUP)
            stage[rows_of(target, SENT, PART, 16)] = packed(rim)
    sent[...] = stage[...].astype(BF)


def middle_kernel(place, arrived, sent, held, stage):
    held[...] = arrived[...].astype(F32)
    total = held[0:PART]
    for j in range(1, GROUP):
        total = total + held[j * SENT : j * SENT + PART]
    planes = stage.shape[0] // ONWARD
    for j in range(planes):
        stage[j * ONWARD : j * ONWARD + PART] = total
        stage[j * ONWARD + PART : (j + 1) * ONWARD] = jnp.zeros((24, 128), F32)
    lane = lax.broadcasted_iota(jnp.int32, (8, 128), 1)
    for a in (-1, 1):
        rims = {
            b: held[rows_of(lax.rem(place[0] - STEPS[a, b] + GROUP, GROUP), SENT, PART, 16 if b == 0 else 8)]
            for b in (-1, 0, 1)
        }
        edges = jnp.where(lane < 32, rims[-1], pltpu.roll(rims[1], 32, 1))
        target = place[1] + a

        @pl.when((target >= 0) & (target < planes))
        def _():
            stage[rows_of(target, ONWARD, PART, 24)] = jnp.concatenate([rims[0], edges], axis=0)

    sent[...] = stage[...].astype(BF)


def sum_kernel(scale, arrived, sent):
    values = arrived[...].astype(F32)
    total = values[0:PART]
    for j in range(1, values.shape[0] // ONWARD):
        total = total + values[j * ONWARD : j * ONWARD + PART]
    sent[...] = jnp.concatenate([total * scale] * GROUP, axis=0).astype(BF)


def final_kernel(send, place, mask, own, direct, onward, out, total, held, passed):
    total[...] = own[...]
    held[...] = direct[...].astype(F32)
    passed[...] = onward[...].astype(F32)
    inner, outer = place[0], place[1]
    for dx, dy in MOVES:
        s = send[MOVES.index((dx, dy))]
        origin = inner - STEPS[dx, dy]
        size = 8 if dx and dy else 16
        rows = held[rows_of(lax.rem(origin + GROUP, GROUP), SENT, PART, size)]
        if dx:
            passer = jnp.clip(outer - dx, 0, passed.shape[0] // ONWARD - 1)
            other = passed[rows_of(passer, ONWARD, PART + 16 if dy else PART, size)]
            if dy == 1:
                other = pltpu.roll(other, 96, 1)
            rows = jnp.where((origin >= 0) & (origin < GROUP), rows, other)
        piece = unpacked(rows, 1 if dx and dy else 8)
        nx = 8 if dx == 0 else 1
        piece = piece.reshape(nx, piece.shape[0] // nx, 8, 128)
        for brick in range(2):
            total[brick, SIDE[dx], SIDE[dy]] += jnp.where(s == brick, piece, 0.0)
    for brick in range(2):
        rows = total[brick].reshape(512, 128).T[0:32] * mask[brick : brick + 1, :]
        out[brick] = rows.astype(BF)


SMEM = pl.BlockSpec(memory_space=pltpu.SMEM)
VMEM = pl.BlockSpec(memory_space=pltpu.VMEM)


def call(kernel, name, smem, vmem, outs, scratch, limit, cost=None):
    shapes = [jax.ShapeDtypeStruct(s, d) for s, d in outs]
    return pl.pallas_call(
        kernel,
        out_shape=shapes,
        in_specs=[SMEM] * len(smem) + [VMEM] * len(vmem),
        out_specs=[VMEM] * len(outs),
        scratch_shapes=[pltpu.VMEM(s, d) for s, d in scratch],
        compiler_params=pltpu.CompilerParams(vmem_limit_bytes=limit << 20),
        cost_estimate=cost,
        name=name,
    )(*smem, *vmem)


def passed_along(shard, by):
    count = lax.axis_size("space")
    pairs = [(i, i + by) for i in range(count) if 0 <= i + by < count]
    if abs(by) == 1:
        pairs = [(i, j) for i, j in pairs if i // 4 == j // 4]
    return lax.ppermute(shard, "space", pairs)


def unpack_mask(packed):
    shifts = jnp.arange(32, dtype=jnp.int32)
    bits = lax.shift_right_logical(packed[:, :, None], shifts[None, None, :]) & 1
    return bits.reshape(packed.shape[0], packed.shape[1] * 32).astype(F32)


def exchanged(values, far):
    count = lax.axis_size("space")
    planes = count // GROUP
    groups = [[j * GROUP + i for i in range(GROUP)] for j in range(planes)]
    if far:
        groups = [list(members) for members in zip(*groups)]
    return lax.all_to_all(values, "space", 0, 0, tiled=True, axis_index_groups=groups)


def on_device(features, mask_packed, neighbours, send_list, weights, cotangent):
    chan = lax.axis_index("chan").astype(jnp.int32).reshape(1)
    send = send_list.reshape(8)
    where = lax.axis_index("space").astype(jnp.int32)
    place = jnp.stack([where % GROUP, where // GROUP])
    planes = lax.axis_size("space") // GROUP
    mask = unpack_mask(mask_packed)
    (copies,) = call(feature_copies_kernel, "sent", [], [features], [((4, 32, 2, 512), BF)], [], 16)
    gathered = lax.all_to_all(copies, "chan", 0, 0, tiled=True)
    by_lanes = cotangent.reshape(32, 8, 128).transpose(1, 0, 2)
    (extra,) = call(
        copies_kernel, "copies", [], [weights, by_lanes], [((4, 35, 32, 128), BF)], [], 16,
        pl.CostEstimate(flops=0, bytes_accessed=8 << 20, transcendentals=0),
    )
    local, to_b, face_a = call(
        rims_kernel, "rims", [send], [mask, gathered],
        [((2, 8, 8, 8, 128), F32), ((2, 80, 128), BF), ((2, 64, 128), BF)], [], 16,
    )
    extra, to_b = lax.optimization_barrier((extra, to_b))
    extra = lax.all_to_all(extra, "chan", 0, 0, tiled=True)
    from_bm, from_bp = passed_along(to_b[0], 1), passed_along(to_b[1], -1)
    to_am = jnp.concatenate([face_a[0], from_bm[64:72], from_bp[64:72]], axis=0)
    to_ap = jnp.concatenate([face_a[1], from_bm[72:80], from_bp[72:80]], axis=0)
    from_am, from_ap = passed_along(to_am, 4), passed_along(to_ap, -4)
    center_pre, center_own = call(
        center_kernel, "center", [neighbours, chan], [local, from_bm, from_bp, extra],
        [((8, 8, 16, 128), F32), ((8, 10, 16, 128), BF)], [((3, 10, 10, 16, 128), BF)], 24,
        pl.CostEstimate(flops=1 << 30, bytes_accessed=3 << 20, transcendentals=0),
    )
    act, sent, own = call(
        main_kernel, "conv", [neighbours, chan, place],
        [mask, local, from_am, from_ap, center_pre, center_own, extra, weights],
        [
            ((2, 32, 512), BF), ((GROUP * SENT, 128), BF), ((2, 8, 8, 8, 128), F32),
        ],
        [
            ((2, 3, 10, 16, 128), BF), ((12, 12, 16, 128), BF), ((10, 10, 16, 128), BF),
            ((2, 128, 512), BF), ((3, 2, 10, 10, 8, 128), F32), ((GROUP * SENT, 128), F32),
        ],
        32,
    )
    scale = 1.0 / math.sqrt(2 * lax.axis_size("space") * 512)
    direct = exchanged(sent, False)
    (sent,) = call(
        middle_kernel, "middle", [place], [direct], [((planes * ONWARD, 128), BF)],
        [((GROUP * SENT, 128), F32), ((planes * ONWARD, 128), F32)], 16,
    )
    onward = exchanged(sent, True)
    (sent,) = call(
        functools.partial(sum_kernel, scale), "sums", [], [onward], [((GROUP * PART, 128), BF)], [], 16
    )
    summed = exchanged(sent, False)
    grad_weights = summed[:864].astype(F32).reshape(27, 32, 128)
    (grad,) = call(
        final_kernel, "grad", [send, place], [mask, own, direct, onward],
        [((2, 32, 512), BF)],
        [((2, 8, 8, 8, 128), F32), ((GROUP * SENT, 128), F32), ((planes * ONWARD, 128), F32)], 16,
    )
    return act.transpose(1, 0, 2), grad.transpose(1, 0, 2), grad_weights


def solution(mesh):
    return jax.shard_map(
        on_device,
        mesh=mesh,
        in_specs=(
            P("chan", "space", None),
            P("space", None),
            P("space", None),
            P("space", None, None),
            P(None, "chan", None),
            P("chan", "space", None),
        ),
        out_specs=(P("chan", "space", None), P("chan", "space", None), P(None, "chan", None)),
        check_vma=False,
    )
```

```python
import functools
import math

import jax
import jax.numpy as jnp
from jax import lax
from jax.experimental import pallas as pl
from jax.experimental.pallas import tpu as pltpu
from jax.sharding import PartitionSpec as P

BF = jnp.bfloat16
F32 = jnp.float32
SIDE = {-1: slice(7, 8), 0: slice(0, 8), 1: slice(0, 1)}
RIM = {-1: slice(0, 1), 0: slice(1, 9), 1: slice(9, 10)}
PLANAR = [(a, b) for a in (-1, 0, 1) for b in (-1, 0, 1)]
MOVES = [m for m in PLANAR if m != (0, 0)]
STEPS = {(a, b): 4 * a + b for a, b in MOVES}
GROUP = 16
PART = 56
SENT = PART + 16
ONWARD = PART + 24


def slot_of(dx, dy, dz):
    linear = (dx + 1) * 9 + (dy + 1) * 3 + dz + 1
    return linear if linear < 13 else linear - 1


def planar_slots(dx, dy):
    return [None if (dx, dy, dz) == (0, 0, 0) else slot_of(dx, dy, dz) for dz in (-1, 0, 1)]


def tiles(ref_or_value, dx, dy):
    part = ref_or_value[SIDE[dx], SIDE[dy]]
    return part.reshape(-1, 8, 128)


def packed(rim):
    if rim.shape[0] == 1:
        return jnp.concatenate([rim[0], jnp.zeros((8, 128), F32)], axis=0)
    lane = lax.broadcasted_iota(jnp.int32, (8, 128), 1)
    halves = []
    for first in (0, 4):
        value = rim[first]
        for j in (1, 2, 3):
            value = jnp.where(lane < 32 * j, value, pltpu.roll(rim[first + j], 32 * j, 1))
        halves.append(value)
    return jnp.concatenate(halves, axis=0)


def unpacked(rows, count):
    pieces = []
    for i in range(count):
        value = rows[8 * (i // 4) : 8 * (i // 4) + 8]
        pieces.append(pltpu.roll(value, 128 - 32 * (i % 4), 1) if i % 4 else value)
    return jnp.stack(pieces)


def rows_of(index, stride, first, count):
    return pl.ds(pl.multiple_of(index * stride + first, 8), count)


def feature_copies_kernel(features, out):
    value = features[...]
    for i in range(out.shape[0]):
        out[i] = value


def copies_kernel(weights, by_lanes, out):
    for i in range(out.shape[0]):
        out[i, 0:27] = weights[...]
        out[i, 27:35] = by_lanes[...]


def rims_kernel(send, mask, gathered, local, to_b, face_a):
    both = gathered[...].reshape(128, 2, 512).astype(F32)
    for brick in range(2):
        rows = both[:, brick] * mask[brick : brick + 1, :]
        local[brick] = rows.T.reshape(8, 8, 8, 128)

    def chosen(move):
        s = send[MOVES.index(move)]
        first, second = (tiles(local[brick], *move) for brick in range(2))
        return jnp.where(s == 0, first, jnp.where(s == 1, second, 0.0))

    for i, b in enumerate((-1, 1)):
        parts = [chosen((0, b)), chosen((-1, b)), chosen((1, b))]
        to_b[i] = jnp.concatenate(parts, axis=0).reshape(80, 128).astype(BF)
    for i, a in enumerate((-1, 1)):
        face_a[i] = chosen((a, 0)).reshape(64, 128).astype(BF)


def block_tiles(near, local, arrived, dx, dy):
    z = lax.broadcasted_iota(jnp.int32, (1, 8, 128), 1)
    options = [tiles(local[0], dx, dy), tiles(local[1], dx, dy)]
    rows = [0, 1]
    if (dx, dy) != (0, 0):
        options.append(arrived)
        rows.append(2 + MOVES.index((dx, dy)))

    def pick(r):
        value = 0.0
        for row, option in zip(rows, options):
            value = jnp.where(r == row, option, value)
        return value

    shifted = [[], [], []]
    for brick in range(2):
        below, level, above = planar_slots(dx, dy)
        center = options[brick] if level is None else pick(near[brick, level])
        under, over = pick(near[brick, below]), pick(near[brick, above])
        shifted[0].append(pltpu.roll(jnp.where(z == 7, under, center), 1, 1))
        shifted[1].append(center)
        shifted[2].append(pltpu.roll(jnp.where(z == 0, over, center), 7, 1))
    return [jnp.stack(pair, axis=1).reshape(-1, 16, 128).astype(BF) for pair in shifted]


def selection(chan):
    row = lax.broadcasted_iota(jnp.int32, (384, 128), 0)
    column = lax.broadcasted_iota(jnp.int32, (384, 128), 1)
    wanted = (row >> 7 == column >> 5) & ((row & 127) == chan * 32 + (column & 31))
    return jnp.where(wanted, 1.0, 0.0).astype(BF)


def center_kernel(near, chan, local, from_bm, from_bp, extra, pre_out, own_out, blocks):
    for i in range(3):
        for plane in (0, 9):
            blocks[i, plane] = jnp.zeros((10, 16, 128), BF)
    for dy, part in ((-1, from_bm), (0, None), (1, from_bp)):
        arrived = None if part is None else part[0:64].astype(F32).reshape(8, 8, 128)
        for i, value in enumerate(block_tiles(near, local, arrived, 0, dy)):
            blocks[i, 1:9, RIM[dy]] = value.reshape(8, -1, 16, 128)

    def lefts(first, count):
        return jnp.concatenate(
            [
                blocks[dz, dx : dx + 8, first : first + count].reshape(128 * count, 128)
                for dx in range(3)
                for dz in range(3)
            ],
            axis=1,
        )

    def rights(dy):
        return jnp.concatenate(
            [
                extra[:, 9 * dx + 3 * dy + dz].reshape(128, 128)
                for dx in range(3)
                for dz in range(3)
            ],
            axis=0,
        )

    pair = jnp.concatenate([rights(0), rights(1)], axis=1)
    pair = jnp.dot(lefts(0, 9), pair, preferred_element_type=F32).reshape(8, 9, 16, 256)
    pre = jnp.dot(lefts(2, 8), rights(2), preferred_element_type=F32).reshape(8, 8, 16, 128)
    pre_out[...] = pre + pair[:, 0:8, :, 0:128] + pair[:, 1:9, :, 128:256]
    stacked = jnp.concatenate([blocks[dz, 1:9].reshape(1280, 128) for dz in range(3)], axis=1)
    own = jnp.dot(stacked, selection(chan[0]), preferred_element_type=F32).astype(BF)
    own_out[...] = own.reshape(8, 10, 16, 128)


def main_kernel(
    near, chan, place, mask, local, from_am, from_ap, center_pre, center_own, extra, own_weights,
    act_out, sent, own_out,
    rim, grads, own_block, act_all, terms, stage,
):
    z = lax.broadcasted_iota(jnp.int32, (1, 8, 128), 1)
    own_block[1:9] = center_own[...]
    edges = []
    for side, (dx, part) in enumerate(((-1, from_am), (1, from_ap))):
        corner = part[64:80].astype(F32).reshape(2, 8, 128)
        face = part[0:64].astype(F32).reshape(8, 8, 128)
        for dy, arrived in ((-1, corner[0:1]), (0, face), (1, corner[1:2])):
            for i, value in enumerate(block_tiles(near, local, arrived, dx, dy)):
                rim[side, i, RIM[dy]] = value
        left = jnp.concatenate(
            [rim[side, dz, dy : dy + 8].reshape(128, 128) for dy in range(3) for dz in range(3)],
            axis=1,
        )
        right = jnp.concatenate(
            [extra[:, 9 * (dx + 1) + o].reshape(128, 128) for o in range(9)], axis=0
        )
        edges.append(jnp.dot(left, right, preferred_element_type=F32).reshape(1, 8, 16, 128))
        stacked = jnp.concatenate([rim[side, dz].reshape(160, 128) for dz in range(3)], axis=1)
        own = jnp.dot(stacked, selection(chan[0]), preferred_element_type=F32).astype(BF)
        own_block[9 * side] = own.reshape(10, 16, 128)
    pre = center_pre[...]
    pre = jnp.concatenate([pre[0:1] + edges[0], pre[1:7], pre[7:8] + edges[1]], axis=0)
    pre = pre.reshape(64, 2, 8, 128)

    back = []
    for brick in range(2):
        on = mask[brick : brick + 1, :]
        pre_act = pre[:, brick].reshape(512, 128).T * on
        gate = jax.nn.sigmoid(pre_act)
        act_all[brick] = (pre_act * gate).astype(BF)
        cotangent = jnp.concatenate(
            [extra[:, 27 + 4 * brick + i].reshape(128, 128).astype(F32) for i in range(4)], axis=1
        )
        grad = cotangent * on * gate * (1.0 + pre_act * (1.0 - gate))
        back.append(grad.T.reshape(64, 8, 128))
    start = pl.multiple_of(chan[0] * 32, 32)
    for brick in range(2):
        act_out[brick] = act_all[brick, pl.ds(start, 32), :]
    back = jnp.stack(back, axis=1).reshape(1024, 128)
    grads[...] = jnp.zeros(grads.shape, BF)
    grads[2:10, 2:10] = back.astype(BF).reshape(8, 8, 16, 128)
    back_t = back.T.astype(BF)

    def put_part(tile, value):
        first = tile // 7 * SENT + tile % 7 * 8
        stage[first : first + 8] = value

    for first in range(0, 9, 2):
        windows = [
            own_block[dx + 1 : dx + 9, dy + 1 : dy + 9].reshape(1024, 128)
            for dx, dy in PLANAR[first : first + 2]
        ]
        product = jnp.dot(back_t, jnp.concatenate(windows, axis=1), preferred_element_type=F32)
        for i in range(len(windows)):
            turned = product[:, 128 * i : 128 * i + 128].T
            for tile in range(12):
                put_part(12 * (first + i) + tile, turned[8 * tile : 8 * tile + 8])
    for tile in range(108, 112):
        put_part(tile, jnp.zeros((8, 128), F32))
    for j in range(GROUP):
        stage[j * SENT + PART : (j + 1) * SENT] = jnp.zeros((16, 128), F32)

    def grad_lefts(first, count):
        return jnp.concatenate(
            [
                grads[1 - dx : 11 - dx, first : first + count].reshape(160 * count, 128)
                for dx in (-1, 0, 1)
            ],
            axis=1,
        )

    def grad_rights(dy):
        pieces = []
        for dx in (-1, 0, 1):
            first = (dx + 1) * 9 + (dy + 1) * 3
            piece = own_weights[first : first + 3].reshape(96, 128).astype(F32)
            piece = jnp.concatenate([piece, jnp.zeros((32, 128), F32)], axis=0)
            pieces.append(piece.T.astype(BF))
        return jnp.concatenate(pieces, axis=0)

    pair = jnp.concatenate([grad_rights(1), grad_rights(0)], axis=1)
    pair = jnp.dot(grad_lefts(0, 11), pair, preferred_element_type=F32).reshape(10, 11, 16, 256)
    spread = jnp.dot(grad_lefts(2, 10), grad_rights(-1), preferred_element_type=F32)
    spread = spread.reshape(10, 10, 16, 128)
    spread = spread + pair[:, 0:10, :, 0:128] + pair[:, 1:11, :, 128:256]
    spread = spread.reshape(100, 2, 8, 128)
    for brick in range(2):
        part = spread[:, brick]
        up = pltpu.roll(part, 7, 1)
        down = pltpu.roll(pltpu.roll(part, 64, 2), 1, 1)
        center = (
            pltpu.roll(part, 96, 2) + jnp.where(z < 7, up, 0.0) + jnp.where(z > 0, down, 0.0)
        )
        terms[0, brick] = jnp.where(z == 7, up, 0.0).reshape(10, 10, 8, 128)
        terms[1, brick] = center.reshape(10, 10, 8, 128)
        terms[2, brick] = jnp.where(z == 0, down, 0.0).reshape(10, 10, 8, 128)
    for brick in range(2):
        own_out[brick] = terms[1, brick, 1:9, 1:9]
    for dx, dy in PLANAR:
        pieces = [
            (near[brick, slot], terms[i, brick, RIM[dx], RIM[dy]])
            for brick in range(2)
            for i, slot in enumerate(planar_slots(dx, dy))
            if slot is not None
        ]

        def collected(target):
            total = 0.0
            for r, piece in pieces:
                total = total + jnp.where(r == target, piece, 0.0)
            return total

        for brick in range(2):
            own_out[brick, SIDE[dx], SIDE[dy]] += collected(brick)
        if (dx, dy) != (0, 0):
            rim = collected(2 + MOVES.index((dx, dy))).reshape(-1, 8, 128)
            target = lax.rem(place[0] + STEPS[dx, dy] + GROUP, GROUP)
            stage[rows_of(target, SENT, PART, 16)] = packed(rim)
    sent[...] = stage[...].astype(BF)


def middle_kernel(place, arrived, sent, held, stage):
    held[...] = arrived[...].astype(F32)
    total = held[0:PART]
    for j in range(1, GROUP):
        total = total + held[j * SENT : j * SENT + PART]
    planes = stage.shape[0] // ONWARD
    for j in range(planes):
        stage[j * ONWARD : j * ONWARD + PART] = total
        stage[j * ONWARD + PART : (j + 1) * ONWARD] = jnp.zeros((24, 128), F32)
    lane = lax.broadcasted_iota(jnp.int32, (8, 128), 1)
    for a in (-1, 1):
        rims = {
            b: held[rows_of(lax.rem(place[0] - STEPS[a, b] + GROUP, GROUP), SENT, PART, 16 if b == 0 else 8)]
            for b in (-1, 0, 1)
        }
        edges = jnp.where(lane < 32, rims[-1], pltpu.roll(rims[1], 32, 1))
        target = place[1] + a

        @pl.when((target >= 0) & (target < planes))
        def _():
            stage[rows_of(target, ONWARD, PART, 24)] = jnp.concatenate([rims[0], edges], axis=0)

    sent[...] = stage[...].astype(BF)


def sum_kernel(scale, arrived, sent):
    values = arrived[...].astype(F32)
    total = values[0:PART]
    for j in range(1, values.shape[0] // ONWARD):
        total = total + values[j * ONWARD : j * ONWARD + PART]
    sent[...] = jnp.concatenate([total * scale] * GROUP, axis=0).astype(BF)


def final_kernel(send, place, mask, own, direct, onward, out, total, held, passed):
    total[...] = own[...]
    held[...] = direct[...].astype(F32)
    passed[...] = onward[...].astype(F32)
    inner, outer = place[0], place[1]
    for dx, dy in MOVES:
        s = send[MOVES.index((dx, dy))]
        origin = inner - STEPS[dx, dy]
        size = 8 if dx and dy else 16
        rows = held[rows_of(lax.rem(origin + GROUP, GROUP), SENT, PART, size)]
        if dx:
            passer = jnp.clip(outer - dx, 0, passed.shape[0] // ONWARD - 1)
            other = passed[rows_of(passer, ONWARD, PART + 16 if dy else PART, size)]
            if dy == 1:
                other = pltpu.roll(other, 96, 1)
            rows = jnp.where((origin >= 0) & (origin < GROUP), rows, other)
        piece = unpacked(rows, 1 if dx and dy else 8)
        nx = 8 if dx == 0 else 1
        piece = piece.reshape(nx, piece.shape[0] // nx, 8, 128)
        for brick in range(2):
            total[brick, SIDE[dx], SIDE[dy]] += jnp.where(s == brick, piece, 0.0)
    for brick in range(2):
        rows = total[brick].reshape(512, 128).T[0:32] * mask[brick : brick + 1, :]
        out[brick] = rows.astype(BF)


SMEM = pl.BlockSpec(memory_space=pltpu.SMEM)
VMEM = pl.BlockSpec(memory_space=pltpu.VMEM)


def call(kernel, name, smem, vmem, outs, scratch, limit, cost=None):
    shapes = [jax.ShapeDtypeStruct(s, d) for s, d in outs]
    return pl.pallas_call(
        kernel,
        out_shape=shapes,
        in_specs=[SMEM] * len(smem) + [VMEM] * len(vmem),
        out_specs=[VMEM] * len(outs),
        scratch_shapes=[pltpu.VMEM(s, d) for s, d in scratch],
        compiler_params=pltpu.CompilerParams(vmem_limit_bytes=limit << 20),
        cost_estimate=cost,
        name=name,
    )(*smem, *vmem)


def passed_along(shard, by):
    count = lax.axis_size("space")
    pairs = [(i, i + by) for i in range(count) if 0 <= i + by < count]
    if abs(by) == 1:
        pairs = [(i, j) for i, j in pairs if i // 4 == j // 4]
    return lax.ppermute(shard, "space", pairs)


def unpack_mask(packed):
    shifts = jnp.arange(32, dtype=jnp.int32)
    bits = lax.shift_right_logical(packed[:, :, None], shifts[None, None, :]) & 1
    return bits.reshape(packed.shape[0], packed.shape[1] * 32).astype(F32)


def exchanged(values, far):
    count = lax.axis_size("space")
    planes = count // GROUP
    groups = [[j * GROUP + i for i in range(GROUP)] for j in range(planes)]
    if far:
        groups = [list(members) for members in zip(*groups)]
    return lax.all_to_all(values, "space", 0, 0, tiled=True, axis_index_groups=groups)


def on_device(features, mask_packed, neighbours, send_list, weights, cotangent):
    chan = lax.axis_index("chan").astype(jnp.int32).reshape(1)
    send = send_list.reshape(8)
    where = lax.axis_index("space").astype(jnp.int32)
    place = jnp.stack([where % GROUP, where // GROUP])
    planes = lax.axis_size("space") // GROUP
    mask = unpack_mask(mask_packed)
    (copies,) = call(feature_copies_kernel, "sent", [], [features], [((4, 32, 2, 512), BF)], [], 16)
    gathered = lax.all_to_all(copies, "chan", 0, 0, tiled=True)
    by_lanes = cotangent.reshape(32, 8, 128).transpose(1, 0, 2)
    (extra,) = call(
        copies_kernel, "copies", [], [weights, by_lanes], [((4, 35, 32, 128), BF)], [], 16,
        pl.CostEstimate(flops=0, bytes_accessed=8 << 20, transcendentals=0),
    )
    local, to_b, face_a = call(
        rims_kernel, "rims", [send], [mask, gathered],
        [((2, 8, 8, 8, 128), F32), ((2, 80, 128), BF), ((2, 64, 128), BF)], [], 16,
    )
    from_bm, from_bp = passed_along(to_b[0], 1), passed_along(to_b[1], -1)
    extra, from_bm = lax.optimization_barrier((extra, from_bm))
    extra = lax.all_to_all(extra, "chan", 0, 0, tiled=True)
    to_am = jnp.concatenate([face_a[0], from_bm[64:72], from_bp[64:72]], axis=0)
    to_ap = jnp.concatenate([face_a[1], from_bm[72:80], from_bp[72:80]], axis=0)
    from_am, from_ap = passed_along(to_am, 4), passed_along(to_ap, -4)
    center_pre, center_own = call(
        center_kernel, "center", [neighbours, chan], [local, from_bm, from_bp, extra],
        [((8, 8, 16, 128), F32), ((8, 10, 16, 128), BF)], [((3, 10, 10, 16, 128), BF)], 24,
        pl.CostEstimate(flops=1 << 30, bytes_accessed=3 << 20, transcendentals=0),
    )
    act, sent, own = call(
        main_kernel, "conv", [neighbours, chan, place],
        [mask, local, from_am, from_ap, center_pre, center_own, extra, weights],
        [
            ((2, 32, 512), BF), ((GROUP * SENT, 128), BF), ((2, 8, 8, 8, 128), F32),
        ],
        [
            ((2, 3, 10, 16, 128), BF), ((12, 12, 16, 128), BF), ((10, 10, 16, 128), BF),
            ((2, 128, 512), BF), ((3, 2, 10, 10, 8, 128), F32), ((GROUP * SENT, 128), F32),
        ],
        32,
    )
    scale = 1.0 / math.sqrt(2 * lax.axis_size("space") * 512)
    direct = exchanged(sent, False)
    (sent,) = call(
        middle_kernel, "middle", [place], [direct], [((planes * ONWARD, 128), BF)],
        [((GROUP * SENT, 128), F32), ((planes * ONWARD, 128), F32)], 16,
    )
    onward = exchanged(sent, True)
    (sent,) = call(
        functools.partial(sum_kernel, scale), "sums", [], [onward], [((GROUP * PART, 128), BF)], [], 16
    )
    summed = exchanged(sent, False)
    grad_weights = summed[:864].astype(F32).reshape(27, 32, 128)
    (grad,) = call(
        final_kernel, "grad", [send, place], [mask, own, direct, onward],
        [((2, 32, 512), BF)],
        [((2, 8, 8, 8, 128), F32), ((GROUP * SENT, 128), F32), ((planes * ONWARD, 128), F32)], 16,
    )
    return act.transpose(1, 0, 2), grad.transpose(1, 0, 2), grad_weights


def solution(mesh):
    return jax.shard_map(
        on_device,
        mesh=mesh,
        in_specs=(
            P("chan", "space", None),
            P("space", None),
            P("space", None),
            P("space", None, None),
            P(None, "chan", None),
            P("chan", "space", None),
        ),
        out_specs=(P("chan", "space", None), P("chan", "space", None), P(None, "chan", None)),
        check_vma=False,
    )
```

```python
import functools
import math

import jax
import jax.numpy as jnp
from jax import lax
from jax.experimental import pallas as pl
from jax.experimental.pallas import tpu as pltpu
from jax.sharding import PartitionSpec as P

BF = jnp.bfloat16
F32 = jnp.float32
SIDE = {-1: slice(7, 8), 0: slice(0, 8), 1: slice(0, 1)}
RIM = {-1: slice(0, 1), 0: slice(1, 9), 1: slice(9, 10)}
PLANAR = [(a, b) for a in (-1, 0, 1) for b in (-1, 0, 1)]
MOVES = [m for m in PLANAR if m != (0, 0)]
STEPS = {(a, b): 4 * a + b for a, b in MOVES}
GROUP = 16
PART = 56
SENT = PART + 16
ONWARD = PART + 24


def slot_of(dx, dy, dz):
    linear = (dx + 1) * 9 + (dy + 1) * 3 + dz + 1
    return linear if linear < 13 else linear - 1


def planar_slots(dx, dy):
    return [None if (dx, dy, dz) == (0, 0, 0) else slot_of(dx, dy, dz) for dz in (-1, 0, 1)]


def tiles(ref_or_value, dx, dy):
    part = ref_or_value[SIDE[dx], SIDE[dy]]
    return part.reshape(-1, 8, 128)


def packed(rim):
    if rim.shape[0] == 1:
        return jnp.concatenate([rim[0], jnp.zeros((8, 128), F32)], axis=0)
    lane = lax.broadcasted_iota(jnp.int32, (8, 128), 1)
    halves = []
    for first in (0, 4):
        value = rim[first]
        for j in (1, 2, 3):
            value = jnp.where(lane < 32 * j, value, pltpu.roll(rim[first + j], 32 * j, 1))
        halves.append(value)
    return jnp.concatenate(halves, axis=0)


def unpacked(rows, count):
    pieces = []
    for i in range(count):
        value = rows[8 * (i // 4) : 8 * (i // 4) + 8]
        pieces.append(pltpu.roll(value, 128 - 32 * (i % 4), 1) if i % 4 else value)
    return jnp.stack(pieces)


def rows_of(index, stride, first, count):
    return pl.ds(pl.multiple_of(index * stride + first, 8), count)


def feature_copies_kernel(features, out):
    value = features[...]
    for i in range(out.shape[0]):
        out[i] = value


def copies_kernel(weights, by_lanes, out):
    for i in range(out.shape[0]):
        out[i, 0:27] = weights[...]
        out[i, 27:35] = by_lanes[...]


def rims_kernel(send, mask, gathered, local, to_b, face_a):
    both = gathered[...].reshape(128, 2, 512).astype(F32)
    for brick in range(2):
        rows = both[:, brick] * mask[brick : brick + 1, :]
        local[brick] = rows.T.reshape(8, 8, 8, 128)

    def chosen(move):
        s = send[MOVES.index(move)]
        first, second = (tiles(local[brick], *move) for brick in range(2))
        return jnp.where(s == 0, first, jnp.where(s == 1, second, 0.0))

    for i, b in enumerate((-1, 1)):
        parts = [chosen((0, b)), chosen((-1, b)), chosen((1, b))]
        to_b[i] = jnp.concatenate(parts, axis=0).reshape(80, 128).astype(BF)
    for i, a in enumerate((-1, 1)):
        face_a[i] = chosen((a, 0)).reshape(64, 128).astype(BF)


def block_tiles(near, local, arrived, dx, dy):
    z = lax.broadcasted_iota(jnp.int32, (1, 8, 128), 1)
    options = [tiles(local[0], dx, dy), tiles(local[1], dx, dy)]
    rows = [0, 1]
    if (dx, dy) != (0, 0):
        options.append(arrived)
        rows.append(2 + MOVES.index((dx, dy)))

    def pick(r):
        value = 0.0
        for row, option in zip(rows, options):
            value = jnp.where(r == row, option, value)
        return value

    shifted = [[], [], []]
    for brick in range(2):
        below, level, above = planar_slots(dx, dy)
        center = options[brick] if level is None else pick(near[brick, level])
        under, over = pick(near[brick, below]), pick(near[brick, above])
        shifted[0].append(pltpu.roll(jnp.where(z == 7, under, center), 1, 1))
        shifted[1].append(center)
        shifted[2].append(pltpu.roll(jnp.where(z == 0, over, center), 7, 1))
    return [jnp.stack(pair, axis=1).reshape(-1, 16, 128).astype(BF) for pair in shifted]


def selection(chan):
    row = lax.broadcasted_iota(jnp.int32, (384, 128), 0)
    column = lax.broadcasted_iota(jnp.int32, (384, 128), 1)
    wanted = (row >> 7 == column >> 5) & ((row & 127) == chan * 32 + (column & 31))
    return jnp.where(wanted, 1.0, 0.0).astype(BF)


def center_kernel(
    near, chan, local, from_bm, from_bp, extra, own_weights, pre_out, own_out, turned, blocks
):
    for i in range(9):
        piece = own_weights[3 * i : 3 * i + 3].reshape(96, 128).astype(F32)
        piece = jnp.concatenate([piece, jnp.zeros((32, 128), F32)], axis=0)
        turned[i] = piece.T.astype(BF)
    for i in range(3):
        for plane in (0, 9):
            blocks[i, plane] = jnp.zeros((10, 16, 128), BF)
    for dy, part in ((-1, from_bm), (0, None), (1, from_bp)):
        arrived = None if part is None else part[0:64].astype(F32).reshape(8, 8, 128)
        for i, value in enumerate(block_tiles(near, local, arrived, 0, dy)):
            blocks[i, 1:9, RIM[dy]] = value.reshape(8, -1, 16, 128)

    def lefts(first, count):
        return jnp.concatenate(
            [
                blocks[dz, dx : dx + 8, first : first + count].reshape(128 * count, 128)
                for dx in range(3)
                for dz in range(3)
            ],
            axis=1,
        )

    def rights(dy):
        return jnp.concatenate(
            [
                extra[:, 9 * dx + 3 * dy + dz].reshape(128, 128)
                for dx in range(3)
                for dz in range(3)
            ],
            axis=0,
        )

    pair = jnp.concatenate([rights(0), rights(1)], axis=1)
    pair = jnp.dot(lefts(0, 9), pair, preferred_element_type=F32).reshape(8, 9, 16, 256)
    pre = jnp.dot(lefts(2, 8), rights(2), preferred_element_type=F32).reshape(8, 8, 16, 128)
    pre_out[...] = pre + pair[:, 0:8, :, 0:128] + pair[:, 1:9, :, 128:256]
    stacked = jnp.concatenate([blocks[dz, 1:9].reshape(1280, 128) for dz in range(3)], axis=1)
    own = jnp.dot(stacked, selection(chan[0]), preferred_element_type=F32).astype(BF)
    own_out[...] = own.reshape(8, 10, 16, 128)


def main_kernel(
    near, chan, place, mask, local, from_am, from_ap, center_pre, center_own, extra, turned,
    act_out, sent, own_out,
    rim, grads, own_block, act_all, terms, stage,
):
    z = lax.broadcasted_iota(jnp.int32, (1, 8, 128), 1)
    own_block[1:9] = center_own[...]
    edges = []
    for side, (dx, part) in enumerate(((-1, from_am), (1, from_ap))):
        corner = part[64:80].astype(F32).reshape(2, 8, 128)
        face = part[0:64].astype(F32).reshape(8, 8, 128)
        for dy, arrived in ((-1, corner[0:1]), (0, face), (1, corner[1:2])):
            for i, value in enumerate(block_tiles(near, local, arrived, dx, dy)):
                rim[side, i, RIM[dy]] = value
        left = jnp.concatenate(
            [rim[side, dz, dy : dy + 8].reshape(128, 128) for dy in range(3) for dz in range(3)],
            axis=1,
        )
        right = jnp.concatenate(
            [extra[:, 9 * (dx + 1) + o].reshape(128, 128) for o in range(9)], axis=0
        )
        edges.append(jnp.dot(left, right, preferred_element_type=F32).reshape(1, 8, 16, 128))
        stacked = jnp.concatenate([rim[side, dz].reshape(160, 128) for dz in range(3)], axis=1)
        own = jnp.dot(stacked, selection(chan[0]), preferred_element_type=F32).astype(BF)
        own_block[9 * side] = own.reshape(10, 16, 128)
    pre = center_pre[...]
    pre = jnp.concatenate([pre[0:1] + edges[0], pre[1:7], pre[7:8] + edges[1]], axis=0)
    pre = pre.reshape(64, 2, 8, 128)

    back = []
    for brick in range(2):
        on = mask[brick : brick + 1, :]
        pre_act = pre[:, brick].reshape(512, 128).T * on
        gate = jax.nn.sigmoid(pre_act)
        act_all[brick] = (pre_act * gate).astype(BF)
        cotangent = jnp.concatenate(
            [extra[:, 27 + 4 * brick + i].reshape(128, 128).astype(F32) for i in range(4)], axis=1
        )
        grad = cotangent * on * gate * (1.0 + pre_act * (1.0 - gate))
        back.append(grad.T.reshape(64, 8, 128))
    start = pl.multiple_of(chan[0] * 32, 32)
    for brick in range(2):
        act_out[brick] = act_all[brick, pl.ds(start, 32), :]
    back = jnp.stack(back, axis=1).reshape(1024, 128)
    grads[...] = jnp.zeros(grads.shape, BF)
    grads[2:10, 2:10] = back.astype(BF).reshape(8, 8, 16, 128)
    back_t = back.T.astype(BF)

    def put_part(tile, value):
        first = tile // 7 * SENT + tile % 7 * 8
        stage[first : first + 8] = value

    for first in range(0, 9, 2):
        windows = [
            own_block[dx + 1 : dx + 9, dy + 1 : dy + 9].reshape(1024, 128)
            for dx, dy in PLANAR[first : first + 2]
        ]
        product = jnp.dot(back_t, jnp.concatenate(windows, axis=1), preferred_element_type=F32)
        for i in range(len(windows)):
            flipped = product[:, 128 * i : 128 * i + 128].T
            for tile in range(12):
                put_part(12 * (first + i) + tile, flipped[8 * tile : 8 * tile + 8])
    for tile in range(108, 112):
        put_part(tile, jnp.zeros((8, 128), F32))
    for j in range(GROUP):
        stage[j * SENT + PART : (j + 1) * SENT] = jnp.zeros((16, 128), F32)

    def grad_lefts(first, count):
        return jnp.concatenate(
            [
                grads[1 - dx : 11 - dx, first : first + count].reshape(160 * count, 128)
                for dx in (-1, 0, 1)
            ],
            axis=1,
        )

    def grad_rights(dy):
        return jnp.concatenate([turned[3 * dx + dy + 1] for dx in range(3)], axis=0)

    pair = jnp.concatenate([grad_rights(1), grad_rights(0)], axis=1)
    pair = jnp.dot(grad_lefts(0, 11), pair, preferred_element_type=F32).reshape(10, 11, 16, 256)
    spread = jnp.dot(grad_lefts(2, 10), grad_rights(-1), preferred_element_type=F32)
    spread = spread.reshape(10, 10, 16, 128)
    spread = spread + pair[:, 0:10, :, 0:128] + pair[:, 1:11, :, 128:256]
    spread = spread.reshape(100, 2, 8, 128)
    for brick in range(2):
        part = spread[:, brick]
        up = pltpu.roll(part, 7, 1)
        down = pltpu.roll(pltpu.roll(part, 64, 2), 1, 1)
        center = (
            pltpu.roll(part, 96, 2) + jnp.where(z < 7, up, 0.0) + jnp.where(z > 0, down, 0.0)
        )
        terms[0, brick] = jnp.where(z == 7, up, 0.0).reshape(10, 10, 8, 128)
        terms[1, brick] = center.reshape(10, 10, 8, 128)
        terms[2, brick] = jnp.where(z == 0, down, 0.0).reshape(10, 10, 8, 128)
    for brick in range(2):
        own_out[brick] = terms[1, brick, 1:9, 1:9]
    for dx, dy in PLANAR:
        pieces = [
            (near[brick, slot], terms[i, brick, RIM[dx], RIM[dy]])
            for brick in range(2)
            for i, slot in enumerate(planar_slots(dx, dy))
            if slot is not None
        ]

        def collected(target):
            total = 0.0
            for r, piece in pieces:
                total = total + jnp.where(r == target, piece, 0.0)
            return total

        for brick in range(2):
            own_out[brick, SIDE[dx], SIDE[dy]] += collected(brick)
        if (dx, dy) != (0, 0):
            rim = collected(2 + MOVES.index((dx, dy))).reshape(-1, 8, 128)
            target = lax.rem(place[0] + STEPS[dx, dy] + GROUP, GROUP)
            stage[rows_of(target, SENT, PART, 16)] = packed(rim)
    sent[...] = stage[...].astype(BF)


def middle_kernel(place, arrived, sent, held, stage):
    held[...] = arrived[...].astype(F32)
    total = held[0:PART]
    for j in range(1, GROUP):
        total = total + held[j * SENT : j * SENT + PART]
    planes = stage.shape[0] // ONWARD
    for j in range(planes):
        stage[j * ONWARD : j * ONWARD + PART] = total
        stage[j * ONWARD + PART : (j + 1) * ONWARD] = jnp.zeros((24, 128), F32)
    lane = lax.broadcasted_iota(jnp.int32, (8, 128), 1)
    for a in (-1, 1):
        rims = {
            b: held[rows_of(lax.rem(place[0] - STEPS[a, b] + GROUP, GROUP), SENT, PART, 16 if b == 0 else 8)]
            for b in (-1, 0, 1)
        }
        edges = jnp.where(lane < 32, rims[-1], pltpu.roll(rims[1], 32, 1))
        target = place[1] + a

        @pl.when((target >= 0) & (target < planes))
        def _():
            stage[rows_of(target, ONWARD, PART, 24)] = jnp.concatenate([rims[0], edges], axis=0)

    sent[...] = stage[...].astype(BF)


def sum_kernel(scale, arrived, sent):
    values = arrived[...].astype(F32)
    total = values[0:PART]
    for j in range(1, values.shape[0] // ONWARD):
        total = total + values[j * ONWARD : j * ONWARD + PART]
    sent[...] = jnp.concatenate([total * scale] * GROUP, axis=0).astype(BF)


def final_kernel(send, place, mask, own, direct, onward, out, total, held, passed):
    total[...] = own[...]
    held[...] = direct[...].astype(F32)
    passed[...] = onward[...].astype(F32)
    inner, outer = place[0], place[1]
    for dx, dy in MOVES:
        s = send[MOVES.index((dx, dy))]
        origin = inner - STEPS[dx, dy]
        size = 8 if dx and dy else 16
        rows = held[rows_of(lax.rem(origin + GROUP, GROUP), SENT, PART, size)]
        if dx:
            passer = jnp.clip(outer - dx, 0, passed.shape[0] // ONWARD - 1)
            other = passed[rows_of(passer, ONWARD, PART + 16 if dy else PART, size)]
            if dy == 1:
                other = pltpu.roll(other, 96, 1)
            rows = jnp.where((origin >= 0) & (origin < GROUP), rows, other)
        piece = unpacked(rows, 1 if dx and dy else 8)
        nx = 8 if dx == 0 else 1
        piece = piece.reshape(nx, piece.shape[0] // nx, 8, 128)
        for brick in range(2):
            total[brick, SIDE[dx], SIDE[dy]] += jnp.where(s == brick, piece, 0.0)
    for brick in range(2):
        rows = total[brick].reshape(512, 128).T[0:32] * mask[brick : brick + 1, :]
        out[brick] = rows.astype(BF)


SMEM = pl.BlockSpec(memory_space=pltpu.SMEM)
VMEM = pl.BlockSpec(memory_space=pltpu.VMEM)


def call(kernel, name, smem, vmem, outs, scratch, limit, cost=None):
    shapes = [jax.ShapeDtypeStruct(s, d) for s, d in outs]
    return pl.pallas_call(
        kernel,
        out_shape=shapes,
        in_specs=[SMEM] * len(smem) + [VMEM] * len(vmem),
        out_specs=[VMEM] * len(outs),
        scratch_shapes=[pltpu.VMEM(s, d) for s, d in scratch],
        compiler_params=pltpu.CompilerParams(vmem_limit_bytes=limit << 20),
        cost_estimate=cost,
        name=name,
    )(*smem, *vmem)


def passed_along(shard, by):
    count = lax.axis_size("space")
    pairs = [(i, i + by) for i in range(count) if 0 <= i + by < count]
    if abs(by) == 1:
        pairs = [(i, j) for i, j in pairs if i // 4 == j // 4]
    return lax.ppermute(shard, "space", pairs)


def unpack_mask(packed):
    shifts = jnp.arange(32, dtype=jnp.int32)
    bits = lax.shift_right_logical(packed[:, :, None], shifts[None, None, :]) & 1
    return bits.reshape(packed.shape[0], packed.shape[1] * 32).astype(F32)


def exchanged(values, far):
    count = lax.axis_size("space")
    planes = count // GROUP
    groups = [[j * GROUP + i for i in range(GROUP)] for j in range(planes)]
    if far:
        groups = [list(members) for members in zip(*groups)]
    return lax.all_to_all(values, "space", 0, 0, tiled=True, axis_index_groups=groups)


def on_device(features, mask_packed, neighbours, send_list, weights, cotangent):
    chan = lax.axis_index("chan").astype(jnp.int32).reshape(1)
    send = send_list.reshape(8)
    where = lax.axis_index("space").astype(jnp.int32)
    place = jnp.stack([where % GROUP, where // GROUP])
    planes = lax.axis_size("space") // GROUP
    mask = unpack_mask(mask_packed)
    (copies,) = call(feature_copies_kernel, "sent", [], [features], [((4, 32, 2, 512), BF)], [], 16)
    gathered = lax.all_to_all(copies, "chan", 0, 0, tiled=True)
    by_lanes = cotangent.reshape(32, 8, 128).transpose(1, 0, 2)
    (extra,) = call(
        copies_kernel, "copies", [], [weights, by_lanes], [((4, 35, 32, 128), BF)], [], 16,
        pl.CostEstimate(flops=0, bytes_accessed=8 << 20, transcendentals=0),
    )
    extra = lax.all_to_all(extra, "chan", 0, 0, tiled=True)
    local, to_b, face_a = call(
        rims_kernel, "rims", [send], [mask, gathered],
        [((2, 8, 8, 8, 128), F32), ((2, 80, 128), BF), ((2, 64, 128), BF)], [], 16,
    )
    from_bm, from_bp = passed_along(to_b[0], 1), passed_along(to_b[1], -1)
    to_am = jnp.concatenate([face_a[0], from_bm[64:72], from_bp[64:72]], axis=0)
    to_ap = jnp.concatenate([face_a[1], from_bm[72:80], from_bp[72:80]], axis=0)
    from_am, from_ap = passed_along(to_am, 4), passed_along(to_ap, -4)
    center_pre, center_own, turned = call(
        center_kernel, "center", [neighbours, chan], [local, from_bm, from_bp, extra, weights],
        [((8, 8, 16, 128), F32), ((8, 10, 16, 128), BF), ((9, 128, 128), BF)], [((3, 10, 10, 16, 128), BF)], 24,
        pl.CostEstimate(flops=1 << 30, bytes_accessed=3 << 20, transcendentals=0),
    )
    act, sent, own = call(
        main_kernel, "conv", [neighbours, chan, place],
        [mask, local, from_am, from_ap, center_pre, center_own, extra, turned],
        [
            ((2, 32, 512), BF), ((GROUP * SENT, 128), BF), ((2, 8, 8, 8, 128), F32),
        ],
        [
            ((2, 3, 10, 16, 128), BF), ((12, 12, 16, 128), BF), ((10, 10, 16, 128), BF),
            ((2, 128, 512), BF), ((3, 2, 10, 10, 8, 128), F32), ((GROUP * SENT, 128), F32),
        ],
        32,
    )
    scale = 1.0 / math.sqrt(2 * lax.axis_size("space") * 512)
    direct = exchanged(sent, False)
    (sent,) = call(
        middle_kernel, "middle", [place], [direct], [((planes * ONWARD, 128), BF)],
        [((GROUP * SENT, 128), F32), ((planes * ONWARD, 128), F32)], 16,
    )
    onward = exchanged(sent, True)
    (sent,) = call(
        functools.partial(sum_kernel, scale), "sums", [], [onward], [((GROUP * PART, 128), BF)], [], 16
    )
    summed = exchanged(sent, False)
    grad_weights = summed[:864].astype(F32).reshape(27, 32, 128)
    (grad,) = call(
        final_kernel, "grad", [send, place], [mask, own, direct, onward],
        [((2, 32, 512), BF)],
        [((2, 8, 8, 8, 128), F32), ((GROUP * SENT, 128), F32), ((planes * ONWARD, 128), F32)], 16,
    )
    return act.transpose(1, 0, 2), grad.transpose(1, 0, 2), grad_weights


def solution(mesh):
    return jax.shard_map(
        on_device,
        mesh=mesh,
        in_specs=(
            P("chan", "space", None),
            P("space", None),
            P("space", None),
            P("space", None, None),
            P(None, "chan", None),
            P("chan", "space", None),
        ),
        out_specs=(P("chan", "space", None), P("chan", "space", None), P(None, "chan", None)),
        check_vma=False,
    )
```
